32 devices in a mesh: gz: 4 (over z), gy: 2 (over x), gx: 4 (over y, core).
Axes of the slice: x: 2, y: 2, z: 4, core: 2. Of those that a mesh axis runs over, the one named last changes fastest.
Arguments:
- fields: float32 [5, 128, 32, 512], P(None, 'gz', 'gy', 'gx'), may hold values from -6 to 6
- diffusivity: float32 [128, 32, 512], P('gz', 'gy', 'gx'), may hold values from 0.01 to 0.08
- courant: float32 [5, 3], replicated, may hold values from 0.03 to 0.1
- tf_center: float32 [16], replicated, may hold values from -1.5 to 1.5
- tf_sharp: float32 [16], replicated, may hold values from 0.5 to 4
- tf_gain: float32 [16], replicated, may hold values from 0.01 to 0.12
- tf_color: float32 [3, 16], replicated, may hold values from 0.2 to 1
- tile_mask: int32 [4, 16, 32, 4], P('gz', None, 'gy', 'gx'), may hold values from 0 to 1, as said below
- tile_perm: int32 [2, 4, 256], P('gy', 'gx'), may hold values from 0 to 255, each once within a row
Outputs:
- advanced: float32 [5, 128, 32, 512], P(None, 'gz', 'gy', 'gx')
- picture: float32 [2, 4, 256, 4, 128], P('gy', 'gx', 'gz')
The draws below stay inside these ranges and needn't reach their ends.
Inputs may be any that keep to these rules, and one draw needn't show every extreme that they name: `tile_mask`: 1 marks an active tile; the share of active tiles differs from slab to slab.
All inputs are finite; a program needn't handle non-finite values.
Results may differ from the reference program's by a relative error of at most 0.0001.
Values sent between devices are 32-bit elements; how exact they have to be, the bound alone decides.
No kernel may reach another device: no remote copies, remote signals or barrier semaphores. Data moves between devices by JAX's collectives and lax.ppermute only.
A program may use at most 64 MiB of HBM per device.

```python
import math
import jax
import jax.numpy as jnp
from jax import lax

F = 5
TF = 16
CX = 128
CY = 16
CZ = 32
SLABS = 4
NZ = 128
NY = 32
NX = 512
NBY = 2
NBX = 4
TILES = 256


def draw_tile_mask(key, part):
    key_rate, key_roll = jax.random.split(jax.random.fold_in(key, 17))
    thresholds = jax.random.randint(key_rate, (SLABS, 1, 1, 1), 20, 96)
    rolls = jax.random.randint(key_roll, (SLABS, TF, NY, NX // 128), 0, 100)
    return (rolls < thresholds).astype(jnp.int32)


def levels(key, dims, cuts, least, high):
    level = 1.0
    for dim, parts in cuts:
        heights = jax.random.uniform(jax.random.fold_in(jax.random.fold_in(key, 6), dim), (parts,), jnp.float32, least / len(cuts), high / len(cuts))
        level = level * jnp.repeat(jnp.exp(heights), dims[dim] // parts).reshape((-1,) + (1,) * (len(dims) - 1 - dim))
    return level


def normal_values(rng, dims, spread, bound, cuts=(), dtype=jnp.bfloat16):
    level = levels(rng, dims, cuts, -0.22, 0.18) if cuts else 1.0
    drawn = jax.random.normal(rng, dims, jnp.float32) * spread * level
    return jnp.minimum(jnp.maximum(drawn, -bound), bound).astype(dtype)


def setup_inputs(seed: int = 0) -> dict:
    key_of = jax.random.split(jax.random.key(seed), 10)
    fields = normal_values(key_of[0], (F, NZ, NY, NX), 1.0, 6.0, ((1, 4), (2, 2), (3, 4)), jnp.float32)
    diffusivity = jnp.clip(jnp.exp(math.log(0.08) - 2.0794415 * jax.random.uniform(key_of[1], (NZ, NY, NX), jnp.float32) ** levels(key_of[1], (NZ, NY, NX), ((0, 4), (1, 2), (2, 4)), -0.2, 0.2)), 0.01, 0.08)
    courant = jnp.clip(jax.random.uniform(key_of[2], (F, 3), jnp.float32, 0.03, 0.1), 0.03, 0.1)
    tf_center = jnp.clip(jax.random.uniform(key_of[3], (TF,), jnp.float32, -1.5, 1.5), -1.5, 1.5)
    tf_sharp = jnp.clip(jnp.exp(jax.random.uniform(key_of[4], (TF,), jnp.float32, math.log(0.5), math.log(4.0))), 0.5, 4.0)
    tf_gain = jnp.clip(jnp.exp(jax.random.uniform(key_of[5], (TF,), jnp.float32, math.log(0.01), math.log(0.12))), 0.01, 0.12)
    tf_color = jnp.clip(jax.random.uniform(key_of[6], (3, TF), jnp.float32, 0.2, 1.0), 0.2, 1.0)
    tile_mask = draw_tile_mask(jax.random.fold_in(key_of[9], 71), 0)
    tile_perm = jax.vmap(lambda own: jax.random.permutation(own, TILES))(jax.random.split(key_of[8], NBY * NBX)).reshape((NBY, NBX, TILES)).astype(jnp.int32)
    return dict(fields=fields, diffusivity=diffusivity, courant=courant, tf_center=tf_center, tf_sharp=tf_sharp, tf_gain=tf_gain, tf_color=tf_color, tile_mask=tile_mask, tile_perm=tile_perm)


def inner(source, leading, axis_pos, offset):
    picks = [slice(None)] * leading + [slice(1, -1)] * 3
    length = source.shape[leading + axis_pos]
    picks[leading + axis_pos] = slice(1 + offset, length - 1 + offset)
    return source[tuple(picks)]

def advance(padded, kappa_pad, courant):
    center = inner(padded, 1, 0, 0)
    kappa_mid = inner(kappa_pad, 0, 0, 0)
    result = center
    for axis_pos in range(3):
        upper = inner(padded, 1, axis_pos, 1)
        lower = inner(padded, 1, axis_pos, -1)
        kappa_up = inner(kappa_pad, 0, axis_pos, 1)
        kappa_down = inner(kappa_pad, 0, axis_pos, -1)
        speed = courant[:, axis_pos][:, None, None, None]
        result = result + 0.5 * (kappa_mid + kappa_up) * (upper - center) + 0.5 * (kappa_mid + kappa_down) * (lower - center) - speed * (center - lower)
    return result

def reference(fields, diffusivity, courant, tf_center, tf_sharp, tf_gain, tf_color, tile_mask, tile_perm):
    kappa_pad = jnp.pad(diffusivity, 1)
    state = fields
    for level in range(2):
        state = advance(jnp.pad(state, ((0, 0), (1, 1), (1, 1), (1, 1))), kappa_pad, courant)
    scalar = state[0]
    spad = jnp.pad(scalar, 1)
    grad_z = 0.5 * (spad[2:, 1:-1, 1:-1] - spad[:-2, 1:-1, 1:-1])
    grad_y = 0.5 * (spad[1:-1, 2:, 1:-1] - spad[1:-1, :-2, 1:-1])
    grad_x = 0.5 * (spad[1:-1, 1:-1, 2:] - spad[1:-1, 1:-1, :-2])
    shade = 0.35 + 0.65 * jnp.abs(0.64 * grad_z + 0.6 * grad_y + 0.48 * grad_x) / jnp.sqrt(grad_z * grad_z + grad_y * grad_y + grad_x * grad_x + 1.0)
    modul = 1.0 + 0.5 * jnp.tanh(state[4])
    bases = [(shade * jax.nn.sigmoid(state[1 + k])).reshape(SLABS, CZ, NY, NX) for k in range(3)]
    masks = jnp.transpose(tile_mask, (1, 0, 2, 3))

    def render(items):
        center, sharp, gain, color, mask_t = items
        depth = gain * jnp.exp(-sharp * (scalar - center) ** 2) * modul
        depth = depth.reshape(SLABS, CZ, NY, NX)
        before = jnp.cumsum(depth, axis=1) - depth
        weight = jnp.exp(-before) * (1.0 - jnp.exp(-depth))
        cover = jnp.repeat(mask_t, CX, axis=2).astype(jnp.float32)
        colors = jnp.stack([lax.optimization_barrier(jnp.sum(weight * bases[k], axis=1)) * color[k] for k in range(3)], 0) * cover[None]
        alpha = (1.0 - jnp.exp(-lax.optimization_barrier(jnp.sum(depth, axis=1)))) * cover
        acc_c = colors[:, 0]
        acc_a = alpha[0]
        for slab in range(1, SLABS):
            acc_c = acc_c + (1.0 - acc_a)[None] * colors[:, slab]
            acc_a = acc_a + (1.0 - acc_a) * alpha[slab]
        return jnp.concatenate([acc_c, acc_a[None]], 0)
    image = lax.map(render, (tf_center, tf_sharp, tf_gain, tf_color.T, masks))
    tiles = image.reshape(TF, 4, NBY, CY, NBX, CX)
    tiles = jnp.transpose(tiles, (2, 4, 0, 3, 1, 5)).reshape(NBY, NBX, TF * CY, 4, CX)
    picture = jax.vmap(jax.vmap(lambda table, order: table[order]))(tiles, tile_perm)
    return (state, picture)
```

```python
import jax
import jax.numpy as jnp
from jax import lax
from jax.experimental import pallas as pl
from jax.experimental.pallas import tpu as pltpu
from jax.sharding import PartitionSpec as P


def extended(cells, sides, width):
    for axis, dim in sides:
        count = lax.axis_size(axis)
        ends = count - 1
        head = lax.slice_in_dim(cells, 0, width, axis=dim)
        tail = lax.slice_in_dim(cells, cells.shape[dim] - width, cells.shape[dim], axis=dim)
        cells = jnp.concatenate(
            [
                lax.ppermute(tail, axis, [(i, (i + 1) % count) for i in range(ends)]),
                cells,
                lax.ppermute(head, axis, [((i + 1) % count, i) for i in range(ends)]),
            ],
            axis=dim,
        )
    return cells


def inner(source, leading, axis_pos, offset):
    picks = [slice(None)] * leading + [slice(1, -1)] * 3
    length = source.shape[leading + axis_pos]
    picks[leading + axis_pos] = slice(1 + offset, length - 1 + offset)
    return source[tuple(picks)]


def advance(padded, kappa_pad, courant):
    center = inner(padded, 1, 0, 0)
    kappa_mid = inner(kappa_pad, 0, 0, 0)
    result = center
    for axis_pos in range(3):
        upper = inner(padded, 1, axis_pos, 1)
        lower = inner(padded, 1, axis_pos, -1)
        kappa_up = inner(kappa_pad, 0, axis_pos, 1)
        kappa_down = inner(kappa_pad, 0, axis_pos, -1)
        speed = courant[:, axis_pos][:, None, None, None]
        result = (
            result
            + 0.5 * (kappa_mid + kappa_up) * (upper - center)
            + 0.5 * (kappa_mid + kappa_down) * (lower - center)
            - speed * (center - lower)
        )
    return result


def inside(position, total, length):
    start = position * length - 1
    cells = start + jnp.arange(length + 2, dtype=jnp.int32)
    return ((cells >= 0) & (cells < length * total)).astype(jnp.float32)


LOG2E = 1.4426950408889634


def march_kernel(
    center_ref, sharp_ref, gain_ref, color_ref, mask_ref, order_ref, s_ref, modul_ref, base_ref,
    out_ref, tile_ref,
):
    depth_len, rows, lanes = s_ref.shape
    ntf = center_ref.shape[0]
    chunk = 4 if ntf % 4 == 0 else 1
    sub = 8
    halves = rows // sub

    @pl.loop(0, (ntf // chunk) * halves)
    def _(step):
        first = (step // halves) * chunk
        row = pl.multiple_of((step % halves) * sub, sub)
        shape = (sub, lanes)
        mid = [jnp.full(shape, center_ref[first + j], jnp.float32) for j in range(chunk)]
        bend = [jnp.full(shape, sharp_ref[first + j] * -LOG2E, jnp.float32) for j in range(chunk)]
        dense = [jnp.full(shape, gain_ref[first + j] * -LOG2E, jnp.float32) for j in range(chunk)]
        passed = [jnp.ones(shape, jnp.float32)] * chunk
        total = [jnp.zeros(shape, jnp.float32)] * chunk
        acc = [[jnp.zeros(shape, jnp.float32)] * 3 for _ in range(chunk)]
        for z in range(depth_len):
            s = s_ref[z, pl.ds(row, sub), :]
            modul = modul_ref[z, pl.ds(row, sub), :]
            base = [base_ref[k, z, pl.ds(row, sub), :] for k in range(3)]
            for j in range(chunk):
                diff = s - mid[j]
                total[j] = total[j] + modul * jnp.exp2(diff * diff * bend[j])
                after = jnp.exp2(total[j] * dense[j])
                weight = passed[j] - after
                passed[j] = after
                acc[j] = [acc[j][k] + weight * base[k] for k in range(3)]
        for j in range(chunk):
            start = ((first + j) * rows + row) * 4
            for k in range(3):
                tile_ref[pl.ds(start + k, sub, stride=4), :] = acc[j][k] * color_ref[k, first + j]
            tile_ref[pl.ds(start + 3, sub, stride=4), :] = 1.0 - passed[j]

    @pl.loop(0, order_ref.shape[0], unroll=8)
    def _(slot):
        tile = order_ref[slot]
        cover = mask_ref[tile].astype(jnp.float32)
        out_ref[slot] = tile_ref[pl.ds(pl.multiple_of(tile * 4, 4), 4), :] * cover


def march(center, sharp, gain, color, mask, order, s, modul, base):
    lanes = s.shape[-1]
    smem = pl.BlockSpec(memory_space=pltpu.SMEM)
    vmem = pl.BlockSpec(memory_space=pltpu.VMEM)
    return pl.pallas_call(
        march_kernel,
        out_shape=jax.ShapeDtypeStruct((order.shape[0], 4, lanes), jnp.float32),
        in_specs=[smem] * 6 + [vmem] * 3,
        out_specs=vmem,
        scratch_shapes=[pltpu.VMEM((order.shape[0] * 4, lanes), jnp.float32)],
        compiler_params=pltpu.CompilerParams(vmem_limit_bytes=32 * 1024 * 1024),
        name="march",
    )(center, sharp, gain, color, mask, order, s, modul, base)


def compose_kernel(part_ref, out_ref):
    slabs, rows, _ = part_ref.shape

    @pl.loop(0, rows // 32)
    def _(step):
        def load(slab, k):
            return part_ref[slab, pl.ds(step * 32 + k, 8, stride=4), :]

        acc = [load(0, k) for k in range(4)]
        for slab in range(1, slabs):
            clear = 1.0 - acc[3]
            acc = [acc[k] + clear * load(slab, k) for k in range(4)]
        for k in range(4):
            out_ref[pl.ds(step * 32 + k, 8, stride=4), :] = acc[k]


def compose(parts):
    vmem = pl.BlockSpec(memory_space=pltpu.VMEM)
    return pl.pallas_call(
        compose_kernel,
        out_shape=jax.ShapeDtypeStruct(parts.shape[1:], jnp.float32),
        in_specs=[vmem],
        out_specs=vmem,
        compiler_params=pltpu.CompilerParams(vmem_limit_bytes=32 * 1024 * 1024),
        name="compose",
    )(parts)


def shards(
    fields, diffusivity, courant, tf_center, tf_sharp, tf_gain, tf_color, tile_mask, tile_perm
):
    nfield, depth_len, rows_len, cols_len = fields.shape
    stacked = jnp.concatenate([fields, diffusivity[None]], 0)
    padded = extended(stacked, (("gz", 1), ("gy", 2), ("gx", 3)), 2)
    kappa_pad = padded[nfield]
    widened = advance(padded[:nfield], kappa_pad, courant)
    valid_z = inside(lax.axis_index("gz"), lax.axis_size("gz"), depth_len)
    valid_y = inside(lax.axis_index("gy"), lax.axis_size("gy"), rows_len)
    valid_x = inside(lax.axis_index("gx"), lax.axis_size("gx"), cols_len)
    valid = valid_z[:, None, None] * valid_y[None, :, None] * valid_x[None, None, :]
    widened = widened * valid[None]
    state = advance(widened, inner(kappa_pad, 0, 0, 0), courant)
    scalar = state[0]
    spad = extended(scalar, (("gz", 0), ("gy", 1), ("gx", 2)), 1)
    grad_z = 0.5 * (spad[2:, 1:-1, 1:-1] - spad[:-2, 1:-1, 1:-1])
    grad_y = 0.5 * (spad[1:-1, 2:, 1:-1] - spad[1:-1, :-2, 1:-1])
    grad_x = 0.5 * (spad[1:-1, 1:-1, 2:] - spad[1:-1, 1:-1, :-2])
    shade = 0.35 + 0.65 * jnp.abs(0.64 * grad_z + 0.6 * grad_y + 0.48 * grad_x) / jnp.sqrt(
        grad_z * grad_z + grad_y * grad_y + grad_x * grad_x + 1.0
    )
    modul = 1.0 + 0.5 * jnp.tanh(state[4])
    bases = shade[None] * jax.nn.sigmoid(state[1:4])
    count = lax.axis_size("gz")
    order = tile_perm[0, 0]
    per_owner = order.shape[0] // count
    tiles = march(
        tf_center, tf_sharp, tf_gain, tf_color, tile_mask[0].reshape(-1), order, scalar, modul, bases
    )
    grouped = tiles.reshape(count, per_owner * 4, cols_len)
    composed = compose(lax.all_to_all(grouped, "gz", split_axis=0, concat_axis=0, tiled=True))
    picture = composed.reshape(1, 1, per_owner, 4, cols_len)
    return (state, picture)


def solution(mesh):
    return jax.shard_map(
        shards,
        mesh=mesh,
        in_specs=(
            P(None, "gz", "gy", "gx"),
            P("gz", "gy", "gx"),
            P(),
            P(),
            P(),
            P(),
            P(),
            P("gz", None, "gy", "gx"),
            P("gy", "gx", None),
        ),
        out_specs=(P(None, "gz", "gy", "gx"), P("gy", "gx", "gz", None, None)),
        check_vma=False,
    )
```

```python
import jax
import jax.numpy as jnp
from jax import lax
from jax.experimental import pallas as pl
from jax.experimental.pallas import tpu as pltpu
from jax.sharding import PartitionSpec as P

LOG2E = 1.4426950408889634
W = 3
SUB = 8
F32 = jnp.float32


def reach(field, nfield):
    return W if field in (0, nfield) else W - 1


def tiles_of(first, last):
    return [min(start, last - SUB) for start in range(first, last, SUB)]


def z_plan(nfield):
    plan, at = [], 0
    for field in range(nfield + 1):
        plan.append((field, at, reach(field, nfield)))
        at += reach(field, nfield)
    return plan, at


def y_plan(nfield, depth_len):
    plan, at = [], 0
    for field in range(nfield + 1):
        wide = reach(field, nfield)
        for away in range(1, wide + 1):
            extra = wide - away
            plan.append((field, away, -extra, depth_len + 2 * extra, at))
            at += depth_len + 2 * extra
    return plan, at + (-at) % SUB


def source_plane(refs, field, z):
    fields_ref, kappa_ref, zlo_ref, zhi_ref = refs
    nfield, depth_len = fields_ref.shape[:2]
    _, at, wide = z_plan(nfield)[0][field]
    if z < 0:
        return zlo_ref.at[at + wide + z]
    if z >= depth_len:
        return zhi_ref.at[at + z - depth_len]
    return kappa_ref.at[z] if field == nfield else fields_ref.at[field, z]


def pack_rows_kernel(fields_ref, kappa_ref, zlo_ref, zhi_ref, lo_ref, hi_ref):
    refs = (fields_ref, kappa_ref, zlo_ref, zhi_ref)
    nfield, depth_len, rows, lanes = fields_ref.shape
    flat_fields = fields_ref.reshape(nfield * depth_len * rows, lanes)
    flat_kappa = kappa_ref.reshape(depth_len * rows, lanes)
    plan, used = y_plan(nfield, depth_len)
    for out_ref, top in ((lo_ref, True), (hi_ref, False)):
        for field, away, first, length, at in plan:
            row = away - 1 if top else rows - away
            for z in list(range(first, 0)) + list(range(depth_len, first + length)):
                out_ref[at + z - first, :] = source_plane(refs, field, z)[row, :]
            flat, base = (flat_kappa, 0) if field == nfield else (flat_fields, field * depth_len * rows)
            for z in range(0, depth_len, SUB):
                out_ref[pl.ds(at - first + z, SUB), :] = flat[
                    pl.ds(base + z * rows + row, SUB, stride=rows), :
                ]
        spare = plan[-1][3] + plan[-1][4]
        if used > spare:
            out_ref[spare:used, :] = jnp.zeros((used - spare, lanes), F32)


def assemble(refs, ylo_ref, yhi_ref, flags_ref, pad_ref):
    fields_ref, kappa_ref, zlo_ref, zhi_ref = refs
    nfield, depth_len, rows, lanes = fields_ref.shape
    planes, pitch = depth_len + 2 * W, rows + 8

    @pl.loop(0, depth_len)
    def _(z):
        for field in range(nfield + 1):
            for r in range(0, rows, SUB):
                value = kappa_ref[z, r : r + SUB, :] if field == nfield else fields_ref[field, z, r : r + SUB, :]
                pad_ref[field * planes + W + z, W + r : W + r + SUB, :] = value

    for field, at, wide in z_plan(nfield)[0]:
        for k in range(wide):
            for r in range(0, rows, SUB):
                pad_ref[field * planes + W - wide + k, W + r : W + r + SUB, :] = zlo_ref[at + k, r : r + SUB, :]
                pad_ref[field * planes + W + depth_len + k, W + r : W + r + SUB, :] = zhi_ref[at + k, r : r + SUB, :]
    flat = pad_ref.reshape((nfield + 1) * planes * pitch, lanes)
    low, high = flags_ref[2], flags_ref[3]
    for field, away, first, length, at in y_plan(nfield, depth_len)[0]:
        for ref, flag, row in ((ylo_ref, low, W - away), (yhi_ref, high, W + rows + away - 1)):
            for start in tiles_of(0, length):
                flat[pl.ds((field * planes + W + first + start) * pitch + row, SUB, stride=pitch), :] = (
                    ref[pl.ds(at + start, SUB), :] * flag
                )


def clear_pad(pad_ref):
    @pl.loop(0, pad_ref.shape[0])
    def _(plane):
        pad_ref[plane] = jnp.zeros(pad_ref.shape[1:], F32)


def pack_columns_kernel(
    flags_ref, fields_ref, kappa_ref, zlo_ref, zhi_ref, ylo_ref, yhi_ref, lo_ref, hi_ref, pad_ref
):
    refs = (fields_ref, kappa_ref, zlo_ref, zhi_ref)
    nfield, depth_len, rows, lanes = fields_ref.shape
    planes, pitch = depth_len + 2 * W, rows + 8
    clear_pad(pad_ref)
    assemble(refs, ylo_ref, yhi_ref, flags_ref, pad_ref)
    lane = lax.broadcasted_iota(jnp.int32, (SUB, lanes), 1)

    @pl.loop(0, nfield + 1)
    def _(field):
        for r in range(0, pitch, SUB):

            def body(zi, carry):
                low, high = carry
                value = pad_ref[field * planes + zi, r : r + SUB, :]
                mine = (lane >= W * zi) & (lane < W * zi + W)
                low = jnp.where(mine, pltpu.roll(value, W * zi, 1), low)
                high = jnp.where(mine, pltpu.roll(value, lax.rem(W * zi + W, lanes), 1), high)
                return low, high

            zero = jnp.zeros((SUB, lanes), F32)
            low, high = lax.fori_loop(0, planes, body, (zero, zero), unroll=planes)
            lo_ref[field, r : r + SUB, :] = low
            hi_ref[field, r : r + SUB, :] = high


def stencil(u, coefs, ups, downs, speeds):
    total = u
    for axis in range(3):
        k_up, k_down = coefs[axis]
        total = total + k_up * (ups[axis] - u) + (k_down + speeds[axis]) * (downs[axis] - u)
    return total


def side_neighbours(near, own, is_left, lanes, col):
    first, second = (near, own) if is_left else (own, near)
    first_up = jnp.where(col == W - 1, pltpu.roll(second, W - 1, 1), pltpu.roll(first, lanes - 1, 1))
    first_down = pltpu.roll(first, 1, 1)
    second_up = pltpu.roll(second, lanes - 1, 1)
    second_down = jnp.where(col == 0, pltpu.roll(first, lanes - (W - 1), 1), pltpu.roll(second, 1, 1))
    pair = ((first_up, first_down), (second_up, second_down))
    return pair if is_left else (pair[1], pair[0])


def main_kernel(
    flags_ref, courant_ref, center_ref, sharp_ref, gain_ref, color_ref, mask_ref, order_ref,
    fields_ref, kappa_ref, zlo_ref, zhi_ref, ylo_ref, yhi_ref, xlo_ref, xhi_ref, ownlo_ref, ownhi_ref,
    state_ref, out_ref,
    pad_ref, next_ref, last_ref, side_ref, edge_ref, base_ref, tile_ref,
):
    refs = (fields_ref, kappa_ref, zlo_ref, zhi_ref)
    nfield, depth_len, rows, lanes = fields_ref.shape
    planes, pitch = depth_len + 2 * W, rows + 8
    clear_pad(pad_ref)
    assemble(refs, ylo_ref, yhi_ref, flags_ref, pad_ref)
    lane = lax.broadcasted_iota(jnp.int32, (SUB, lanes), 1)
    sub = lax.broadcasted_iota(jnp.int32, (SUB, lanes), 0)
    zi_of = lane // W
    col = lane - zi_of * W
    flag = [flags_ref[i] for i in range(6)]
    speed = [[courant_ref[f, a] for a in range(3)] for f in range(nfield)]

    def row_mask(r):
        y = sub + (r - W)
        return jnp.where(y < 0, flag[2], jnp.where(y >= rows, flag[3], 1.0))

    def lane_z_mask():
        return jnp.where(zi_of < W, flag[0], jnp.where(zi_of >= W + depth_len, flag[1], 1.0))

    sides = ((xlo_ref, ownlo_ref, True, flag[4]), (xhi_ref, ownhi_ref, False, flag[5]))
    for side, (near_ref, own_ref, _, _) in enumerate(sides):
        for field in range(nfield + 1):
            side_ref[0, side, 0, field] = near_ref[field]
            side_ref[0, side, 1, field] = own_ref[field]

    def edges(level, field):
        for r in range(0, pitch, SUB):
            left = side_ref[level, 0, 0, field, r : r + SUB, :]
            right = side_ref[level, 1, 0, field, r : r + SUB, :]
            edge_ref[level, field, r : r + SUB, :] = jnp.where(col == W - 1, left, pltpu.roll(right, 1, 1))

    def side_step(level, count, r):
        zmask = lane_z_mask() * row_mask(r)
        for side, (_, _, is_left, present) in enumerate(sides):
            def get(block, field, dr=0, lvl=level):
                return side_ref[lvl, side, block, field, r + dr : r + dr + SUB, :]

            blocks = (0, 1)
            kx = side_neighbours(get(0, nfield, 0, 0), get(1, nfield, 0, 0), is_left, lanes, col)
            coefs = []
            for block in blocks:
                k = get(block, nfield, 0, 0)
                coefs.append(
                    [
                        (0.5 * (k + pltpu.roll(k, lanes - W, 1)), 0.5 * (k + pltpu.roll(k, W, 1))),
                        (0.5 * (k + get(block, nfield, 1, 0)), 0.5 * (k + get(block, nfield, -1, 0))),
                        (0.5 * (k + kx[block][0]), 0.5 * (k + kx[block][1])),
                    ]
                )
            for field in range(count):
                ux = side_neighbours(get(0, field), get(1, field), is_left, lanes, col)
                for block in blocks:
                    u = get(block, field)
                    ups = (pltpu.roll(u, lanes - W, 1), get(block, field, 1), ux[block][0])
                    downs = (pltpu.roll(u, W, 1), get(block, field, -1), ux[block][1])
                    value = stencil(u, coefs[block], ups, downs, speed[field])
                    side_ref[level + 1, side, block, field, r : r + SUB, :] = (
                        value * (zmask * present) if block == 0 else value * zmask
                    )

    def along_x(value, zi, edge):
        turned = pltpu.roll(edge, lax.rem(2 * lanes - 2 - W * zi, lanes), 1)
        up = jnp.where(lane == lanes - 1, turned, pltpu.roll(value, lanes - 1, 1))
        down = jnp.where(lane == 0, turned, pltpu.roll(value, 1, 1))
        return up, down

    def kappa_coefs(zi, r):
        plane = nfield * planes + zi
        k = pad_ref[plane, r : r + SUB, :]
        up, down = along_x(k, zi, edge_ref[0, nfield, r : r + SUB, :])
        half = 0.5 * k
        return [
            (half + 0.5 * pad_ref[plane + 1, r : r + SUB, :], half + 0.5 * pad_ref[plane - 1, r : r + SUB, :]),
            (half + 0.5 * pad_ref[plane, r + 1 : r + 1 + SUB, :], half + 0.5 * pad_ref[plane, r - 1 : r - 1 + SUB, :]),
            (half + 0.5 * up, half + 0.5 * down),
        ]

    def step_value(src_ref, level, field, zi, r, coefs):
        plane = field * planes + zi
        u = src_ref[plane, r : r + SUB, :]
        x_up, x_down = along_x(u, zi, edge_ref[level, field, r : r + SUB, :])
        ups = (src_ref[plane + 1, r : r + SUB, :], src_ref[plane, r + 1 : r + 1 + SUB, :], x_up)
        downs = (src_ref[plane - 1, r : r + SUB, :], src_ref[plane, r - 1 : r - 1 + SUB, :], x_down)
        return stencil(u, coefs, ups, downs, speed[field])

    def depth_mask(zi):
        return jnp.where(zi < W, flag[0], jnp.where(zi >= W + depth_len, flag[1], 1.0))

    for field in range(nfield + 1):
        edges(0, field)
    for r in tiles_of(1, rows + 2 * W - 1):
        side_step(0, nfield, r)
    for field in range(nfield):
        edges(1, field)
    for r in tiles_of(2, rows + 2 * W - 2):
        side_step(1, 1, r)
    edges(2, 0)

    @pl.loop(1, planes - 1)
    def _(zi):
        zmask = depth_mask(zi)
        for r in tiles_of(1, rows + 2 * W - 1):
            mask = row_mask(r) * zmask
            coefs = kappa_coefs(zi, r)
            for field in range(nfield):
                next_ref[field * planes + zi, r : r + SUB, :] = mask * step_value(
                    pad_ref, 0, field, zi, r, coefs
                )

    @pl.loop(2, planes - 2)
    def _(zi):
        zmask = depth_mask(zi)
        for r in tiles_of(2, rows + 2 * W - 2):
            value = step_value(next_ref, 1, 0, zi, r, kappa_coefs(zi, r))
            last_ref[zi, r : r + SUB, :] = value * (row_mask(r) * zmask)

    @pl.loop(0, depth_len)
    def _(z):
        zi = z + W
        for r in range(W, W + rows, SUB):
            coefs = kappa_coefs(zi, r)
            s = last_ref[zi, r : r + SUB, :]
            state_ref[0, z, r - W : r - W + SUB, :] = s
            x_up, x_down = along_x(s, zi, edge_ref[2, 0, r : r + SUB, :])
            g_z = 0.5 * (last_ref[zi + 1, r : r + SUB, :] - last_ref[zi - 1, r : r + SUB, :])
            g_y = 0.5 * (last_ref[zi, r + 1 : r + 1 + SUB, :] - last_ref[zi, r - 1 : r - 1 + SUB, :])
            g_x = 0.5 * (x_up - x_down)
            shade = 0.35 + 0.65 * jnp.abs(0.64 * g_z + 0.6 * g_y + 0.48 * g_x) * lax.rsqrt(
                g_z * g_z + g_y * g_y + g_x * g_x + 1.0
            )
            for field in range(1, nfield):
                value = step_value(next_ref, 1, field, zi, r, coefs)
                state_ref[field, z, r - W : r - W + SUB, :] = value
                if field <= 3:
                    base_ref[field, z, r - W : r - W + SUB, :] = shade * (0.5 + 0.5 * jnp.tanh(0.5 * value))
                if field == 4:
                    base_ref[0, z, r - W : r - W + SUB, :] = 1.0 + 0.5 * jnp.tanh(value)

    ntf = center_ref.shape[0]
    chunk = 4 if ntf % 4 == 0 else 1
    halves = rows // SUB

    @pl.loop(0, (ntf // chunk) * halves)
    def _(step):
        first = (step // halves) * chunk
        row = pl.multiple_of((step % halves) * SUB, SUB)
        shape = (SUB, lanes)
        mid = [jnp.full(shape, center_ref[first + j], jnp.float32) for j in range(chunk)]
        bend = [jnp.full(shape, sharp_ref[first + j] * -LOG2E, jnp.float32) for j in range(chunk)]
        dense = [jnp.full(shape, gain_ref[first + j] * -LOG2E, jnp.float32) for j in range(chunk)]
        passed = [jnp.ones(shape, jnp.float32)] * chunk
        total = [jnp.zeros(shape, jnp.float32)] * chunk
        acc = [[jnp.zeros(shape, jnp.float32)] * 3 for _ in range(chunk)]
        for z in range(depth_len):
            s = state_ref[0, z, pl.ds(row, SUB), :]
            modul = base_ref[0, z, pl.ds(row, SUB), :]
            base = [base_ref[k + 1, z, pl.ds(row, SUB), :] for k in range(3)]
            for j in range(chunk):
                diff = s - mid[j]
                total[j] = total[j] + modul * jnp.exp2(diff * diff * bend[j])
                after = jnp.exp2(total[j] * dense[j])
                weight = passed[j] - after
                passed[j] = after
                acc[j] = [acc[j][k] + weight * base[k] for k in range(3)]
        for j in range(chunk):
            start = ((first + j) * rows + row) * 4
            for k in range(3):
                tile_ref[pl.ds(start + k, SUB, stride=4), :] = acc[j][k] * color_ref[k, first + j]
            tile_ref[pl.ds(start + 3, SUB, stride=4), :] = 1.0 - passed[j]

    @pl.loop(0, order_ref.shape[0], unroll=8)
    def _(slot):
        tile = order_ref[slot]
        cover = mask_ref[tile].astype(jnp.float32)
        out_ref[slot] = tile_ref[pl.ds(pl.multiple_of(tile * 4, 4), 4), :] * cover


def compose_kernel(part_ref, out_ref):
    slabs, rows, _ = part_ref.shape

    @pl.loop(0, rows // 32)
    def _(step):
        def load(slab, k):
            return part_ref[slab, pl.ds(step * 32 + k, 8, stride=4), :]

        acc = [load(0, k) for k in range(4)]
        for slab in range(1, slabs):
            clear = 1.0 - acc[3]
            acc = [acc[k] + clear * load(slab, k) for k in range(4)]
        for k in range(4):
            out_ref[pl.ds(step * 32 + k, 8, stride=4), :] = acc[k]


def compose(parts):
    vmem = pl.BlockSpec(memory_space=pltpu.VMEM)
    return pl.pallas_call(
        compose_kernel,
        out_shape=jax.ShapeDtypeStruct(parts.shape[1:], jnp.float32),
        in_specs=[vmem],
        out_specs=vmem,
        compiler_params=pltpu.CompilerParams(vmem_limit_bytes=32 * 1024 * 1024),
        name="compose",
    )(parts)


def shift(message, axis, up):
    count = lax.axis_size(axis)
    pairs = [(i, i + 1) if up else (i + 1, i) for i in range(count - 1)]
    return lax.ppermute(message, axis, pairs)


def present(axis):
    here = lax.axis_index(axis)
    return [(here > 0).astype(F32), (here < lax.axis_size(axis) - 1).astype(F32)]


def shards(
    fields, diffusivity, courant, tf_center, tf_sharp, tf_gain, tf_color, tile_mask, tile_perm
):
    nfield, depth_len, rows_len, cols_len = fields.shape
    planes, pitch = depth_len + 2 * W, rows_len + 8
    smem = pl.BlockSpec(memory_space=pltpu.SMEM)
    vmem = pl.BlockSpec(memory_space=pltpu.VMEM)
    params = pltpu.CompilerParams(vmem_limit_bytes=40 * 1024 * 1024)

    def array(*shape):
        return jax.ShapeDtypeStruct(shape, F32)

    flags = jnp.stack(present("gz") + present("gy") + present("gx"))

    def z_faces(low):
        faces = []
        for field in range(nfield + 1):
            wide = reach(field, nfield)
            source = diffusivity if field == nfield else fields[field]
            faces.append(source[:wide] if low else source[depth_len - wide :])
        return jnp.concatenate(faces, 0)

    zlo = shift(z_faces(False), "gz", True)
    zhi = shift(z_faces(True), "gz", False)
    used = y_plan(nfield, depth_len)[1]
    send_lo, send_hi = pl.pallas_call(
        pack_rows_kernel,
        out_shape=(array(used, cols_len), array(used, cols_len)),
        in_specs=[vmem] * 4,
        out_specs=(vmem, vmem),
        compiler_params=params,
        name="pack_rows",
    )(fields, diffusivity, zlo, zhi)
    if lax.axis_size("gy") == 2:
        mine = jnp.where(lax.axis_index("gy") == 0, send_hi, send_lo)
        ylo = yhi = lax.ppermute(mine, "gy", [(0, 1), (1, 0)])
    else:
        ylo = shift(send_hi, "gy", True)
        yhi = shift(send_lo, "gy", False)
    pad = pltpu.VMEM(((nfield + 1) * planes, pitch, cols_len), F32)
    own_lo, own_hi = pl.pallas_call(
        pack_columns_kernel,
        out_shape=(array(nfield + 1, pitch, cols_len),) * 2,
        in_specs=[smem] + [vmem] * 6,
        out_specs=(vmem, vmem),
        scratch_shapes=[pad],
        compiler_params=params,
        name="pack_columns",
    )(flags, fields, diffusivity, zlo, zhi, ylo, yhi)
    xlo = shift(own_hi, "gx", True)
    xhi = shift(own_lo, "gx", False)
    count = lax.axis_size("gz")
    order = tile_perm[0, 0]
    per_owner = order.shape[0] // count
    state, tiles = pl.pallas_call(
        main_kernel,
        out_shape=(array(*fields.shape), array(order.shape[0], 4, cols_len)),
        in_specs=[smem] * 8 + [vmem] * 10,
        out_specs=(vmem, vmem),
        scratch_shapes=[
            pad,
            pltpu.VMEM((nfield * planes, pitch, cols_len), F32),
            pltpu.VMEM((planes, pitch, cols_len), F32),
            pltpu.VMEM((3, 2, 2, nfield + 1, pitch, cols_len), F32),
            pltpu.VMEM((3, nfield + 1, pitch, cols_len), F32),
            pltpu.VMEM((4, depth_len, rows_len, cols_len), F32),
            pltpu.VMEM((order.shape[0] * 4, cols_len), F32),
        ],
        compiler_params=params,
        name="step_and_march",
    )(
        flags, courant, tf_center, tf_sharp, tf_gain, tf_color, tile_mask[0].reshape(-1), order,
        fields, diffusivity, zlo, zhi, ylo, yhi, xlo, xhi, own_lo, own_hi,
    )
    grouped = tiles.reshape(count, per_owner * 4, cols_len)
    composed = compose(lax.all_to_all(grouped, "gz", split_axis=0, concat_axis=0, tiled=True))
    picture = composed.reshape(1, 1, per_owner, 4, cols_len)
    return (state, picture)


def solution(mesh):
    return jax.shard_map(
        shards,
        mesh=mesh,
        in_specs=(
            P(None, "gz", "gy", "gx"),
            P("gz", "gy", "gx"),
            P(),
            P(),
            P(),
            P(),
            P(),
            P("gz", None, "gy", "gx"),
            P("gy", "gx", None),
        ),
        out_specs=(P(None, "gz", "gy", "gx"), P("gy", "gx", "gz", None, None)),
        check_vma=False,
    )
```

```python
import jax
import jax.numpy as jnp
from jax import lax
from jax.experimental import pallas as pl
from jax.experimental.pallas import tpu as pltpu
from jax.sharding import PartitionSpec as P

LOG2E = 1.4426950408889634
W = 3
SUB = 8
F32 = jnp.float32


def reach(field, nfield):
    return W if field in (0, nfield) else W - 1


def tiles_of(first, last):
    return [min(start, last - SUB) for start in range(first, last, SUB)]


def z_plan(nfield):
    plan, at = [], 0
    for field in range(nfield + 1):
        plan.append((field, at, reach(field, nfield)))
        at += reach(field, nfield)
    return plan, at


def y_plan(nfield, depth_len):
    plan, at = [], 0
    for field in range(nfield + 1):
        wide = reach(field, nfield)
        for away in range(1, wide + 1):
            extra = wide - away
            plan.append((field, away, -extra, depth_len + 2 * extra, at))
            at += depth_len + 2 * extra
    return plan, at + (-at) % SUB


def pack_planes_kernel(fields_ref, kappa_ref, lo_ref, hi_ref):
    nfield, depth_len = fields_ref.shape[:2]
    for field, at, wide in z_plan(nfield)[0]:
        source = kappa_ref if field == nfield else fields_ref.at[field]
        for k in range(wide):
            lo_ref[at + k] = source[k]
            hi_ref[at + k] = source[depth_len - wide + k]


def source_plane(refs, field, z):
    fields_ref, kappa_ref, zlo_ref, zhi_ref = refs
    nfield, depth_len = fields_ref.shape[:2]
    _, at, wide = z_plan(nfield)[0][field]
    if z < 0:
        return zlo_ref.at[at + wide + z]
    if z >= depth_len:
        return zhi_ref.at[at + z - depth_len]
    return kappa_ref.at[z] if field == nfield else fields_ref.at[field, z]


def pack_rows_kernel(fields_ref, kappa_ref, zlo_ref, zhi_ref, lo_ref, hi_ref):
    refs = (fields_ref, kappa_ref, zlo_ref, zhi_ref)
    nfield, depth_len, rows, lanes = fields_ref.shape
    flat_fields = fields_ref.reshape(nfield * depth_len * rows, lanes)
    flat_kappa = kappa_ref.reshape(depth_len * rows, lanes)
    plan, used = y_plan(nfield, depth_len)
    for out_ref, top in ((lo_ref, True), (hi_ref, False)):
        for field, away, first, length, at in plan:
            row = away - 1 if top else rows - away
            for z in list(range(first, 0)) + list(range(depth_len, first + length)):
                out_ref[at + z - first, :] = source_plane(refs, field, z)[row, :]
            flat, base = (flat_kappa, 0) if field == nfield else (flat_fields, field * depth_len * rows)
            for z in range(0, depth_len, SUB):
                out_ref[pl.ds(at - first + z, SUB), :] = flat[
                    pl.ds(base + z * rows + row, SUB, stride=rows), :
                ]
        spare = plan[-1][3] + plan[-1][4]
        if used > spare:
            out_ref[spare:used, :] = jnp.zeros((used - spare, lanes), F32)


def assemble(refs, ylo_ref, yhi_ref, flags_ref, pad_ref):
    fields_ref, kappa_ref, zlo_ref, zhi_ref = refs
    nfield, depth_len, rows, lanes = fields_ref.shape
    planes, pitch = depth_len + 2 * W, rows + SUB
    halo = jnp.zeros((SUB, lanes), F32)

    @pl.loop(0, depth_len)
    def _(z):
        for field in range(nfield + 1):
            plane = field * planes + W + z
            pad_ref[plane, :rows, :] = kappa_ref[z] if field == nfield else fields_ref[field, z]
            pad_ref[plane, rows:, :] = halo

    for field, at, wide in z_plan(nfield)[0]:
        for k in range(W):
            below, above = field * planes + W - 1 - k, field * planes + W + depth_len + k
            if k < wide:
                pad_ref[below, :rows, :] = zlo_ref[at + wide - 1 - k]
                pad_ref[above, :rows, :] = zhi_ref[at + k]
            for plane in (below, above):
                if k >= wide:
                    pad_ref[plane, :rows, :] = jnp.zeros((rows, lanes), F32)
                pad_ref[plane, rows:, :] = halo
    flat = pad_ref.reshape((nfield + 1) * planes * pitch, lanes)
    low, high = flags_ref[2], flags_ref[3]
    for field, away, first, length, at in y_plan(nfield, depth_len)[0]:
        for ref, flag, row in ((ylo_ref, low, pitch - away), (yhi_ref, high, rows + away - 1)):
            for start in tiles_of(0, length):
                flat[pl.ds((field * planes + W + first + start) * pitch + row, SUB, stride=pitch), :] = (
                    ref[pl.ds(at + start, SUB), :] * flag
                )


def pack_columns_kernel(
    flags_ref, fields_ref, kappa_ref, zlo_ref, zhi_ref, ylo_ref, yhi_ref, lo_ref, hi_ref, pad_ref
):
    refs = (fields_ref, kappa_ref, zlo_ref, zhi_ref)
    nfield, depth_len, rows, lanes = fields_ref.shape
    planes, pitch = depth_len + 2 * W, rows + SUB
    assemble(refs, ylo_ref, yhi_ref, flags_ref, pad_ref)
    lane = lax.broadcasted_iota(jnp.int32, (pitch, lanes), 1)
    group = (nfield + 1) // 2

    for start in range(0, nfield + 1, group):

        def body(zi, carry):
            mine = (lane >= W * zi) & (lane < W * zi + W)
            fresh = []
            for field in range(start, start + group):
                low, high = carry[field - start]
                value = pad_ref[field * planes + zi]
                low = jnp.where(mine, pltpu.roll(value, W * zi, 1), low)
                high = jnp.where(mine, pltpu.roll(value, lax.rem(W * zi + W, lanes), 1), high)
                fresh.append((low, high))
            return tuple(fresh)

        zero = jnp.zeros((pitch, lanes), F32)
        done = lax.fori_loop(0, planes, body, ((zero, zero),) * group)
        for field in range(start, start + group):
            lo_ref[field], hi_ref[field] = done[field - start]


def stencil(u, coefs, ups, downs, speeds):
    total = (coefs[3] - (speeds[0] + speeds[1] + speeds[2])) * u
    for axis in range(3):
        k_up, k_down = coefs[axis]
        total = total + k_up * ups[axis] + (k_down + speeds[axis]) * downs[axis]
    return total


def weights(k, ups, downs):
    half = 0.5 * k
    coefs = [(half + 0.5 * ups[a], half + 0.5 * downs[a]) for a in range(3)]
    rest = 1.0
    for up, down in coefs:
        rest = rest - (up + down)
    return coefs + [rest]


def side_neighbours(near, own, is_left, lanes, col):
    first, second = (near, own) if is_left else (own, near)
    first_up = jnp.where(col == W - 1, pltpu.roll(second, W - 1, 1), pltpu.roll(first, lanes - 1, 1))
    first_down = pltpu.roll(first, 1, 1)
    second_up = pltpu.roll(second, lanes - 1, 1)
    second_down = jnp.where(col == 0, pltpu.roll(first, lanes - (W - 1), 1), pltpu.roll(second, 1, 1))
    pair = ((first_up, first_down), (second_up, second_down))
    return pair if is_left else (pair[1], pair[0])


def main_kernel(
    flags_ref, courant_ref, center_ref, sharp_ref, gain_ref, color_ref, mask_ref, order_ref,
    pad_ref, xlo_ref, xhi_ref, ownlo_ref, ownhi_ref,
    state_ref, out_ref,
    next_ref, last_ref, side_ref, edge_ref, base_ref, tile_ref,
):
    nfield, depth_len, rows, lanes = state_ref.shape
    planes, pitch = depth_len + 2 * W, rows + SUB
    lane = lax.broadcasted_iota(jnp.int32, (pitch, lanes), 1)
    r = lax.broadcasted_iota(jnp.int32, (pitch, lanes), 0)
    zi_of = lane // W
    col = lane - zi_of * W
    flag = [flags_ref[i] for i in range(6)]
    speed = [[courant_ref[f, a] for a in range(3)] for f in range(nfield)]
    row_mask = jnp.where(r < rows, 1.0, jnp.where(r < rows + SUB // 2, flag[3], flag[2]))

    def along_y(value):
        return pltpu.roll(value, pitch - 1, 0), pltpu.roll(value, 1, 0)

    sides = ((xlo_ref, ownlo_ref, True, flag[4]), (xhi_ref, ownhi_ref, False, flag[5]))

    def block_of(level, side, block, field):
        if level == 0 or field == nfield:
            return sides[side][block][field]
        return side_ref[level - 1, side, block, field]

    def edges(level, field):
        left, right = block_of(level, 0, 0, field), block_of(level, 1, 0, field)
        edge_ref[level, field] = jnp.where(col == W - 1, left, pltpu.roll(right, 1, 1))

    def side_step(level, count):
        zmask = row_mask * jnp.where(
            zi_of < W, flag[0], jnp.where(zi_of >= W + depth_len, flag[1], 1.0)
        )
        for side, (_, _, is_left, present) in enumerate(sides):
            blocks = (0, 1) if level == 0 else (0,)

            def around(lvl, field):
                pair = [block_of(lvl, side, block, field) for block in (0, 1)]
                x = side_neighbours(pair[0], pair[1], is_left, lanes, col)
                found = []
                for block in blocks:
                    value = pair[block]
                    y_up, y_down = along_y(value)
                    ups = (pltpu.roll(value, lanes - W, 1), y_up, x[block][0])
                    downs = (pltpu.roll(value, W, 1), y_down, x[block][1])
                    found.append((value, ups, downs))
                return found

            coefs = [weights(*found) for found in around(0, nfield)]
            for field in range(count):
                for block, (u, ups, downs) in zip(blocks, around(level, field)):
                    value = stencil(u, coefs[block], ups, downs, speed[field])
                    side_ref[level, side, block, field] = value * (zmask * present if block == 0 else zmask)

    def along_x(value, zi, edge):
        n = value.shape[0]
        turned = pltpu.roll(edge, lax.rem(2 * lanes - 2 - W * zi, lanes), 1)
        up = jnp.where(lane[:n] == lanes - 1, turned, pltpu.roll(value, lanes - 1, 1))
        down = jnp.where(lane[:n] == 0, turned, pltpu.roll(value, 1, 1))
        return up, down

    def around(src_ref, level, field, zi, n):
        plane = field * planes + zi
        whole = src_ref[plane]
        value = whole[:n]
        y_up, y_down = along_y(whole)
        x_up, x_down = along_x(value, zi, edge_ref[level, field, :n, :])
        return (
            value,
            (src_ref[plane + 1, :n, :], y_up[:n], x_up),
            (src_ref[plane - 1, :n, :], y_down[:n], x_down),
        )

    def step_value(src_ref, level, field, zi, n, coefs):
        u, ups, downs = around(src_ref, level, field, zi, n)
        return stencil(u, coefs, ups, downs, speed[field])

    def depth_mask(zi):
        return jnp.where(zi < W, flag[0], jnp.where(zi >= W + depth_len, flag[1], 1.0))

    for field in range(nfield + 1):
        edges(0, field)
    side_step(0, nfield)
    for field in range(nfield):
        edges(1, field)
    side_step(1, 1)
    edges(2, 0)

    @pl.loop(1, planes - 1)
    def _(zi):
        mask = row_mask * depth_mask(zi)
        coefs = weights(*around(pad_ref, 0, nfield, zi, pitch))
        for field in range(nfield):
            next_ref[field * planes + zi] = mask * step_value(pad_ref, 0, field, zi, pitch, coefs)

    @pl.loop(2, planes - 2)
    def _(zi):
        coefs = weights(*around(pad_ref, 0, nfield, zi, pitch))
        last_ref[zi] = step_value(next_ref, 1, 0, zi, pitch, coefs) * (row_mask * depth_mask(zi))

    @pl.loop(0, depth_len)
    def _(z):
        zi = z + W
        coefs = weights(*around(pad_ref, 0, nfield, zi, rows))
        s, ups, downs = around(last_ref, 2, 0, zi, rows)
        state_ref[0, z] = s
        g_z, g_y, g_x = [0.5 * (ups[a] - downs[a]) for a in range(3)]
        shade = 0.35 + 0.65 * jnp.abs(0.64 * g_z + 0.6 * g_y + 0.48 * g_x) * lax.rsqrt(
            g_z * g_z + g_y * g_y + g_x * g_x + 1.0
        )
        for field in range(1, nfield):
            value = step_value(next_ref, 1, field, zi, rows, coefs)
            state_ref[field, z] = value
            if field <= 3:
                base_ref[field, z] = shade * (0.5 + 0.5 * jnp.tanh(0.5 * value))
            if field == 4:
                base_ref[0, z] = 1.0 + 0.5 * jnp.tanh(value)

    ntf = center_ref.shape[0]
    chunk = 4 if ntf % 4 == 0 else 1
    halves = rows // SUB

    @pl.loop(0, (ntf // chunk) * halves)
    def _(step):
        first = (step // halves) * chunk
        row = pl.multiple_of((step % halves) * SUB, SUB)
        shape = (SUB, lanes)
        mid = [jnp.full(shape, center_ref[first + j], jnp.float32) for j in range(chunk)]
        bend = [jnp.full(shape, sharp_ref[first + j] * -LOG2E, jnp.float32) for j in range(chunk)]
        dense = [jnp.full(shape, gain_ref[first + j] * -LOG2E, jnp.float32) for j in range(chunk)]
        passed = [jnp.ones(shape, jnp.float32)] * chunk
        total = [jnp.zeros(shape, jnp.float32)] * chunk
        acc = [[jnp.zeros(shape, jnp.float32)] * 3 for _ in range(chunk)]
        for z in range(depth_len):
            s = state_ref[0, z, pl.ds(row, SUB), :]
            modul = base_ref[0, z, pl.ds(row, SUB), :]
            base = [base_ref[k + 1, z, pl.ds(row, SUB), :] for k in range(3)]
            for j in range(chunk):
                diff = s - mid[j]
                total[j] = total[j] + modul * jnp.exp2(diff * diff * bend[j])
                after = jnp.exp2(total[j] * dense[j])
                weight = passed[j] - after
                passed[j] = after
                acc[j] = [acc[j][k] + weight * base[k] for k in range(3)]
        for j in range(chunk):
            start = ((first + j) * rows + row) * 4
            for k in range(3):
                tile_ref[pl.ds(start + k, SUB, stride=4), :] = acc[j][k] * color_ref[k, first + j]
            tile_ref[pl.ds(start + 3, SUB, stride=4), :] = 1.0 - passed[j]

    @pl.loop(0, order_ref.shape[0], unroll=8)
    def _(slot):
        tile = order_ref[slot]
        cover = mask_ref[tile].astype(jnp.float32)
        out_ref[slot] = tile_ref[pl.ds(pl.multiple_of(tile * 4, 4), 4), :] * cover


def compose_kernel(part_ref, out_ref):
    slabs, rows, _ = part_ref.shape

    @pl.loop(0, rows // 32)
    def _(step):
        def load(slab, k):
            return part_ref[slab, pl.ds(step * 32 + k, 8, stride=4), :]

        acc = [load(0, k) for k in range(4)]
        for slab in range(1, slabs):
            clear = 1.0 - acc[3]
            acc = [acc[k] + clear * load(slab, k) for k in range(4)]
        for k in range(4):
            out_ref[pl.ds(step * 32 + k, 8, stride=4), :] = acc[k]


def compose(parts):
    vmem = pl.BlockSpec(memory_space=pltpu.VMEM)
    return pl.pallas_call(
        compose_kernel,
        out_shape=jax.ShapeDtypeStruct(parts.shape[1:], jnp.float32),
        in_specs=[vmem],
        out_specs=vmem,
        compiler_params=pltpu.CompilerParams(vmem_limit_bytes=16 * 1024 * 1024),
        name="compose",
    )(parts)


def shift(message, axis, up):
    count = lax.axis_size(axis)
    pairs = [(i, i + 1) if up else (i + 1, i) for i in range(count - 1)]
    return lax.ppermute(message, axis, pairs)


def present(axis):
    here = lax.axis_index(axis)
    return [(here > 0).astype(F32), (here < lax.axis_size(axis) - 1).astype(F32)]


def shards(
    fields, diffusivity, courant, tf_center, tf_sharp, tf_gain, tf_color, tile_mask, tile_perm
):
    nfield, depth_len, rows_len, cols_len = fields.shape
    planes, pitch = depth_len + 2 * W, rows_len + SUB
    smem = pl.BlockSpec(memory_space=pltpu.SMEM)
    vmem = pl.BlockSpec(memory_space=pltpu.VMEM)
    params = pltpu.CompilerParams(vmem_limit_bytes=16 * 1024 * 1024)

    def array(*shape):
        return jax.ShapeDtypeStruct(shape, F32)

    flags = jnp.stack(present("gz") + present("gy") + present("gx"))

    faces = z_plan(nfield)[1]
    face_lo, face_hi = pl.pallas_call(
        pack_planes_kernel,
        out_shape=(array(faces, rows_len, cols_len),) * 2,
        in_specs=[vmem] * 2,
        out_specs=(vmem, vmem),
        compiler_params=params,
        name="pack_planes",
    )(fields, diffusivity)
    zlo = shift(face_hi, "gz", True)
    zhi = shift(face_lo, "gz", False)
    used = y_plan(nfield, depth_len)[1]
    send_lo, send_hi = pl.pallas_call(
        pack_rows_kernel,
        out_shape=(array(used, cols_len), array(used, cols_len)),
        in_specs=[vmem] * 4,
        out_specs=(vmem, vmem),
        compiler_params=params,
        name="pack_rows",
    )(fields, diffusivity, zlo, zhi)
    if lax.axis_size("gy") == 2:
        mine = jnp.where(lax.axis_index("gy") == 0, send_hi, send_lo)
        ylo = yhi = lax.ppermute(mine, "gy", [(0, 1), (1, 0)])
    else:
        ylo = shift(send_hi, "gy", True)
        yhi = shift(send_lo, "gy", False)
    own_lo, own_hi, pad = pl.pallas_call(
        pack_columns_kernel,
        out_shape=(array(nfield + 1, pitch, cols_len),) * 2
        + (array((nfield + 1) * planes, pitch, cols_len),),
        in_specs=[smem] + [vmem] * 6,
        out_specs=(vmem,) * 3,
        compiler_params=params,
        name="pack_columns",
    )(flags, fields, diffusivity, zlo, zhi, ylo, yhi)
    xlo = shift(own_hi, "gx", True)
    xhi = shift(own_lo, "gx", False)
    count = lax.axis_size("gz")
    order = tile_perm[0, 0]
    per_owner = order.shape[0] // count
    state, tiles = pl.pallas_call(
        main_kernel,
        out_shape=(array(*fields.shape), array(order.shape[0], 4, cols_len)),
        in_specs=[smem] * 8 + [vmem] * 5,
        out_specs=(vmem, vmem),
        scratch_shapes=[
            pltpu.VMEM((nfield * planes, pitch, cols_len), F32),
            pltpu.VMEM((planes, pitch, cols_len), F32),
            pltpu.VMEM((2, 2, 2, nfield, pitch, cols_len), F32),
            pltpu.VMEM((3, nfield + 1, pitch, cols_len), F32),
            pltpu.VMEM((4, depth_len, rows_len, cols_len), F32),
            pltpu.VMEM((order.shape[0] * 4, cols_len), F32),
        ],
        compiler_params=params,
        name="step_and_march",
    )(
        flags, courant, tf_center, tf_sharp, tf_gain, tf_color, tile_mask[0].reshape(-1), order,
        pad, xlo, xhi, own_lo, own_hi,
    )
    grouped = tiles.reshape(count, per_owner * 4, cols_len)
    composed = compose(lax.all_to_all(grouped, "gz", split_axis=0, concat_axis=0, tiled=True))
    picture = composed.reshape(1, 1, per_owner, 4, cols_len)
    return (state, picture)


def solution(mesh):
    return jax.shard_map(
        shards,
        mesh=mesh,
        in_specs=(
            P(None, "gz", "gy", "gx"),
            P("gz", "gy", "gx"),
            P(),
            P(),
            P(),
            P(),
            P(),
            P("gz", None, "gy", "gx"),
            P("gy", "gx", None),
        ),
        out_specs=(P(None, "gz", "gy", "gx"), P("gy", "gx", "gz", None, None)),
        check_vma=False,
    )
```

```python
import jax
import jax.numpy as jnp
from jax import lax
from jax.experimental import pallas as pl
from jax.experimental.pallas import tpu as pltpu
from jax.sharding import PartitionSpec as P

LOG2E = 1.4426950408889634
W = 3
SUB = 8
F32 = jnp.float32


def reach(field, nfield):
    return W if field in (0, nfield) else W - 1


def tiles_of(first, last):
    return [min(start, last - SUB) for start in range(first, last, SUB)]


def z_plan(nfield):
    plan, at = [], 0
    for field in range(nfield + 1):
        plan.append((field, at, reach(field, nfield)))
        at += reach(field, nfield)
    return plan, at


def y_plan(nfield, depth_len):
    plan, at = [], 0
    for field in range(nfield + 1):
        wide = reach(field, nfield)
        for away in range(1, wide + 1):
            extra = wide - away
            plan.append((field, away, -extra, depth_len + 2 * extra, at))
            at += depth_len + 2 * extra
    return plan, at + (-at) % SUB


def pack_planes_kernel(fields_ref, kappa_ref, lo_ref, hi_ref, sems):
    nfield, depth_len = fields_ref.shape[:2]
    copies = []
    for field, at, wide in z_plan(nfield)[0]:
        source = kappa_ref if field == nfield else fields_ref.at[field]
        for first, target in ((0, lo_ref), (depth_len - wide, hi_ref)):
            copies.append(
                pltpu.make_async_copy(
                    source.at[pl.ds(first, wide)], target.at[pl.ds(at, wide)], sems.at[len(copies)]
                )
            )
    for copy in copies:
        copy.start()
    for copy in copies:
        copy.wait()


def steps(count, most):
    return max(k for k in range(1, most + 1) if count % k == 0)


def source_plane(refs, field, z):
    fields_ref, kappa_ref, zlo_ref, zhi_ref = refs
    nfield, depth_len = fields_ref.shape[:2]
    _, at, wide = z_plan(nfield)[0][field]
    if z < 0:
        return zlo_ref.at[at + wide + z]
    if z >= depth_len:
        return zhi_ref.at[at + z - depth_len]
    return kappa_ref.at[z] if field == nfield else fields_ref.at[field, z]


def pack_rows_kernel(fields_ref, kappa_ref, zlo_ref, zhi_ref, lo_ref, hi_ref):
    refs = (fields_ref, kappa_ref, zlo_ref, zhi_ref)
    nfield, depth_len, rows, lanes = fields_ref.shape
    flat_fields = fields_ref.reshape(nfield * depth_len * rows, lanes)
    flat_kappa = kappa_ref.reshape(depth_len * rows, lanes)
    plan, used = y_plan(nfield, depth_len)
    for out_ref, top in ((lo_ref, True), (hi_ref, False)):
        for field, away, first, length, at in plan:
            row = away - 1 if top else rows - away
            for z in list(range(first, 0)) + list(range(depth_len, first + length)):
                out_ref[at + z - first, :] = source_plane(refs, field, z)[row, :]
            flat, base = (flat_kappa, 0) if field == nfield else (flat_fields, field * depth_len * rows)
            for z in range(0, depth_len, SUB):
                out_ref[pl.ds(at - first + z, SUB), :] = flat[
                    pl.ds(base + z * rows + row, SUB, stride=rows), :
                ]
        spare = plan[-1][3] + plan[-1][4]
        if used > spare:
            out_ref[spare:used, :] = jnp.zeros((used - spare, lanes), F32)


def assemble(refs, ylo_ref, yhi_ref, flags_ref, pad_ref):
    fields_ref, kappa_ref, zlo_ref, zhi_ref = refs
    nfield, depth_len, rows, lanes = fields_ref.shape
    planes, pitch = depth_len + 2 * W, rows + SUB
    halo = jnp.zeros((SUB, lanes), F32)

    @pl.loop(0, depth_len, unroll=steps(depth_len, 4))
    def _(z):
        for field in range(nfield + 1):
            plane = field * planes + W + z
            pad_ref[plane, :rows, :] = kappa_ref[z] if field == nfield else fields_ref[field, z]
            pad_ref[plane, rows:, :] = halo

    for field, at, wide in z_plan(nfield)[0]:
        for k in range(W):
            below, above = field * planes + W - 1 - k, field * planes + W + depth_len + k
            if k < wide:
                pad_ref[below, :rows, :] = zlo_ref[at + wide - 1 - k]
                pad_ref[above, :rows, :] = zhi_ref[at + k]
            for plane in (below, above):
                if k >= wide:
                    pad_ref[plane, :rows, :] = jnp.zeros((rows, lanes), F32)
                pad_ref[plane, rows:, :] = halo
    flat = pad_ref.reshape((nfield + 1) * planes * pitch, lanes)
    low, high = flags_ref[2], flags_ref[3]
    for field, away, first, length, at in y_plan(nfield, depth_len)[0]:
        for ref, flag, row in ((ylo_ref, low, pitch - away), (yhi_ref, high, rows + away - 1)):
            for start in tiles_of(0, length):
                flat[pl.ds((field * planes + W + first + start) * pitch + row, SUB, stride=pitch), :] = (
                    ref[pl.ds(at + start, SUB), :] * flag
                )


def pack_columns_kernel(
    flags_ref, fields_ref, kappa_ref, zlo_ref, zhi_ref, ylo_ref, yhi_ref, lo_ref, hi_ref, pad_ref
):
    refs = (fields_ref, kappa_ref, zlo_ref, zhi_ref)
    nfield, depth_len, rows, lanes = fields_ref.shape
    planes, pitch = depth_len + 2 * W, rows + SUB
    assemble(refs, ylo_ref, yhi_ref, flags_ref, pad_ref)
    lane = lax.broadcasted_iota(jnp.int32, (1, lanes), 1)

    @pl.loop(0, nfield + 1)
    def _(field):
        low = high = jnp.zeros((pitch, lanes), F32)
        for zi in range(planes):
            mine = (lane >= W * zi) & (lane < W * zi + W)
            value = pad_ref[field * planes + zi]
            low = jnp.where(mine, pltpu.roll(value, W * zi, 1), low)
            high = jnp.where(mine, pltpu.roll(value, (W * zi + W) % lanes, 1), high)
        lo_ref[field] = low
        hi_ref[field] = high


def stencil(u, coefs, ups, downs, speeds):
    total = (coefs[3] - (speeds[0] + speeds[1] + speeds[2])) * u
    for axis in range(3):
        k_up, k_down = coefs[axis]
        total = total + k_up * ups[axis] + (k_down + speeds[axis]) * downs[axis]
    return total


def weights(k, ups, downs):
    half = 0.5 * k
    coefs = [(half + 0.5 * ups[a], half + 0.5 * downs[a]) for a in range(3)]
    rest = 1.0
    for up, down in coefs:
        rest = rest - (up + down)
    return coefs + [rest]


def side_neighbours(near, own, is_left, lanes, col):
    first, second = (near, own) if is_left else (own, near)
    first_up = jnp.where(col == W - 1, pltpu.roll(second, W - 1, 1), pltpu.roll(first, lanes - 1, 1))
    first_down = pltpu.roll(first, 1, 1)
    second_up = pltpu.roll(second, lanes - 1, 1)
    second_down = jnp.where(col == 0, pltpu.roll(first, lanes - (W - 1), 1), pltpu.roll(second, 1, 1))
    pair = ((first_up, first_down), (second_up, second_down))
    return pair if is_left else (pair[1], pair[0])


def main_kernel(
    flags_ref, courant_ref, center_ref, sharp_ref, gain_ref, color_ref, mask_ref, order_ref,
    fields_ref, kappa_ref, zlo_ref, zhi_ref, ylo_ref, yhi_ref, xlo_ref, xhi_ref, ownlo_ref, ownhi_ref,
    state_ref, out_ref,
    pad_ref, next_ref, last_ref, side_ref, edge_ref, base_ref, tile_ref,
):
    nfield, depth_len, rows, lanes = state_ref.shape
    planes, pitch = depth_len + 2 * W, rows + SUB
    lane = lax.broadcasted_iota(jnp.int32, (pitch, lanes), 1)
    r = lax.broadcasted_iota(jnp.int32, (pitch, lanes), 0)
    zi_of = lane // W
    col = lane - zi_of * W
    flag = [flags_ref[i] for i in range(6)]
    speed = [[courant_ref[f, a] for a in range(3)] for f in range(nfield)]
    row_mask = jnp.where(r < rows, 1.0, jnp.where(r < rows + SUB // 2, flag[3], flag[2]))

    def along_y(value):
        return pltpu.roll(value, pitch - 1, 0), pltpu.roll(value, 1, 0)

    sides = ((xlo_ref, ownlo_ref, True, flag[4]), (xhi_ref, ownhi_ref, False, flag[5]))

    def block_of(level, side, block, field):
        if level == 0 or field == nfield:
            return sides[side][block][field]
        return side_ref[level - 1, side, block, field]

    def edges(level, field):
        left, right = block_of(level, 0, 0, field), block_of(level, 1, 0, field)
        edge_ref[level, field] = jnp.where(col == W - 1, left, pltpu.roll(right, 1, 1))

    def side_step(level, count):
        zmask = row_mask * jnp.where(
            zi_of < W, flag[0], jnp.where(zi_of >= W + depth_len, flag[1], 1.0)
        )
        for side, (_, _, is_left, present) in enumerate(sides):
            blocks = (0, 1) if level == 0 else (0,)

            def around(lvl, field):
                pair = [block_of(lvl, side, block, field) for block in (0, 1)]
                x = side_neighbours(pair[0], pair[1], is_left, lanes, col)
                found = []
                for block in blocks:
                    value = pair[block]
                    y_up, y_down = along_y(value)
                    ups = (pltpu.roll(value, lanes - W, 1), y_up, x[block][0])
                    downs = (pltpu.roll(value, W, 1), y_down, x[block][1])
                    found.append((value, ups, downs))
                return found

            coefs = [weights(*found) for found in around(0, nfield)]
            for field in range(count):
                for block, (u, ups, downs) in zip(blocks, around(level, field)):
                    value = stencil(u, coefs[block], ups, downs, speed[field])
                    side_ref[level, side, block, field] = value * (zmask * present if block == 0 else zmask)

    def along_x(value, zi, edge):
        n = value.shape[0]
        turned = pltpu.roll(edge, lax.rem(2 * lanes - 2 - W * zi, lanes), 1)
        up = jnp.where(lane[:n] == lanes - 1, turned, pltpu.roll(value, lanes - 1, 1))
        down = jnp.where(lane[:n] == 0, turned, pltpu.roll(value, 1, 1))
        return up, down

    def around(src_ref, level, field, zi, n):
        plane = field * planes + zi
        whole = src_ref[plane]
        value = whole[:n]
        y_up, y_down = along_y(whole)
        x_up, x_down = along_x(value, zi, edge_ref[level, field, :n, :])
        return (
            value,
            (src_ref[plane + 1, :n, :], y_up[:n], x_up),
            (src_ref[plane - 1, :n, :], y_down[:n], x_down),
        )

    def step_value(src_ref, level, field, zi, n, coefs):
        u, ups, downs = around(src_ref, level, field, zi, n)
        return stencil(u, coefs, ups, downs, speed[field])

    def depth_mask(zi):
        return jnp.where(zi < W, flag[0], jnp.where(zi >= W + depth_len, flag[1], 1.0))

    assemble((fields_ref, kappa_ref, zlo_ref, zhi_ref), ylo_ref, yhi_ref, flags_ref, pad_ref)
    for field in range(nfield + 1):
        edges(0, field)
    side_step(0, nfield)
    for field in range(nfield):
        edges(1, field)
    side_step(1, 1)
    edges(2, 0)

    @pl.loop(1, planes - 1, unroll=steps(planes - 2, 4))
    def _(zi):
        mask = row_mask * depth_mask(zi)
        coefs = weights(*around(pad_ref, 0, nfield, zi, pitch))
        for field in range(nfield):
            next_ref[field * planes + zi] = mask * step_value(pad_ref, 0, field, zi, pitch, coefs)

    @pl.loop(2, planes - 2, unroll=steps(planes - 4, 4))
    def _(zi):
        coefs = weights(*around(pad_ref, 0, nfield, zi, pitch))
        last_ref[zi] = step_value(next_ref, 1, 0, zi, pitch, coefs) * (row_mask * depth_mask(zi))

    @pl.loop(0, depth_len, unroll=steps(depth_len, 4))
    def _(z):
        zi = z + W
        coefs = weights(*around(pad_ref, 0, nfield, zi, rows))
        s, ups, downs = around(last_ref, 2, 0, zi, rows)
        state_ref[0, z] = s
        g_z, g_y, g_x = [0.5 * (ups[a] - downs[a]) for a in range(3)]
        shade = 0.35 + 0.65 * jnp.abs(0.64 * g_z + 0.6 * g_y + 0.48 * g_x) * lax.rsqrt(
            g_z * g_z + g_y * g_y + g_x * g_x + 1.0
        )
        for field in range(1, nfield):
            value = step_value(next_ref, 1, field, zi, rows, coefs)
            state_ref[field, z] = value
            if field <= 3:
                base_ref[field, z] = shade * (0.5 + 0.5 * jnp.tanh(0.5 * value))
            if field == 4:
                base_ref[0, z] = 1.0 + 0.5 * jnp.tanh(value)

    ntf = center_ref.shape[0]
    chunk = 4 if ntf % 4 == 0 else 1
    halves = rows // SUB

    @pl.loop(0, (ntf // chunk) * halves)
    def _(step):
        first = (step // halves) * chunk
        row = pl.multiple_of((step % halves) * SUB, SUB)
        shape = (SUB, lanes)
        mid = [jnp.full(shape, center_ref[first + j], jnp.float32) for j in range(chunk)]
        bend = [jnp.full(shape, sharp_ref[first + j] * -LOG2E, jnp.float32) for j in range(chunk)]
        dense = [jnp.full(shape, gain_ref[first + j] * -LOG2E, jnp.float32) for j in range(chunk)]
        passed = [jnp.ones(shape, jnp.float32)] * chunk
        total = [jnp.zeros(shape, jnp.float32)] * chunk
        acc = [[jnp.zeros(shape, jnp.float32)] * 3 for _ in range(chunk)]
        for z in range(depth_len):
            s = state_ref[0, z, pl.ds(row, SUB), :]
            modul = base_ref[0, z, pl.ds(row, SUB), :]
            base = [base_ref[k + 1, z, pl.ds(row, SUB), :] for k in range(3)]
            for j in range(chunk):
                diff = s - mid[j]
                total[j] = total[j] + modul * jnp.exp2(diff * diff * bend[j])
                after = jnp.exp2(total[j] * dense[j])
                weight = passed[j] - after
                passed[j] = after
                acc[j] = [acc[j][k] + weight * base[k] for k in range(3)]
        for j in range(chunk):
            start = ((first + j) * rows + row) * 4
            for k in range(3):
                tile_ref[pl.ds(start + k, SUB, stride=4), :] = acc[j][k] * color_ref[k, first + j]
            tile_ref[pl.ds(start + 3, SUB, stride=4), :] = 1.0 - passed[j]

    @pl.loop(0, order_ref.shape[0], unroll=8)
    def _(slot):
        tile = order_ref[slot]
        cover = mask_ref[tile].astype(jnp.float32)
        out_ref[slot] = tile_ref[pl.ds(pl.multiple_of(tile * 4, 4), 4), :] * cover


def compose_kernel(part_ref, out_ref):
    slabs, rows, _ = part_ref.shape

    @pl.loop(0, rows // 32)
    def _(step):
        def load(slab, k):
            return part_ref[slab, pl.ds(step * 32 + k, 8, stride=4), :]

        acc = [load(0, k) for k in range(4)]
        for slab in range(1, slabs):
            clear = 1.0 - acc[3]
            acc = [acc[k] + clear * load(slab, k) for k in range(4)]
        for k in range(4):
            out_ref[pl.ds(step * 32 + k, 8, stride=4), :] = acc[k]


def compose(parts):
    vmem = pl.BlockSpec(memory_space=pltpu.VMEM)
    return pl.pallas_call(
        compose_kernel,
        out_shape=jax.ShapeDtypeStruct(parts.shape[1:], jnp.float32),
        in_specs=[vmem],
        out_specs=vmem,
        compiler_params=pltpu.CompilerParams(vmem_limit_bytes=16 * 1024 * 1024),
        name="compose",
    )(parts)


def shift(message, axis, up):
    count = lax.axis_size(axis)
    pairs = [(i, i + 1) if up else (i + 1, i) for i in range(count - 1)]
    return lax.ppermute(message, axis, pairs)


def present(axis):
    here = lax.axis_index(axis)
    return [(here > 0).astype(F32), (here < lax.axis_size(axis) - 1).astype(F32)]


def shards(
    fields, diffusivity, courant, tf_center, tf_sharp, tf_gain, tf_color, tile_mask, tile_perm
):
    nfield, depth_len, rows_len, cols_len = fields.shape
    planes, pitch = depth_len + 2 * W, rows_len + SUB
    smem = pl.BlockSpec(memory_space=pltpu.SMEM)
    vmem = pl.BlockSpec(memory_space=pltpu.VMEM)
    params = pltpu.CompilerParams(vmem_limit_bytes=16 * 1024 * 1024)

    def array(*shape):
        return jax.ShapeDtypeStruct(shape, F32)

    flags = jnp.stack(present("gz") + present("gy") + present("gx"))

    faces = z_plan(nfield)[1]
    face_lo, face_hi = pl.pallas_call(
        pack_planes_kernel,
        out_shape=(array(faces, rows_len, cols_len),) * 2,
        in_specs=[pl.BlockSpec(memory_space=pl.ANY)] * 2,
        out_specs=(vmem, vmem),
        scratch_shapes=[pltpu.SemaphoreType.DMA((2 * nfield + 2,))],
        compiler_params=params,
        name="pack_planes",
    )(fields, diffusivity)
    zlo = shift(face_hi, "gz", True)
    zhi = shift(face_lo, "gz", False)
    used = y_plan(nfield, depth_len)[1]
    send_lo, send_hi = pl.pallas_call(
        pack_rows_kernel,
        out_shape=(array(used, cols_len), array(used, cols_len)),
        in_specs=[vmem] * 4,
        out_specs=(vmem, vmem),
        compiler_params=params,
        name="pack_rows",
    )(fields, diffusivity, zlo, zhi)
    if lax.axis_size("gy") == 2:
        mine = jnp.where(lax.axis_index("gy") == 0, send_hi, send_lo)
        ylo = yhi = lax.ppermute(mine, "gy", [(0, 1), (1, 0)])
    else:
        ylo = shift(send_hi, "gy", True)
        yhi = shift(send_lo, "gy", False)
    pad = pltpu.VMEM(((nfield + 1) * planes, pitch, cols_len), F32)
    own_lo, own_hi = pl.pallas_call(
        pack_columns_kernel,
        out_shape=(array(nfield + 1, pitch, cols_len),) * 2,
        in_specs=[smem] + [vmem] * 6,
        out_specs=(vmem,) * 2,
        scratch_shapes=[pad],
        compiler_params=params,
        name="pack_columns",
    )(flags, fields, diffusivity, zlo, zhi, ylo, yhi)
    xlo = shift(own_hi, "gx", True)
    xhi = shift(own_lo, "gx", False)
    count = lax.axis_size("gz")
    order = tile_perm[0, 0]
    per_owner = order.shape[0] // count
    state, tiles = pl.pallas_call(
        main_kernel,
        out_shape=(array(*fields.shape), array(order.shape[0], 4, cols_len)),
        in_specs=[smem] * 8 + [vmem] * 10,
        out_specs=(vmem, vmem),
        scratch_shapes=[
            pad,
            pltpu.VMEM((nfield * planes, pitch, cols_len), F32),
            pltpu.VMEM((planes, pitch, cols_len), F32),
            pltpu.VMEM((2, 2, 2, nfield, pitch, cols_len), F32),
            pltpu.VMEM((3, nfield + 1, pitch, cols_len), F32),
            pltpu.VMEM((4, depth_len, rows_len, cols_len), F32),
            pltpu.VMEM((order.shape[0] * 4, cols_len), F32),
        ],
        compiler_params=params,
        name="step_and_march",
    )(
        flags, courant, tf_center, tf_sharp, tf_gain, tf_color, tile_mask[0].reshape(-1), order,
        fields, diffusivity, zlo, zhi, ylo, yhi, xlo, xhi, own_lo, own_hi,
    )
    grouped = tiles.reshape(count, per_owner * 4, cols_len)
    composed = compose(lax.all_to_all(grouped, "gz", split_axis=0, concat_axis=0, tiled=True))
    picture = composed.reshape(1, 1, per_owner, 4, cols_len)
    return (state, picture)


def solution(mesh):
    return jax.shard_map(
        shards,
        mesh=mesh,
        in_specs=(
            P(None, "gz", "gy", "gx"),
            P("gz", "gy", "gx"),
            P(),
            P(),
            P(),
            P(),
            P(),
            P("gz", None, "gy", "gx"),
            P("gy", "gx", None),
        ),
        out_specs=(P(None, "gz", "gy", "gx"), P("gy", "gx", "gz", None, None)),
        check_vma=False,
    )
```

```python
import jax
import jax.numpy as jnp
from jax import lax
from jax.experimental import pallas as pl
from jax.experimental.pallas import tpu as pltpu
from jax.sharding import PartitionSpec as P

LOG2E = 1.4426950408889634
W = 3
SUB = 8
F32 = jnp.float32


def reach(field, nfield):
    return W if field in (0, nfield) else W - 1


def tiles_of(first, last):
    return [min(start, last - SUB) for start in range(first, last, SUB)]


def z_plan(nfield):
    plan, at = [], 0
    for field in range(nfield + 1):
        plan.append((field, at, reach(field, nfield)))
        at += reach(field, nfield)
    return plan, at


def y_plan(nfield, depth_len):
    plan, at = [], 0
    for field in range(nfield + 1):
        wide = reach(field, nfield)
        for away in range(1, wide + 1):
            extra = wide - away
            plan.append((field, away, -extra, depth_len + 2 * extra, at))
            at += depth_len + 2 * extra
    return plan, at + (-at) % SUB


def pack_planes_kernel(fields_ref, kappa_ref, lo_ref, hi_ref, sems):
    nfield, depth_len = fields_ref.shape[:2]
    copies = []
    for field, at, wide in z_plan(nfield)[0]:
        source = kappa_ref if field == nfield else fields_ref.at[field]
        for first, target in ((0, lo_ref), (depth_len - wide, hi_ref)):
            copies.append(
                pltpu.make_async_copy(
                    source.at[pl.ds(first, wide)], target.at[pl.ds(at, wide)], sems.at[len(copies)]
                )
            )
    for copy in copies:
        copy.start()
    for copy in copies:
        copy.wait()


def steps(count, most):
    return max(k for k in range(1, most + 1) if count % k == 0)


def source_plane(refs, field, z):
    fields_ref, kappa_ref, zlo_ref, zhi_ref = refs
    nfield, depth_len = fields_ref.shape[:2]
    _, at, wide = z_plan(nfield)[0][field]
    if z < 0:
        return zlo_ref.at[at + wide + z]
    if z >= depth_len:
        return zhi_ref.at[at + z - depth_len]
    return kappa_ref.at[z] if field == nfield else fields_ref.at[field, z]


def pack_rows_kernel(fields_ref, kappa_ref, zlo_ref, zhi_ref, lo_ref, hi_ref):
    refs = (fields_ref, kappa_ref, zlo_ref, zhi_ref)
    nfield, depth_len, rows, lanes = fields_ref.shape
    flat_fields = fields_ref.reshape(nfield * depth_len * rows, lanes)
    flat_kappa = kappa_ref.reshape(depth_len * rows, lanes)
    plan, used = y_plan(nfield, depth_len)
    for out_ref, top in ((lo_ref, True), (hi_ref, False)):
        for field, away, first, length, at in plan:
            row = away - 1 if top else rows - away
            for z in list(range(first, 0)) + list(range(depth_len, first + length)):
                out_ref[at + z - first, :] = source_plane(refs, field, z)[row, :]
            flat, base = (flat_kappa, 0) if field == nfield else (flat_fields, field * depth_len * rows)
            for z in range(0, depth_len, SUB):
                out_ref[pl.ds(at - first + z, SUB), :] = flat[
                    pl.ds(base + z * rows + row, SUB, stride=rows), :
                ]
        spare = plan[-1][3] + plan[-1][4]
        if used > spare:
            out_ref[spare:used, :] = jnp.zeros((used - spare, lanes), F32)


def assemble(refs, ylo_ref, yhi_ref, flags_ref, pad_ref):
    fields_ref, kappa_ref, zlo_ref, zhi_ref = refs
    nfield, depth_len, rows, lanes = fields_ref.shape
    planes, pitch = depth_len + 2 * W, rows + SUB
    halo = jnp.zeros((SUB, lanes), F32)

    @pl.loop(0, depth_len, unroll=steps(depth_len, 4))
    def _(z):
        for field in range(nfield + 1):
            plane = field * planes + W + z
            pad_ref[plane, :rows, :] = kappa_ref[z] if field == nfield else fields_ref[field, z]
            pad_ref[plane, rows:, :] = halo

    for field, at, wide in z_plan(nfield)[0]:
        for k in range(W):
            below, above = field * planes + W - 1 - k, field * planes + W + depth_len + k
            if k < wide:
                pad_ref[below, :rows, :] = zlo_ref[at + wide - 1 - k]
                pad_ref[above, :rows, :] = zhi_ref[at + k]
            for plane in (below, above):
                if k >= wide:
                    pad_ref[plane, :rows, :] = jnp.zeros((rows, lanes), F32)
                pad_ref[plane, rows:, :] = halo
    place_rows(pad_ref, depth_len, rows, ylo_ref, yhi_ref, flags_ref)


def place_rows(pad_ref, depth_len, first_row, ylo_ref, yhi_ref, flags_ref):
    planes = depth_len + 2 * W
    pitch, lanes = pad_ref.shape[1:]
    flat = pad_ref.reshape(pad_ref.shape[0] * pitch, lanes)
    low, high = flags_ref[2], flags_ref[3]
    for field, away, first, length, at in y_plan(pad_ref.shape[0] // planes - 1, depth_len)[0]:
        for ref, flag, row in ((ylo_ref, low, pitch - away), (yhi_ref, high, first_row + away - 1)):
            for start in tiles_of(0, length):
                flat[pl.ds((field * planes + W + first + start) * pitch + row, SUB, stride=pitch), :] = (
                    ref[pl.ds(at + start, SUB), :] * flag
                )


def take_columns(value, zi, lane, low, high):
    lanes = value.shape[-1]
    mine = (lane >= W * zi) & (lane < W * zi + W)
    low = jnp.where(mine, pltpu.roll(value, W * zi, 1), low)
    high = jnp.where(mine, pltpu.roll(value, (W * zi + W) % lanes, 1), high)
    return low, high


def pack_own_kernel(fields_ref, kappa_ref, zlo_ref, zhi_ref, lo_ref, hi_ref):
    refs = (fields_ref, kappa_ref, zlo_ref, zhi_ref)
    nfield, depth_len, rows, lanes = fields_ref.shape
    lane = lax.broadcasted_iota(jnp.int32, (1, lanes), 1)
    for field in range(nfield + 1):
        wide = reach(field, nfield)
        low = high = jnp.zeros((rows, lanes), F32)
        for z in range(-wide, depth_len + wide):
            low, high = take_columns(source_plane(refs, field, z)[...], z + W, lane, low, high)
        lo_ref[field] = low
        hi_ref[field] = high


def pack_columns_kernel(
    flags_ref, ylo_ref, yhi_ref, mainlo_ref, mainhi_ref, lo_ref, hi_ref, halo_ref
):
    nplane, _, lanes = halo_ref.shape
    nfield, rows = mainlo_ref.shape[0] - 1, mainlo_ref.shape[1]
    planes = nplane // (nfield + 1)
    lane = lax.broadcasted_iota(jnp.int32, (1, lanes), 1)
    zero = jnp.zeros((SUB, lanes), F32)
    for plane in range(nplane):
        halo_ref[plane] = zero
    place_rows(halo_ref, planes - 2 * W, 0, ylo_ref, yhi_ref, flags_ref)
    for field in range(nfield + 1):
        low = high = zero
        for zi in range(planes):
            low, high = take_columns(halo_ref[field * planes + zi], zi, lane, low, high)
        lo_ref[field, :rows, :] = mainlo_ref[field]
        hi_ref[field, :rows, :] = mainhi_ref[field]
        lo_ref[field, rows:, :] = low
        hi_ref[field, rows:, :] = high


def stencil(u, coefs, ups, downs, speeds):
    total = (coefs[3] - (speeds[0] + speeds[1] + speeds[2])) * u
    for axis in range(3):
        k_up, k_down = coefs[axis]
        total = total + k_up * ups[axis] + (k_down + speeds[axis]) * downs[axis]
    return total


def weights(k, ups, downs):
    half = 0.5 * k
    coefs = [(half + 0.5 * ups[a], half + 0.5 * downs[a]) for a in range(3)]
    rest = 1.0
    for up, down in coefs:
        rest = rest - (up + down)
    return coefs + [rest]


def side_neighbours(near, own, is_left, lanes, col):
    first, second = (near, own) if is_left else (own, near)
    first_up = jnp.where(col == W - 1, pltpu.roll(second, W - 1, 1), pltpu.roll(first, lanes - 1, 1))
    first_down = pltpu.roll(first, 1, 1)
    second_up = pltpu.roll(second, lanes - 1, 1)
    second_down = jnp.where(col == 0, pltpu.roll(first, lanes - (W - 1), 1), pltpu.roll(second, 1, 1))
    pair = ((first_up, first_down), (second_up, second_down))
    return pair if is_left else (pair[1], pair[0])


def main_kernel(
    flags_ref, courant_ref, center_ref, sharp_ref, gain_ref, color_ref, mask_ref, order_ref,
    fields_ref, kappa_ref, zlo_ref, zhi_ref, ylo_ref, yhi_ref, xlo_ref, xhi_ref, ownlo_ref, ownhi_ref,
    state_ref, out_ref,
    pad_ref, next_ref, last_ref, side_ref, edge_ref, base_ref, tile_ref, coef_ref, held_ref, sem,
):
    nfield, depth_len, rows, lanes = state_ref.shape
    planes, pitch = depth_len + 2 * W, rows + SUB
    lane = lax.broadcasted_iota(jnp.int32, (pitch, lanes), 1)
    r = lax.broadcasted_iota(jnp.int32, (pitch, lanes), 0)
    zi_of = lane // W
    col = lane - zi_of * W
    flag = [flags_ref[i] for i in range(6)]
    speed = [[courant_ref[f, a] for a in range(3)] for f in range(nfield)]
    row_mask = jnp.where(r < rows, 1.0, jnp.where(r < rows + SUB // 2, flag[3], flag[2]))

    def along_y(value):
        return pltpu.roll(value, pitch - 1, 0), pltpu.roll(value, 1, 0)

    sides = ((xlo_ref, ownlo_ref, True, flag[4]), (xhi_ref, ownhi_ref, False, flag[5]))

    def block_of(level, side, block, field):
        if level == 0 or field == nfield:
            return sides[side][block][field]
        return side_ref[level - 1, side, block, field]

    def edges(level, field):
        left, right = block_of(level, 0, 0, field), block_of(level, 1, 0, field)
        edge_ref[level, field] = jnp.where(col == W - 1, left, pltpu.roll(right, 1, 1))

    def side_step(level, count):
        zmask = row_mask * jnp.where(
            zi_of < W, flag[0], jnp.where(zi_of >= W + depth_len, flag[1], 1.0)
        )
        for side, (_, _, is_left, present) in enumerate(sides):
            blocks = (0, 1) if level == 0 else (0,)

            def around(lvl, field):
                pair = [block_of(lvl, side, block, field) for block in (0, 1)]
                x = side_neighbours(pair[0], pair[1], is_left, lanes, col)
                found = []
                for block in blocks:
                    value = pair[block]
                    y_up, y_down = along_y(value)
                    ups = (pltpu.roll(value, lanes - W, 1), y_up, x[block][0])
                    downs = (pltpu.roll(value, W, 1), y_down, x[block][1])
                    found.append((value, ups, downs))
                return found

            coefs = [weights(*found) for found in around(0, nfield)]
            for field in range(count):
                for block, (u, ups, downs) in zip(blocks, around(level, field)):
                    value = stencil(u, coefs[block], ups, downs, speed[field])
                    side_ref[level, side, block, field] = value * (zmask * present if block == 0 else zmask)

    def along_x(value, zi, edge):
        n = value.shape[0]
        turned = pltpu.roll(edge, lax.rem(2 * lanes - 2 - W * zi, lanes), 1)
        up = jnp.where(lane[:n] == lanes - 1, turned, pltpu.roll(value, lanes - 1, 1))
        down = jnp.where(lane[:n] == 0, turned, pltpu.roll(value, 1, 1))
        return up, down

    def around(src_ref, level, field, zi, n):
        plane = field * planes + zi
        whole = src_ref[plane]
        value = whole[:n]
        y_up, y_down = along_y(whole)
        x_up, x_down = along_x(value, zi, edge_ref[level, field, :n, :])
        return (
            value,
            (src_ref[plane + 1, :n, :], y_up[:n], x_up),
            (src_ref[plane - 1, :n, :], y_down[:n], x_down),
        )

    def step_value(src_ref, level, field, zi, n, coefs):
        u, ups, downs = around(src_ref, level, field, zi, n)
        return stencil(u, coefs, ups, downs, speed[field])

    def kept(zi, n):
        found = [coef_ref[i, zi, :n, :] for i in range(7)]
        return [found[0:2], found[2:4], found[4:6], found[6]]

    def depth_mask(zi):
        return jnp.where(zi < W, flag[0], jnp.where(zi >= W + depth_len, flag[1], 1.0))

    assemble((fields_ref, kappa_ref, zlo_ref, zhi_ref), ylo_ref, yhi_ref, flags_ref, pad_ref)
    for field in range(nfield + 1):
        edges(0, field)
    side_step(0, nfield)
    for field in range(nfield):
        edges(1, field)
    side_step(1, 1)
    edges(2, 0)

    @pl.loop(1, planes - 1, unroll=steps(planes - 2, 4))
    def _(zi):
        mask = row_mask * depth_mask(zi)
        coefs = weights(*around(pad_ref, 0, nfield, zi, pitch))
        for i, value in enumerate(sum(coefs[:3], ()) + (coefs[3],)):
            coef_ref[i, zi] = value
        for field in range(nfield):
            next_ref[field * planes + zi] = mask * step_value(pad_ref, 0, field, zi, pitch, coefs)

    @pl.loop(2, planes - 2, unroll=steps(planes - 4, 4))
    def _(zi):
        coefs = kept(zi, pitch)
        last_ref[zi] = step_value(next_ref, 1, 0, zi, pitch, coefs) * (row_mask * depth_mask(zi))

    @pl.loop(0, depth_len, unroll=steps(depth_len, 4))
    def _(z):
        zi = z + W
        coefs = kept(zi, rows)
        s, ups, downs = around(last_ref, 2, 0, zi, rows)
        held_ref[0, z] = s
        g_z, g_y, g_x = [0.5 * (ups[a] - downs[a]) for a in range(3)]
        shade = 0.35 + 0.65 * jnp.abs(0.64 * g_z + 0.6 * g_y + 0.48 * g_x) * lax.rsqrt(
            g_z * g_z + g_y * g_y + g_x * g_x + 1.0
        )
        for field in range(1, nfield):
            value = step_value(next_ref, 1, field, zi, rows, coefs)
            held_ref[field, z] = value
            if field <= 3:
                base_ref[field, z] = shade * (0.5 + 0.5 * jnp.tanh(0.5 * value))
            if field == 4:
                base_ref[0, z] = 1.0 + 0.5 * jnp.tanh(value)

    keep = pltpu.make_async_copy(held_ref, state_ref, sem)
    keep.start()
    ntf = center_ref.shape[0]
    chunk = 4 if ntf % 4 == 0 else 1
    halves = rows // SUB

    @pl.loop(0, (ntf // chunk) * halves)
    def _(step):
        first = (step // halves) * chunk
        row = pl.multiple_of((step % halves) * SUB, SUB)
        shape = (SUB, lanes)
        mid = [jnp.full(shape, center_ref[first + j], jnp.float32) for j in range(chunk)]
        bend = [jnp.full(shape, sharp_ref[first + j] * -LOG2E, jnp.float32) for j in range(chunk)]
        dense = [jnp.full(shape, gain_ref[first + j] * -LOG2E, jnp.float32) for j in range(chunk)]
        passed = [jnp.ones(shape, jnp.float32)] * chunk
        total = [jnp.zeros(shape, jnp.float32)] * chunk
        acc = [[jnp.zeros(shape, jnp.float32)] * 3 for _ in range(chunk)]
        for z in range(depth_len):
            s = held_ref[0, z, pl.ds(row, SUB), :]
            modul = base_ref[0, z, pl.ds(row, SUB), :]
            base = [base_ref[k + 1, z, pl.ds(row, SUB), :] for k in range(3)]
            for j in range(chunk):
                diff = s - mid[j]
                total[j] = total[j] + modul * jnp.exp2(diff * diff * bend[j])
                after = jnp.exp2(total[j] * dense[j])
                weight = passed[j] - after
                passed[j] = after
                acc[j] = [acc[j][k] + weight * base[k] for k in range(3)]
        for j in range(chunk):
            start = ((first + j) * rows + row) * 4
            for k in range(3):
                tile_ref[pl.ds(start + k, SUB, stride=4), :] = acc[j][k] * color_ref[k, first + j]
            tile_ref[pl.ds(start + 3, SUB, stride=4), :] = 1.0 - passed[j]

    @pl.loop(0, order_ref.shape[0], unroll=8)
    def _(slot):
        tile = order_ref[slot]
        cover = mask_ref[tile].astype(jnp.float32)
        out_ref[slot] = tile_ref[pl.ds(pl.multiple_of(tile * 4, 4), 4), :] * cover
    keep.wait()


def compose_kernel(part_ref, out_ref):
    slabs, rows, _ = part_ref.shape

    @pl.loop(0, rows // 32, unroll=rows // 32)
    def _(step):
        def load(slab, k):
            return part_ref[slab, pl.ds(step * 32 + k, 8, stride=4), :]

        acc = [load(0, k) for k in range(4)]
        for slab in range(1, slabs):
            clear = 1.0 - acc[3]
            acc = [acc[k] + clear * load(slab, k) for k in range(4)]
        for k in range(4):
            out_ref[pl.ds(step * 32 + k, 8, stride=4), :] = acc[k]


def compose(parts):
    vmem = pl.BlockSpec(memory_space=pltpu.VMEM)
    return pl.pallas_call(
        compose_kernel,
        out_shape=jax.ShapeDtypeStruct(parts.shape[1:], jnp.float32),
        in_specs=[vmem],
        out_specs=vmem,
        compiler_params=pltpu.CompilerParams(vmem_limit_bytes=16 * 1024 * 1024),
        name="compose",
    )(parts)


def shift(message, axis, up):
    count = lax.axis_size(axis)
    pairs = [(i, i + 1) if up else (i + 1, i) for i in range(count - 1)]
    return lax.ppermute(message, axis, pairs)


def present(axis):
    here = lax.axis_index(axis)
    return [(here > 0).astype(F32), (here < lax.axis_size(axis) - 1).astype(F32)]


def shards(
    fields, diffusivity, courant, tf_center, tf_sharp, tf_gain, tf_color, tile_mask, tile_perm
):
    nfield, depth_len, rows_len, cols_len = fields.shape
    planes, pitch = depth_len + 2 * W, rows_len + SUB
    smem = pl.BlockSpec(memory_space=pltpu.SMEM)
    vmem = pl.BlockSpec(memory_space=pltpu.VMEM)
    params = pltpu.CompilerParams(vmem_limit_bytes=16 * 1024 * 1024)

    def array(*shape):
        return jax.ShapeDtypeStruct(shape, F32)

    flags = jnp.stack(present("gz") + present("gy") + present("gx"))

    faces = z_plan(nfield)[1]
    face_lo, face_hi = pl.pallas_call(
        pack_planes_kernel,
        out_shape=(array(faces, rows_len, cols_len),) * 2,
        in_specs=[pl.BlockSpec(memory_space=pl.ANY)] * 2,
        out_specs=(vmem, vmem),
        scratch_shapes=[pltpu.SemaphoreType.DMA((2 * nfield + 2,))],
        compiler_params=pltpu.CompilerParams(vmem_limit_bytes=60 * 1024 * 1024),
        name="pack_planes",
    )(fields, diffusivity)
    zlo = shift(face_hi, "gz", True)
    zhi = shift(face_lo, "gz", False)
    used = y_plan(nfield, depth_len)[1]
    send_lo, send_hi = pl.pallas_call(
        pack_rows_kernel,
        out_shape=(array(used, cols_len), array(used, cols_len)),
        in_specs=[vmem] * 4,
        out_specs=(vmem, vmem),
        compiler_params=params,
        name="pack_rows",
    )(fields, diffusivity, zlo, zhi)
    main_lo, main_hi = pl.pallas_call(
        pack_own_kernel,
        out_shape=(array(nfield + 1, rows_len, cols_len),) * 2,
        in_specs=[vmem] * 4,
        out_specs=(vmem,) * 2,
        compiler_params=params,
        cost_estimate=pl.CostEstimate(flops=10**7, bytes_accessed=4 * 10**6, transcendentals=0),
        name="pack_own",
    )(fields, diffusivity, zlo, zhi)
    if lax.axis_size("gy") == 2:
        mine = jnp.where(lax.axis_index("gy") == 0, send_hi, send_lo)
        ylo = yhi = lax.ppermute(mine, "gy", [(0, 1), (1, 0)])
    else:
        ylo = shift(send_hi, "gy", True)
        yhi = shift(send_lo, "gy", False)
    pad = pltpu.VMEM(((nfield + 1) * planes, pitch, cols_len), F32)
    own_lo, own_hi = pl.pallas_call(
        pack_columns_kernel,
        out_shape=(array(nfield + 1, pitch, cols_len),) * 2,
        in_specs=[smem] + [vmem] * 4,
        out_specs=(vmem,) * 2,
        scratch_shapes=[pltpu.VMEM(((nfield + 1) * planes, SUB, cols_len), F32)],
        compiler_params=params,
        name="pack_columns",
    )(flags, ylo, yhi, main_lo, main_hi)
    xlo = shift(own_hi, "gx", True)
    xhi = shift(own_lo, "gx", False)
    count = lax.axis_size("gz")
    order = tile_perm[0, 0]
    per_owner = order.shape[0] // count
    state, tiles = pl.pallas_call(
        main_kernel,
        out_shape=(array(*fields.shape), array(order.shape[0], 4, cols_len)),
        in_specs=[smem] * 8 + [vmem] * 10,
        out_specs=(pl.BlockSpec(memory_space=pl.ANY), vmem),
        scratch_shapes=[
            pad,
            pltpu.VMEM((nfield * planes, pitch, cols_len), F32),
            pltpu.VMEM((planes, pitch, cols_len), F32),
            pltpu.VMEM((2, 2, 2, nfield, pitch, cols_len), F32),
            pltpu.VMEM((3, nfield + 1, pitch, cols_len), F32),
            pltpu.VMEM((4, depth_len, rows_len, cols_len), F32),
            pltpu.VMEM((order.shape[0] * 4, cols_len), F32),
            pltpu.VMEM((7, planes, pitch, cols_len), F32),
            pltpu.VMEM(fields.shape, F32),
            pltpu.SemaphoreType.DMA(()),
        ],
        compiler_params=pltpu.CompilerParams(vmem_limit_bytes=24 * 1024 * 1024),
        name="step_and_march",
    )(
        flags, courant, tf_center, tf_sharp, tf_gain, tf_color, tile_mask[0].reshape(-1), order,
        fields, diffusivity, zlo, zhi, ylo, yhi, xlo, xhi, own_lo, own_hi,
    )
    grouped = tiles.reshape(count, per_owner * 4, cols_len)
    composed = compose(lax.all_to_all(grouped, "gz", split_axis=0, concat_axis=0, tiled=True))
    picture = composed.reshape(1, 1, per_owner, 4, cols_len)
    return (state, picture)


def solution(mesh):
    return jax.shard_map(
        shards,
        mesh=mesh,
        in_specs=(
            P(None, "gz", "gy", "gx"),
            P("gz", "gy", "gx"),
            P(),
            P(),
            P(),
            P(),
            P(),
            P("gz", None, "gy", "gx"),
            P("gy", "gx", None),
        ),
        out_specs=(P(None, "gz", "gy", "gx"), P("gy", "gx", "gz", None, None)),
        check_vma=False,
    )
```

```python
import jax
import jax.numpy as jnp
from jax import lax
from jax.experimental import pallas as pl
from jax.experimental.pallas import tpu as pltpu
from jax.sharding import PartitionSpec as P

LOG2E = 1.4426950408889634
W = 3
SUB = 8
F32 = jnp.float32


def reach(field, nfield):
    return W if field in (0, nfield) else W - 1


def tiles_of(first, last):
    return [min(start, last - SUB) for start in range(first, last, SUB)]


def z_plan(nfield):
    plan, at = [], 0
    for field in range(nfield + 1):
        plan.append((field, at, reach(field, nfield)))
        at += reach(field, nfield)
    return plan, at


def y_plan(nfield):
    kinds, edges = [], []
    for field in range(nfield + 1):
        wide = reach(field, nfield)
        for away in range(1, wide + 1):
            kinds.append((field, away))
            for k in range(1, wide - away + 1):
                edges.append((field, away, -k))
                edges.append((field, away, k))
    return kinds, edges


def pack_planes_kernel(fields_ref, kappa_ref, first_ref, second_ref, sems):
    nfield, depth_len = fields_ref.shape[:2]
    odd = lax.rem(lax.axis_index("gz"), 2)
    copies = []
    for field, at, wide in z_plan(nfield)[0]:
        source = kappa_ref if field == nfield else fields_ref.at[field]
        for place, target in ((1 - odd, first_ref), (odd, second_ref)):
            copies.append(
                pltpu.make_async_copy(
                    source.at[pl.ds(place * (depth_len - wide), wide)], target.at[pl.ds(at, wide)], sems.at[len(copies)]
                )
            )
    for copy in copies:
        copy.start()
    for copy in copies:
        copy.wait()


def steps(count, most):
    return max(k for k in range(1, most + 1) if count % k == 0)


def source_plane(refs, field, z):
    fields_ref, kappa_ref, zlo_ref, zhi_ref = refs
    nfield, depth_len = fields_ref.shape[:2]
    _, at, wide = z_plan(nfield)[0][field]
    if z < 0:
        return zlo_ref.at[at + wide + z]
    if z >= depth_len:
        return zhi_ref.at[at + z - depth_len]
    return kappa_ref.at[z] if field == nfield else fields_ref.at[field, z]


def pack_rows_kernel(fields_ref, kappa_ref, lo_ref, hi_ref):
    nfield, depth_len, rows, lanes = fields_ref.shape
    flat_fields = fields_ref.reshape(nfield * depth_len * rows, lanes)
    flat_kappa = kappa_ref.reshape(depth_len * rows, lanes)
    for out_ref, top in ((lo_ref, True), (hi_ref, False)):
        for i, (field, away) in enumerate(y_plan(nfield)[0]):
            row = away - 1 if top else rows - away
            flat, base = (flat_kappa, 0) if field == nfield else (flat_fields, field * depth_len * rows)
            for z in range(0, depth_len, SUB):
                out_ref[i, z : z + SUB, :] = flat[pl.ds(base + z * rows + row, SUB, stride=rows), :]


def pack_edges_kernel(fields_ref, kappa_ref, zlo_ref, zhi_ref, lo_ref, hi_ref):
    refs = (fields_ref, kappa_ref, zlo_ref, zhi_ref)
    nfield, depth_len, rows, _ = fields_ref.shape
    for i, (field, away, k) in enumerate(y_plan(nfield)[1]):
        plane = source_plane(refs, field, k if k < 0 else depth_len - 1 + k)
        lo_ref[i : i + 1, :] = plane[away - 1 : away, :]
        hi_ref[i : i + 1, :] = plane[rows - away : rows - away + 1, :]


def assemble(refs, halo_rows, flags_ref, pad_ref):
    fields_ref, kappa_ref, zlo_ref, zhi_ref = refs
    nfield, depth_len, rows, lanes = fields_ref.shape
    planes, pitch = depth_len + 2 * W, rows + SUB
    halo = jnp.zeros((SUB, lanes), F32)

    @pl.loop(0, depth_len, unroll=steps(depth_len, 4))
    def _(z):
        for field in range(nfield + 1):
            plane = field * planes + W + z
            pad_ref[plane, :rows, :] = kappa_ref[z] if field == nfield else fields_ref[field, z]
            pad_ref[plane, rows:, :] = halo

    for field, at, wide in z_plan(nfield)[0]:
        for k in range(W):
            below, above = field * planes + W - 1 - k, field * planes + W + depth_len + k
            if k < wide:
                pad_ref[below, :rows, :] = zlo_ref[at + wide - 1 - k]
                pad_ref[above, :rows, :] = zhi_ref[at + k]
            for plane in (below, above):
                if k >= wide:
                    pad_ref[plane, :rows, :] = jnp.zeros((rows, lanes), F32)
                pad_ref[plane, rows:, :] = halo
    place_rows(pad_ref, depth_len, rows, halo_rows, flags_ref)


def place_rows(pad_ref, depth_len, first_row, halo_rows, flags_ref):
    planes = depth_len + 2 * W
    pitch, lanes = pad_ref.shape[1:]
    flat = pad_ref.reshape(pad_ref.shape[0] * pitch, lanes)
    kinds, edges = y_plan(pad_ref.shape[0] // planes - 1)
    for low, (ref, edge_ref) in ((True, halo_rows[:2]), (False, halo_rows[2:])):
        flag = flags_ref[2] if low else flags_ref[3]
        for i, (field, away) in enumerate(kinds):
            row = pitch - away if low else first_row + away - 1
            for z in range(0, depth_len, SUB):
                flat[pl.ds((field * planes + W + z) * pitch + row, SUB, stride=pitch), :] = (
                    ref[i, z : z + SUB, :] * flag
                )
        for i, (field, away, k) in enumerate(edges):
            row = pitch - away if low else first_row + away - 1
            plane = field * planes + W + (k if k < 0 else depth_len - 1 + k)
            pad_ref[plane, row : row + 1, :] = edge_ref[i : i + 1, :] * flag


def take_columns(value, zi, lane, low, high):
    lanes = value.shape[-1]
    mine = (lane >= W * zi) & (lane < W * zi + W)
    low = jnp.where(mine, pltpu.roll(value, W * zi, 1), low)
    high = jnp.where(mine, pltpu.roll(value, (W * zi + W) % lanes, 1), high)
    return low, high


def pack_own_kernel(fields_ref, kappa_ref, zlo_ref, zhi_ref, lo_ref, hi_ref):
    refs = (fields_ref, kappa_ref, zlo_ref, zhi_ref)
    nfield, depth_len, rows, lanes = fields_ref.shape
    lane = lax.broadcasted_iota(jnp.int32, (1, lanes), 1)
    for field in range(nfield + 1):
        wide = reach(field, nfield)
        low = high = jnp.zeros((rows, lanes), F32)
        for z in range(-wide, depth_len + wide):
            low, high = take_columns(source_plane(refs, field, z)[...], z + W, lane, low, high)
        lo_ref[field] = low
        hi_ref[field] = high


def pack_columns_kernel(
    flags_ref, ylo_ref, elo_ref, yhi_ref, ehi_ref, mainlo_ref, mainhi_ref, lo_ref, hi_ref, halo_ref
):
    nplane, _, lanes = halo_ref.shape
    nfield, rows = mainlo_ref.shape[0] - 1, mainlo_ref.shape[1]
    planes = nplane // (nfield + 1)
    lane = lax.broadcasted_iota(jnp.int32, (1, lanes), 1)
    zero = jnp.zeros((SUB, lanes), F32)
    for plane in range(nplane):
        halo_ref[plane] = zero
    place_rows(halo_ref, planes - 2 * W, 0, (ylo_ref, elo_ref, yhi_ref, ehi_ref), flags_ref)
    for field in range(nfield + 1):
        low = high = zero
        for zi in range(planes):
            low, high = take_columns(halo_ref[field * planes + zi], zi, lane, low, high)
        lo_ref[field, :rows, :] = mainlo_ref[field]
        hi_ref[field, :rows, :] = mainhi_ref[field]
        lo_ref[field, rows:, :] = low
        hi_ref[field, rows:, :] = high


def stencil(u, coefs, ups, downs, speeds):
    total = (coefs[3] - (speeds[0] + speeds[1] + speeds[2])) * u
    for axis in range(3):
        k_up, k_down = coefs[axis]
        total = total + k_up * ups[axis] + (k_down + speeds[axis]) * downs[axis]
    return total


def weights(k, ups, downs):
    half = 0.5 * k
    coefs = [(half + 0.5 * ups[a], half + 0.5 * downs[a]) for a in range(3)]
    rest = 1.0
    for up, down in coefs:
        rest = rest - (up + down)
    return coefs + [rest]


def side_neighbours(near, own, is_left, lanes, col):
    first, second = (near, own) if is_left else (own, near)
    first_up = jnp.where(col == W - 1, pltpu.roll(second, W - 1, 1), pltpu.roll(first, lanes - 1, 1))
    first_down = pltpu.roll(first, 1, 1)
    second_up = pltpu.roll(second, lanes - 1, 1)
    second_down = jnp.where(col == 0, pltpu.roll(first, lanes - (W - 1), 1), pltpu.roll(second, 1, 1))
    pair = ((first_up, first_down), (second_up, second_down))
    return pair if is_left else (pair[1], pair[0])


def main_kernel(
    flags_ref, courant_ref, center_ref, sharp_ref, gain_ref, color_ref, mask_ref, order_ref,
    fields_ref, kappa_ref, zlo_ref, zhi_ref,
    ylo_ref, elo_ref, yhi_ref, ehi_ref, xlo_ref, xhi_ref, ownlo_ref, ownhi_ref,
    state_ref, out_ref,
    pad_ref, next_ref, last_ref, side_ref, edge_ref, base_ref, tile_ref, coef_ref, held_ref, sem,
):
    nfield, depth_len, rows, lanes = state_ref.shape
    planes, pitch = depth_len + 2 * W, rows + SUB
    lane = lax.broadcasted_iota(jnp.int32, (pitch, lanes), 1)
    r = lax.broadcasted_iota(jnp.int32, (pitch, lanes), 0)
    zi_of = lane // W
    col = lane - zi_of * W
    flag = [flags_ref[i] for i in range(6)]
    speed = [[courant_ref[f, a] for a in range(3)] for f in range(nfield)]
    row_mask = jnp.where(r < rows, 1.0, jnp.where(r < rows + SUB // 2, flag[3], flag[2]))

    def along_y(value):
        return pltpu.roll(value, pitch - 1, 0), pltpu.roll(value, 1, 0)

    sides = ((xlo_ref, ownlo_ref, True, flag[4]), (xhi_ref, ownhi_ref, False, flag[5]))

    def block_of(level, side, block, field):
        if level == 0 or field == nfield:
            return sides[side][block][field]
        return side_ref[level - 1, side, block, field]

    def edges(level, field):
        left, right = block_of(level, 0, 0, field), block_of(level, 1, 0, field)
        edge_ref[level, field] = jnp.where(col == W - 1, left, pltpu.roll(right, 1, 1))

    def side_step(level, count):
        zmask = row_mask * jnp.where(
            zi_of < W, flag[0], jnp.where(zi_of >= W + depth_len, flag[1], 1.0)
        )
        for side, (_, _, is_left, present) in enumerate(sides):
            blocks = (0, 1) if level == 0 else (0,)

            def around(lvl, field):
                pair = [block_of(lvl, side, block, field) for block in (0, 1)]
                x = side_neighbours(pair[0], pair[1], is_left, lanes, col)
                found = []
                for block in blocks:
                    value = pair[block]
                    y_up, y_down = along_y(value)
                    ups = (pltpu.roll(value, lanes - W, 1), y_up, x[block][0])
                    downs = (pltpu.roll(value, W, 1), y_down, x[block][1])
                    found.append((value, ups, downs))
                return found

            coefs = [weights(*found) for found in around(0, nfield)]
            for field in range(count):
                for block, (u, ups, downs) in zip(blocks, around(level, field)):
                    value = stencil(u, coefs[block], ups, downs, speed[field])
                    side_ref[level, side, block, field] = value * (zmask * present if block == 0 else zmask)

    def along_x(value, zi, edge):
        n = value.shape[0]
        turned = pltpu.roll(edge, lax.rem(2 * lanes - 2 - W * zi, lanes), 1)
        up = jnp.where(lane[:n] == lanes - 1, turned, pltpu.roll(value, lanes - 1, 1))
        down = jnp.where(lane[:n] == 0, turned, pltpu.roll(value, 1, 1))
        return up, down

    def around(src_ref, level, field, zi, n):
        plane = field * planes + zi
        whole = src_ref[plane]
        value = whole[:n]
        y_up, y_down = along_y(whole)
        x_up, x_down = along_x(value, zi, edge_ref[level, field, :n, :])
        return (
            value,
            (src_ref[plane + 1, :n, :], y_up[:n], x_up),
            (src_ref[plane - 1, :n, :], y_down[:n], x_down),
        )

    def step_value(src_ref, level, field, zi, n, coefs):
        u, ups, downs = around(src_ref, level, field, zi, n)
        return stencil(u, coefs, ups, downs, speed[field])

    def kept(zi, n):
        found = [coef_ref[i, zi, :n, :] for i in range(7)]
        return [found[0:2], found[2:4], found[4:6], found[6]]

    def depth_mask(zi):
        return jnp.where(zi < W, flag[0], jnp.where(zi >= W + depth_len, flag[1], 1.0))

    halo_rows = (ylo_ref, elo_ref, yhi_ref, ehi_ref)
    assemble((fields_ref, kappa_ref, zlo_ref, zhi_ref), halo_rows, flags_ref, pad_ref)
    for field in range(nfield + 1):
        edges(0, field)
    side_step(0, nfield)
    for field in range(nfield):
        edges(1, field)
    side_step(1, 1)
    edges(2, 0)

    @pl.loop(1, planes - 1, unroll=steps(planes - 2, 4))
    def _(zi):
        mask = row_mask * depth_mask(zi)
        coefs = weights(*around(pad_ref, 0, nfield, zi, pitch))
        for i, value in enumerate(sum(coefs[:3], ()) + (coefs[3],)):
            coef_ref[i, zi] = value
        for field in range(nfield):
            next_ref[field * planes + zi] = mask * step_value(pad_ref, 0, field, zi, pitch, coefs)

    @pl.loop(2, planes - 2, unroll=steps(planes - 4, 4))
    def _(zi):
        coefs = kept(zi, pitch)
        last_ref[zi] = step_value(next_ref, 1, 0, zi, pitch, coefs) * (row_mask * depth_mask(zi))

    @pl.loop(0, depth_len, unroll=steps(depth_len, 4))
    def _(z):
        zi = z + W
        coefs = kept(zi, rows)
        s, ups, downs = around(last_ref, 2, 0, zi, rows)
        held_ref[0, z] = s
        g_z, g_y, g_x = [0.5 * (ups[a] - downs[a]) for a in range(3)]
        shade = 0.35 + 0.65 * jnp.abs(0.64 * g_z + 0.6 * g_y + 0.48 * g_x) * lax.rsqrt(
            g_z * g_z + g_y * g_y + g_x * g_x + 1.0
        )
        for field in range(1, nfield):
            value = step_value(next_ref, 1, field, zi, rows, coefs)
            held_ref[field, z] = value
            if field <= 3:
                base_ref[field, z] = shade * (0.5 + 0.5 * jnp.tanh(0.5 * value))
            if field == 4:
                base_ref[0, z] = 1.0 + 0.5 * jnp.tanh(value)

    keep = pltpu.make_async_copy(held_ref, state_ref, sem)
    keep.start()
    ntf = center_ref.shape[0]
    chunk = 4 if ntf % 4 == 0 else 1
    halves = rows // SUB

    @pl.loop(0, (ntf // chunk) * halves)
    def _(step):
        first = (step // halves) * chunk
        row = pl.multiple_of((step % halves) * SUB, SUB)
        shape = (SUB, lanes)
        mid = [jnp.full(shape, center_ref[first + j], jnp.float32) for j in range(chunk)]
        bend = [jnp.full(shape, sharp_ref[first + j] * -LOG2E, jnp.float32) for j in range(chunk)]
        dense = [jnp.full(shape, gain_ref[first + j] * -LOG2E, jnp.float32) for j in range(chunk)]
        passed = [jnp.ones(shape, jnp.float32)] * chunk
        total = [jnp.zeros(shape, jnp.float32)] * chunk
        acc = [[jnp.zeros(shape, jnp.float32)] * 3 for _ in range(chunk)]
        for z in range(depth_len):
            s = held_ref[0, z, pl.ds(row, SUB), :]
            modul = base_ref[0, z, pl.ds(row, SUB), :]
            base = [base_ref[k + 1, z, pl.ds(row, SUB), :] for k in range(3)]
            for j in range(chunk):
                diff = s - mid[j]
                total[j] = total[j] + modul * jnp.exp2(diff * diff * bend[j])
                after = jnp.exp2(total[j] * dense[j])
                weight = passed[j] - after
                passed[j] = after
                acc[j] = [acc[j][k] + weight * base[k] for k in range(3)]
        for j in range(chunk):
            start = ((first + j) * rows + row) * 4
            for k in range(3):
                tile_ref[pl.ds(start + k, SUB, stride=4), :] = acc[j][k] * color_ref[k, first + j]
            tile_ref[pl.ds(start + 3, SUB, stride=4), :] = 1.0 - passed[j]

    @pl.loop(0, order_ref.shape[0], unroll=steps(order_ref.shape[0], 64))
    def _(slot):
        tile = order_ref[slot]
        cover = mask_ref[tile].astype(jnp.float32)
        out_ref[slot] = tile_ref[pl.ds(pl.multiple_of(tile * 4, 4), 4), :] * cover
    keep.wait()


def compose_kernel(part_ref, out_ref):
    slabs, rows, _ = part_ref.shape

    @pl.loop(0, rows // 32, unroll=rows // 32)
    def _(step):
        def load(slab, k):
            return part_ref[slab, pl.ds(step * 32 + k, 8, stride=4), :]

        acc = [load(0, k) for k in range(4)]
        for slab in range(1, slabs):
            clear = 1.0 - acc[3]
            acc = [acc[k] + clear * load(slab, k) for k in range(4)]
        for k in range(4):
            out_ref[pl.ds(step * 32 + k, 8, stride=4), :] = acc[k]


def compose(parts):
    vmem = pl.BlockSpec(memory_space=pltpu.VMEM)
    return pl.pallas_call(
        compose_kernel,
        out_shape=jax.ShapeDtypeStruct(parts.shape[1:], jnp.float32),
        in_specs=[vmem],
        out_specs=vmem,
        compiler_params=pltpu.CompilerParams(vmem_limit_bytes=16 * 1024 * 1024),
        name="compose",
    )(parts)


def is_odd(axis):
    return lax.rem(lax.axis_index(axis), 2) == 1


def swap_pairs(first, second, axis):
    count = lax.axis_size(axis)
    came = []
    for start, message in ((0, first), (1, second)):
        pairs = []
        for i in range(start, count - 1, 2):
            pairs += [(i, i + 1), (i + 1, i)]
        came.append(lax.ppermute(message, axis, pairs) if pairs else jnp.zeros_like(message))
    odd = is_odd(axis)
    return jnp.where(odd, came[0], came[1]), jnp.where(odd, came[1], came[0])


def swap_rows(low, high, axis):
    odd = is_odd(axis)
    first = jnp.where(odd, low, high)
    if lax.axis_size(axis) == 2:
        came = lax.ppermute(first, axis, [(0, 1), (1, 0)])
        return came, came
    return swap_pairs(first, jnp.where(odd, high, low), axis)


def present(axis):
    here = lax.axis_index(axis)
    return [(here > 0).astype(F32), (here < lax.axis_size(axis) - 1).astype(F32)]


def shards(
    fields, diffusivity, courant, tf_center, tf_sharp, tf_gain, tf_color, tile_mask, tile_perm
):
    nfield, depth_len, rows_len, cols_len = fields.shape
    planes, pitch = depth_len + 2 * W, rows_len + SUB
    smem = pl.BlockSpec(memory_space=pltpu.SMEM)
    vmem = pl.BlockSpec(memory_space=pltpu.VMEM)
    params = pltpu.CompilerParams(vmem_limit_bytes=16 * 1024 * 1024)

    def array(*shape):
        return jax.ShapeDtypeStruct(shape, F32)

    flags = jnp.stack(present("gz") + present("gy") + present("gx"))

    faces = z_plan(nfield)[1]
    first, second = pl.pallas_call(
        pack_planes_kernel,
        out_shape=(array(faces, rows_len, cols_len),) * 2,
        in_specs=[pl.BlockSpec(memory_space=pl.ANY)] * 2,
        out_specs=(vmem, vmem),
        scratch_shapes=[pltpu.SemaphoreType.DMA((2 * nfield + 2,))],
        compiler_params=pltpu.CompilerParams(vmem_limit_bytes=60 * 1024 * 1024),
        name="pack_planes",
    )(fields, diffusivity)
    zlo, zhi = swap_pairs(first, second, "gz")
    kinds, outer = y_plan(nfield)
    send_lo, send_hi = pl.pallas_call(
        pack_rows_kernel,
        out_shape=(array(len(kinds), depth_len, cols_len),) * 2,
        in_specs=[vmem] * 2,
        out_specs=(vmem, vmem),
        compiler_params=params,
        name="pack_rows",
    )(fields, diffusivity)
    ylo, yhi = swap_rows(send_lo, send_hi, "gy")
    send_lo, send_hi = pl.pallas_call(
        pack_edges_kernel,
        out_shape=(array(len(outer), cols_len),) * 2,
        in_specs=[vmem] * 4,
        out_specs=(vmem, vmem),
        compiler_params=params,
        name="pack_edges",
    )(fields, diffusivity, zlo, zhi)
    elo, ehi = swap_rows(send_lo, send_hi, "gy")
    main_lo, main_hi = pl.pallas_call(
        pack_own_kernel,
        out_shape=(array(nfield + 1, rows_len, cols_len),) * 2,
        in_specs=[vmem] * 4,
        out_specs=(vmem,) * 2,
        compiler_params=params,
        cost_estimate=pl.CostEstimate(flops=10**7, bytes_accessed=4 * 10**6, transcendentals=0),
        name="pack_own",
    )(fields, diffusivity, zlo, zhi)
    pad = pltpu.VMEM(((nfield + 1) * planes, pitch, cols_len), F32)
    own_lo, own_hi = pl.pallas_call(
        pack_columns_kernel,
        out_shape=(array(nfield + 1, pitch, cols_len),) * 2,
        in_specs=[smem] + [vmem] * 6,
        out_specs=(vmem,) * 2,
        scratch_shapes=[pltpu.VMEM(((nfield + 1) * planes, SUB, cols_len), F32)],
        compiler_params=params,
        name="pack_columns",
    )(flags, ylo, elo, yhi, ehi, main_lo, main_hi)
    odd = is_odd("gx")
    xlo, xhi = swap_pairs(jnp.where(odd, own_lo, own_hi), jnp.where(odd, own_hi, own_lo), "gx")
    count = lax.axis_size("gz")
    order = tile_perm[0, 0]
    per_owner = order.shape[0] // count
    state, tiles = pl.pallas_call(
        main_kernel,
        out_shape=(array(*fields.shape), array(order.shape[0], 4, cols_len)),
        in_specs=[smem] * 8 + [vmem] * 12,
        out_specs=(pl.BlockSpec(memory_space=pl.ANY), vmem),
        scratch_shapes=[
            pad,
            pltpu.VMEM((nfield * planes, pitch, cols_len), F32),
            pltpu.VMEM((planes, pitch, cols_len), F32),
            pltpu.VMEM((2, 2, 2, nfield, pitch, cols_len), F32),
            pltpu.VMEM((3, nfield + 1, pitch, cols_len), F32),
            pltpu.VMEM((4, depth_len, rows_len, cols_len), F32),
            pltpu.VMEM((order.shape[0] * 4, cols_len), F32),
            pltpu.VMEM((7, planes, pitch, cols_len), F32),
            pltpu.VMEM(fields.shape, F32),
            pltpu.SemaphoreType.DMA(()),
        ],
        compiler_params=pltpu.CompilerParams(vmem_limit_bytes=24 * 1024 * 1024),
        name="step_and_march",
    )(
        flags, courant, tf_center, tf_sharp, tf_gain, tf_color, tile_mask[0].reshape(-1), order,
        fields, diffusivity, zlo, zhi, ylo, elo, yhi, ehi, xlo, xhi, own_lo, own_hi,
    )
    grouped = tiles.reshape(count, per_owner * 4, cols_len)
    composed = compose(lax.all_to_all(grouped, "gz", split_axis=0, concat_axis=0, tiled=True))
    picture = composed.reshape(1, 1, per_owner, 4, cols_len)
    return (state, picture)


def solution(mesh):
    return jax.shard_map(
        shards,
        mesh=mesh,
        in_specs=(
            P(None, "gz", "gy", "gx"),
            P("gz", "gy", "gx"),
            P(),
            P(),
            P(),
            P(),
            P(),
            P("gz", None, "gy", "gx"),
            P("gy", "gx", None),
        ),
        out_specs=(P(None, "gz", "gy", "gx"), P("gy", "gx", "gz", None, None)),
        check_vma=False,
    )
```

```python
import jax
import jax.numpy as jnp
from jax import lax
from jax.experimental import pallas as pl
from jax.experimental.pallas import tpu as pltpu
from jax.sharding import PartitionSpec as P

LOG2E = 1.4426950408889634
W = 3
SUB = 8
F32 = jnp.float32


def reach(field, nfield):
    return W if field in (0, nfield) else W - 1


def tiles_of(first, last):
    return [min(start, last - SUB) for start in range(first, last, SUB)]


def z_plan(nfield):
    plan, at = [], 0
    for field in range(nfield + 1):
        plan.append((field, at, reach(field, nfield)))
        at += reach(field, nfield)
    return plan, at


def y_plan(nfield):
    kinds, edges = [], []
    for field in range(nfield + 1):
        wide = reach(field, nfield)
        for away in range(1, wide + 1):
            kinds.append((field, away))
            for k in range(1, wide - away + 1):
                edges.append((field, away, -k))
                edges.append((field, away, k))
    return kinds, edges


def pack_planes_kernel(fields_ref, kappa_ref, first_ref, second_ref, sems):
    nfield, depth_len = fields_ref.shape[:2]
    odd = lax.rem(lax.axis_index("gz"), 2)
    copies = []
    for field, at, wide in z_plan(nfield)[0]:
        source = kappa_ref if field == nfield else fields_ref.at[field]
        for place, target in ((1 - odd, first_ref), (odd, second_ref)):
            copies.append(
                pltpu.make_async_copy(
                    source.at[pl.ds(place * (depth_len - wide), wide)], target.at[pl.ds(at, wide)], sems.at[len(copies)]
                )
            )
    for copy in copies:
        copy.start()
    for copy in copies:
        copy.wait()


def steps(count, most):
    return max(k for k in range(1, most + 1) if count % k == 0)


def source_plane(refs, field, z):
    fields_ref, kappa_ref, zlo_ref, zhi_ref = refs
    nfield, depth_len = fields_ref.shape[:2]
    _, at, wide = z_plan(nfield)[0][field]
    if z < 0:
        return zlo_ref.at[at + wide + z]
    if z >= depth_len:
        return zhi_ref.at[at + z - depth_len]
    return kappa_ref.at[z] if field == nfield else fields_ref.at[field, z]


def pack_rows_kernel(fields_ref, kappa_ref, lo_ref, hi_ref):
    nfield, depth_len, rows, lanes = fields_ref.shape
    flat_fields = fields_ref.reshape(nfield * depth_len * rows, lanes)
    flat_kappa = kappa_ref.reshape(depth_len * rows, lanes)
    for out_ref, top in ((lo_ref, True), (hi_ref, False)):
        for i, (field, away) in enumerate(y_plan(nfield)[0]):
            row = away - 1 if top else rows - away
            flat, base = (flat_kappa, 0) if field == nfield else (flat_fields, field * depth_len * rows)
            for z in range(0, depth_len, SUB):
                out_ref[i, z : z + SUB, :] = flat[pl.ds(base + z * rows + row, SUB, stride=rows), :]


def pack_edges_kernel(
    fields_ref, kappa_ref, zlo_ref, zhi_ref, ownlo_ref, ownhi_ref, lo_ref, hi_ref, mainlo_ref, mainhi_ref
):
    refs = (fields_ref, kappa_ref, zlo_ref, zhi_ref)
    nfield, depth_len, rows, lanes = fields_ref.shape
    lane = lax.broadcasted_iota(jnp.int32, (1, lanes), 1)
    edges = y_plan(nfield)[1]
    for i, (field, away, k) in enumerate(edges):
        plane = source_plane(refs, field, k if k < 0 else depth_len - 1 + k)
        lo_ref[i : i + 1, :] = plane[away - 1 : away, :]
        hi_ref[i : i + 1, :] = plane[rows - away : rows - away + 1, :]
    for field in range(nfield + 1):
        wide = reach(field, nfield)
        pair = (ownlo_ref[field], ownhi_ref[field])
        for z in list(range(-wide, 0)) + list(range(depth_len, depth_len + wide)):
            pair = take_columns(source_plane(refs, field, z)[...], z + W, lane, *pair)
        mainlo_ref[field], mainhi_ref[field] = pair
        for side in range(2):
            at = len(edges) + (side * (nfield + 1) + field) * W
            lo_ref[at : at + W, :] = pair[side][:W]
            hi_ref[at : at + W, :] = pair[side][rows - W :]


def assemble(refs, halo_rows, flags_ref, pad_ref):
    fields_ref, kappa_ref, zlo_ref, zhi_ref = refs
    nfield, depth_len, rows, lanes = fields_ref.shape
    planes, pitch = depth_len + 2 * W, rows + SUB
    halo = jnp.zeros((SUB, lanes), F32)

    @pl.loop(0, depth_len, unroll=steps(depth_len, 4))
    def _(z):
        for field in range(nfield + 1):
            plane = field * planes + W + z
            pad_ref[plane, :rows, :] = kappa_ref[z] if field == nfield else fields_ref[field, z]
            pad_ref[plane, rows:, :] = halo

    for field, at, wide in z_plan(nfield)[0]:
        for k in range(W):
            below, above = field * planes + W - 1 - k, field * planes + W + depth_len + k
            if k < wide:
                pad_ref[below, :rows, :] = zlo_ref[at + wide - 1 - k]
                pad_ref[above, :rows, :] = zhi_ref[at + k]
            for plane in (below, above):
                if k >= wide:
                    pad_ref[plane, :rows, :] = jnp.zeros((rows, lanes), F32)
                pad_ref[plane, rows:, :] = halo
    place_rows(pad_ref, depth_len, rows, halo_rows, flags_ref)


def place_rows(pad_ref, depth_len, first_row, halo_rows, flags_ref):
    planes = depth_len + 2 * W
    pitch, lanes = pad_ref.shape[1:]
    flat = pad_ref.reshape(pad_ref.shape[0] * pitch, lanes)
    kinds, edges = y_plan(pad_ref.shape[0] // planes - 1)
    for low, (ref, edge_ref) in ((True, halo_rows[:2]), (False, halo_rows[2:])):
        flag = flags_ref[2] if low else flags_ref[3]
        for i, (field, away) in enumerate(kinds):
            row = pitch - away if low else first_row + away - 1
            for z in range(0, depth_len, SUB):
                flat[pl.ds((field * planes + W + z) * pitch + row, SUB, stride=pitch), :] = (
                    ref[i, z : z + SUB, :] * flag
                )
        for i, (field, away, k) in enumerate(edges):
            row = pitch - away if low else first_row + away - 1
            plane = field * planes + W + (k if k < 0 else depth_len - 1 + k)
            pad_ref[plane, row : row + 1, :] = edge_ref[i : i + 1, :] * flag


def take_columns(value, zi, lane, low, high):
    lanes = value.shape[-1]
    mine = (lane >= W * zi) & (lane < W * zi + W)
    low = jnp.where(mine, pltpu.roll(value, W * zi, 1), low)
    high = jnp.where(mine, pltpu.roll(value, (W * zi + W) % lanes, 1), high)
    return low, high


def pack_own_kernel(fields_ref, kappa_ref, lo_ref, hi_ref):
    nfield, depth_len, rows, lanes = fields_ref.shape
    lane = lax.broadcasted_iota(jnp.int32, (1, lanes), 1)
    for field in range(nfield + 1):
        low = high = jnp.zeros((rows, lanes), F32)
        for z in range(depth_len):
            value = kappa_ref[z] if field == nfield else fields_ref[field, z]
            low, high = take_columns(value, z + W, lane, low, high)
        lo_ref[field] = low
        hi_ref[field] = high


def pack_columns_kernel(
    flags_ref, elo_ref, ehi_ref, mainlo_ref, mainhi_ref, rows_ref, lo_ref, hi_ref
):
    del rows_ref
    count, rows, lanes = mainlo_ref.shape
    at = len(y_plan(count - 1)[1])
    for main_ref, out_ref in ((mainlo_ref, lo_ref), (mainhi_ref, hi_ref)):
        for field in range(count):
            out_ref[field, :rows, :] = main_ref[field]
            out_ref[field, rows:, :] = jnp.zeros((SUB, lanes), F32)
            out_ref[field, rows : rows + W, :] = ehi_ref[at : at + W, :] * flags_ref[3]
            out_ref[field, rows + SUB - W :, :] = elo_ref[at : at + W, :] * flags_ref[2]
            at += W


def stencil(u, coefs, ups, downs, speeds):
    total = (coefs[3] - (speeds[0] + speeds[1] + speeds[2])) * u
    for axis in range(3):
        k_up, k_down = coefs[axis]
        total = total + k_up * ups[axis] + (k_down + speeds[axis]) * downs[axis]
    return total


def weights(k, ups, downs):
    half = 0.5 * k
    coefs = [(half + 0.5 * ups[a], half + 0.5 * downs[a]) for a in range(3)]
    rest = 1.0
    for up, down in coefs:
        rest = rest - (up + down)
    return coefs + [rest]


def side_neighbours(near, own, is_left, lanes, col):
    first, second = (near, own) if is_left else (own, near)
    first_up = jnp.where(col == W - 1, pltpu.roll(second, W - 1, 1), pltpu.roll(first, lanes - 1, 1))
    first_down = pltpu.roll(first, 1, 1)
    second_up = pltpu.roll(second, lanes - 1, 1)
    second_down = jnp.where(col == 0, pltpu.roll(first, lanes - (W - 1), 1), pltpu.roll(second, 1, 1))
    pair = ((first_up, first_down), (second_up, second_down))
    return pair if is_left else (pair[1], pair[0])


def main_kernel(
    flags_ref, courant_ref, center_ref, sharp_ref, gain_ref, color_ref, mask_ref, order_ref,
    fields_ref, kappa_ref, zlo_ref, zhi_ref,
    ylo_ref, elo_ref, yhi_ref, ehi_ref, xlo_ref, xhi_ref, ownlo_ref, ownhi_ref,
    state_ref, out_ref,
    pad_ref, next_ref, last_ref, side_ref, edge_ref, base_ref, tile_ref, coef_ref, held_ref, sem,
):
    nfield, depth_len, rows, lanes = state_ref.shape
    planes, pitch = depth_len + 2 * W, rows + SUB
    lane = lax.broadcasted_iota(jnp.int32, (pitch, lanes), 1)
    r = lax.broadcasted_iota(jnp.int32, (pitch, lanes), 0)
    zi_of = lane // W
    col = lane - zi_of * W
    flag = [flags_ref[i] for i in range(6)]
    speed = [[courant_ref[f, a] for a in range(3)] for f in range(nfield)]
    row_mask = jnp.where(r < rows, 1.0, jnp.where(r < rows + SUB // 2, flag[3], flag[2]))

    def along_y(value):
        return pltpu.roll(value, pitch - 1, 0), pltpu.roll(value, 1, 0)

    sides = ((xlo_ref, ownlo_ref, True, flag[4]), (xhi_ref, ownhi_ref, False, flag[5]))

    def block_of(level, side, block, field):
        if level == 0 or field == nfield:
            return sides[side][block][field]
        return side_ref[level - 1, side, block, field]

    def edges(level, field):
        left, right = block_of(level, 0, 0, field), block_of(level, 1, 0, field)
        edge_ref[level, field] = jnp.where(col == W - 1, left, pltpu.roll(right, 1, 1))

    def side_step(level, count):
        zmask = row_mask * jnp.where(
            zi_of < W, flag[0], jnp.where(zi_of >= W + depth_len, flag[1], 1.0)
        )
        for side, (_, _, is_left, present) in enumerate(sides):
            blocks = (0, 1) if level == 0 else (0,)

            def around(lvl, field):
                pair = [block_of(lvl, side, block, field) for block in (0, 1)]
                x = side_neighbours(pair[0], pair[1], is_left, lanes, col)
                found = []
                for block in blocks:
                    value = pair[block]
                    y_up, y_down = along_y(value)
                    ups = (pltpu.roll(value, lanes - W, 1), y_up, x[block][0])
                    downs = (pltpu.roll(value, W, 1), y_down, x[block][1])
                    found.append((value, ups, downs))
                return found

            coefs = [weights(*found) for found in around(0, nfield)]
            for field in range(count):
                for block, (u, ups, downs) in zip(blocks, around(level, field)):
                    value = stencil(u, coefs[block], ups, downs, speed[field])
                    side_ref[level, side, block, field] = value * (zmask * present if block == 0 else zmask)

    def along_x(value, zi, edge):
        n = value.shape[0]
        turned = pltpu.roll(edge, lax.rem(2 * lanes - 2 - W * zi, lanes), 1)
        up = jnp.where(lane[:n] == lanes - 1, turned, pltpu.roll(value, lanes - 1, 1))
        down = jnp.where(lane[:n] == 0, turned, pltpu.roll(value, 1, 1))
        return up, down

    def around(src_ref, level, field, zi, n):
        plane = field * planes + zi
        whole = src_ref[plane]
        value = whole[:n]
        y_up, y_down = along_y(whole)
        x_up, x_down = along_x(value, zi, edge_ref[level, field, :n, :])
        return (
            value,
            (src_ref[plane + 1, :n, :], y_up[:n], x_up),
            (src_ref[plane - 1, :n, :], y_down[:n], x_down),
        )

    def step_value(src_ref, level, field, zi, n, coefs):
        u, ups, downs = around(src_ref, level, field, zi, n)
        return stencil(u, coefs, ups, downs, speed[field])

    def kept(zi, n):
        found = [coef_ref[i, zi, :n, :] for i in range(7)]
        return [found[0:2], found[2:4], found[4:6], found[6]]

    def depth_mask(zi):
        return jnp.where(zi < W, flag[0], jnp.where(zi >= W + depth_len, flag[1], 1.0))

    halo_rows = (ylo_ref, elo_ref, yhi_ref, ehi_ref)
    assemble((fields_ref, kappa_ref, zlo_ref, zhi_ref), halo_rows, flags_ref, pad_ref)
    for field in range(nfield + 1):
        edges(0, field)
    side_step(0, nfield)
    for field in range(nfield):
        edges(1, field)
    side_step(1, 1)
    edges(2, 0)

    @pl.loop(1, planes - 1, unroll=steps(planes - 2, 6))
    def _(zi):
        mask = row_mask * depth_mask(zi)
        coefs = weights(*around(pad_ref, 0, nfield, zi, pitch))
        for i, value in enumerate(sum(coefs[:3], ()) + (coefs[3],)):
            coef_ref[i, zi] = value
        for field in range(nfield):
            next_ref[field * planes + zi] = mask * step_value(pad_ref, 0, field, zi, pitch, coefs)

    @pl.loop(2, planes - 2, unroll=steps(planes - 4, 17))
    def _(zi):
        coefs = kept(zi, pitch)
        last_ref[zi] = step_value(next_ref, 1, 0, zi, pitch, coefs) * (row_mask * depth_mask(zi))

    @pl.loop(0, depth_len, unroll=steps(depth_len, 8))
    def _(z):
        zi = z + W
        coefs = kept(zi, rows)
        s, ups, downs = around(last_ref, 2, 0, zi, rows)
        held_ref[0, z] = s
        g_z, g_y, g_x = [0.5 * (ups[a] - downs[a]) for a in range(3)]
        shade = 0.35 + 0.65 * jnp.abs(0.64 * g_z + 0.6 * g_y + 0.48 * g_x) * lax.rsqrt(
            g_z * g_z + g_y * g_y + g_x * g_x + 1.0
        )
        for field in range(1, nfield):
            value = step_value(next_ref, 1, field, zi, rows, coefs)
            held_ref[field, z] = value
            if field <= 3:
                base_ref[field, z] = shade * (0.5 + 0.5 * jnp.tanh(0.5 * value))
            if field == 4:
                base_ref[0, z] = 1.0 + 0.5 * jnp.tanh(value)

    keep = pltpu.make_async_copy(held_ref, state_ref, sem)
    keep.start()
    ntf = center_ref.shape[0]
    chunk = 4 if ntf % 4 == 0 else 1
    halves = rows // SUB

    @pl.loop(0, (ntf // chunk) * halves)
    def _(step):
        first = (step // halves) * chunk
        row = pl.multiple_of((step % halves) * SUB, SUB)
        shape = (SUB, lanes)
        mid = [jnp.full(shape, center_ref[first + j], jnp.float32) for j in range(chunk)]
        bend = [jnp.full(shape, sharp_ref[first + j] * -LOG2E, jnp.float32) for j in range(chunk)]
        dense = [jnp.full(shape, gain_ref[first + j] * -LOG2E, jnp.float32) for j in range(chunk)]
        passed = [jnp.ones(shape, jnp.float32)] * chunk
        total = [jnp.zeros(shape, jnp.float32)] * chunk
        acc = [[jnp.zeros(shape, jnp.float32)] * 3 for _ in range(chunk)]
        for z in range(depth_len):
            s = held_ref[0, z, pl.ds(row, SUB), :]
            modul = base_ref[0, z, pl.ds(row, SUB), :]
            base = [base_ref[k + 1, z, pl.ds(row, SUB), :] for k in range(3)]
            for j in range(chunk):
                diff = s - mid[j]
                total[j] = total[j] + modul * jnp.exp2(diff * diff * bend[j])
                after = jnp.exp2(total[j] * dense[j])
                weight = passed[j] - after
                passed[j] = after
                acc[j] = [acc[j][k] + weight * base[k] for k in range(3)]
        for j in range(chunk):
            start = ((first + j) * rows + row) * 4
            for k in range(3):
                tile_ref[pl.ds(start + k, SUB, stride=4), :] = acc[j][k] * color_ref[k, first + j]
            tile_ref[pl.ds(start + 3, SUB, stride=4), :] = 1.0 - passed[j]

    @pl.loop(0, order_ref.shape[0], unroll=steps(order_ref.shape[0], 64))
    def _(slot):
        tile = order_ref[slot]
        cover = mask_ref[lax.div(tile, rows), lax.rem(tile, rows)].astype(F32)
        out_ref[slot] = tile_ref[pl.ds(pl.multiple_of(tile * 4, 4), 4), :] * cover
    keep.wait()


def compose_kernel(part_ref, out_ref):
    slabs, rows, _ = part_ref.shape

    @pl.loop(0, rows // 32, unroll=rows // 32)
    def _(step):
        def load(slab, k):
            return part_ref[slab, pl.ds(step * 32 + k, 8, stride=4), :]

        acc = [load(0, k) for k in range(4)]
        for slab in range(1, slabs):
            clear = 1.0 - acc[3]
            acc = [acc[k] + clear * load(slab, k) for k in range(4)]
        for k in range(4):
            out_ref[pl.ds(step * 32 + k, 8, stride=4), :] = acc[k]


def compose(parts):
    vmem = pl.BlockSpec(memory_space=pltpu.VMEM)
    return pl.pallas_call(
        compose_kernel,
        out_shape=jax.ShapeDtypeStruct(parts.shape[1:], jnp.float32),
        in_specs=[vmem],
        out_specs=vmem,
        compiler_params=pltpu.CompilerParams(vmem_limit_bytes=16 * 1024 * 1024),
        name="compose",
    )(parts)


def is_odd(axis):
    return lax.rem(lax.axis_index(axis), 2) == 1


def swap_pairs(first, second, axis):
    count = lax.axis_size(axis)
    came = []
    for start, message in ((0, first), (1, second)):
        pairs = []
        for i in range(start, count - 1, 2):
            pairs += [(i, i + 1), (i + 1, i)]
        came.append(lax.ppermute(message, axis, pairs) if pairs else jnp.zeros_like(message))
    odd = is_odd(axis)
    return jnp.where(odd, came[0], came[1]), jnp.where(odd, came[1], came[0])


def swap_rows(low, high, axis):
    odd = is_odd(axis)
    first = jnp.where(odd, low, high)
    if lax.axis_size(axis) == 2:
        came = lax.ppermute(first, axis, [(0, 1), (1, 0)])
        return came, came
    return swap_pairs(first, jnp.where(odd, high, low), axis)


def present(axis):
    here = lax.axis_index(axis)
    return [(here > 0).astype(F32), (here < lax.axis_size(axis) - 1).astype(F32)]


def shards(
    fields, diffusivity, courant, tf_center, tf_sharp, tf_gain, tf_color, tile_mask, tile_perm
):
    nfield, depth_len, rows_len, cols_len = fields.shape
    planes, pitch = depth_len + 2 * W, rows_len + SUB
    smem = pl.BlockSpec(memory_space=pltpu.SMEM)
    vmem = pl.BlockSpec(memory_space=pltpu.VMEM)
    params = pltpu.CompilerParams(vmem_limit_bytes=16 * 1024 * 1024)

    def array(*shape):
        return jax.ShapeDtypeStruct(shape, F32)

    flags = jnp.stack(present("gz") + present("gy") + present("gx"))

    faces = z_plan(nfield)[1]
    first, second = pl.pallas_call(
        pack_planes_kernel,
        out_shape=(array(faces, rows_len, cols_len),) * 2,
        in_specs=[pl.BlockSpec(memory_space=pl.ANY)] * 2,
        out_specs=(pl.BlockSpec(memory_space=pl.ANY),) * 2,
        scratch_shapes=[pltpu.SemaphoreType.DMA((2 * nfield + 2,))],
        compiler_params=pltpu.CompilerParams(vmem_limit_bytes=60 * 1024 * 1024),
        name="pack_planes",
    )(fields, diffusivity)
    zlo, zhi = swap_pairs(first, second, "gz")
    kinds, outer = y_plan(nfield)
    send_lo, send_hi = pl.pallas_call(
        pack_rows_kernel,
        out_shape=(array(len(kinds), depth_len, cols_len),) * 2,
        in_specs=[vmem] * 2,
        out_specs=(vmem, vmem),
        compiler_params=params,
        name="pack_rows",
    )(fields, diffusivity)
    ylo, yhi = swap_rows(send_lo, send_hi, "gy")
    part_lo, part_hi = pl.pallas_call(
        pack_own_kernel,
        out_shape=(array(nfield + 1, rows_len, cols_len),) * 2,
        in_specs=[vmem] * 2,
        out_specs=(vmem,) * 2,
        compiler_params=params,
        cost_estimate=pl.CostEstimate(flops=10**7, bytes_accessed=4 * 10**6, transcendentals=0),
        name="pack_own",
    )(fields, diffusivity)
    extra = len(outer) + 2 * (nfield + 1) * W
    send_lo, send_hi, main_lo, main_hi = pl.pallas_call(
        pack_edges_kernel,
        out_shape=(array(extra, cols_len),) * 2 + (array(nfield + 1, rows_len, cols_len),) * 2,
        in_specs=[vmem] * 6,
        out_specs=(vmem,) * 4,
        compiler_params=params,
        name="pack_edges",
    )(fields, diffusivity, zlo, zhi, part_lo, part_hi)
    elo, ehi = swap_rows(send_lo, send_hi, "gy")
    pad = pltpu.VMEM(((nfield + 1) * planes, pitch, cols_len), F32)
    own_lo, own_hi = pl.pallas_call(
        pack_columns_kernel,
        out_shape=(array(nfield + 1, pitch, cols_len),) * 2,
        in_specs=[smem] + [vmem] * 4 + [pl.BlockSpec(memory_space=pl.ANY)],
        out_specs=(vmem,) * 2,
        compiler_params=params,
        name="pack_columns",
    )(flags, elo, ehi, main_lo, main_hi, ylo)
    odd = is_odd("gx")
    xlo, xhi = swap_pairs(jnp.where(odd, own_lo, own_hi), jnp.where(odd, own_hi, own_lo), "gx")
    count = lax.axis_size("gz")
    order = tile_perm[0, 0]
    per_owner = order.shape[0] // count
    state, tiles = pl.pallas_call(
        main_kernel,
        out_shape=(array(*fields.shape), array(order.shape[0], 4, cols_len)),
        in_specs=[smem] * 8 + [vmem] * 12,
        out_specs=(pl.BlockSpec(memory_space=pl.ANY), vmem),
        scratch_shapes=[
            pad,
            pltpu.VMEM((nfield * planes, pitch, cols_len), F32),
            pltpu.VMEM((planes, pitch, cols_len), F32),
            pltpu.VMEM((2, 2, 2, nfield, pitch, cols_len), F32),
            pltpu.VMEM((3, nfield + 1, pitch, cols_len), F32),
            pltpu.VMEM((4, depth_len, rows_len, cols_len), F32),
            pltpu.VMEM((order.shape[0] * 4, cols_len), F32),
            pltpu.VMEM((7, planes, pitch, cols_len), F32),
            pltpu.VMEM(fields.shape, F32),
            pltpu.SemaphoreType.DMA(()),
        ],
        compiler_params=pltpu.CompilerParams(vmem_limit_bytes=24 * 1024 * 1024),
        name="step_and_march",
    )(
        flags, courant, tf_center, tf_sharp, tf_gain, tf_color, tile_mask[0, :, :, 0], order,
        fields, diffusivity, zlo, zhi, ylo, elo, yhi, ehi, xlo, xhi, own_lo, own_hi,
    )
    grouped = tiles.reshape(count, per_owner * 4, cols_len)
    composed = compose(lax.all_to_all(grouped, "gz", split_axis=0, concat_axis=0, tiled=True))
    picture = composed.reshape(1, 1, per_owner, 4, cols_len)
    return (state, picture)


def solution(mesh):
    return jax.shard_map(
        shards,
        mesh=mesh,
        in_specs=(
            P(None, "gz", "gy", "gx"),
            P("gz", "gy", "gx"),
            P(),
            P(),
            P(),
            P(),
            P(),
            P("gz", None, "gy", "gx"),
            P("gy", "gx", None),
        ),
        out_specs=(P(None, "gz", "gy", "gx"), P("gy", "gx", "gz", None, None)),
        check_vma=False,
    )
```

```python
import jax
import jax.numpy as jnp
from jax import lax
from jax.experimental import pallas as pl
from jax.experimental.pallas import tpu as pltpu
from jax.sharding import PartitionSpec as P

LOG2E = 1.4426950408889634
W = 3
SUB = 8
F32 = jnp.float32


def reach(field, nfield):
    return W if field in (0, nfield) else W - 1


def tiles_of(first, last):
    return [min(start, last - SUB) for start in range(first, last, SUB)]


def z_plan(nfield):
    plan, at = [], 0
    for field in range(nfield + 1):
        plan.append((field, at, reach(field, nfield)))
        at += reach(field, nfield)
    return plan, at


def y_plan(nfield):
    kinds, edges = [], []
    for field in range(nfield + 1):
        wide = reach(field, nfield)
        for away in range(1, wide + 1):
            kinds.append((field, away))
            for k in range(1, wide - away + 1):
                edges.append((field, away, -k))
                edges.append((field, away, k))
    return kinds, edges


def pack_planes_kernel(fields_ref, kappa_ref, first_ref, second_ref, sems):
    nfield, depth_len = fields_ref.shape[:2]
    odd = lax.rem(lax.axis_index("gz"), 2)
    copies = []
    for field, at, wide in z_plan(nfield)[0]:
        source = kappa_ref if field == nfield else fields_ref.at[field]
        for place, target in ((1 - odd, first_ref), (odd, second_ref)):
            copies.append(
                pltpu.make_async_copy(
                    source.at[pl.ds(place * (depth_len - wide), wide)], target.at[pl.ds(at, wide)], sems.at[len(copies)]
                )
            )
    for copy in copies:
        copy.start()
    for copy in copies:
        copy.wait()


def present(axis):
    here = lax.axis_index(axis)
    return jnp.where(here > 0, 1.0, 0.0), jnp.where(here < lax.axis_size(axis) - 1, 1.0, 0.0)


def steps(count, most):
    return max(k for k in range(1, most + 1) if count % k == 0)


def source_plane(refs, field, z):
    fields_ref, kappa_ref, zlo_ref, zhi_ref = refs
    nfield, depth_len = fields_ref.shape[:2]
    _, at, wide = z_plan(nfield)[0][field]
    if z < 0:
        return zlo_ref.at[at + wide + z]
    if z >= depth_len:
        return zhi_ref.at[at + z - depth_len]
    return kappa_ref.at[z] if field == nfield else fields_ref.at[field, z]


def pack_rows_kernel(fields_ref, kappa_ref, lo_ref, hi_ref):
    nfield, depth_len, rows, lanes = fields_ref.shape
    flat_fields = fields_ref.reshape(nfield * depth_len * rows, lanes)
    flat_kappa = kappa_ref.reshape(depth_len * rows, lanes)
    for out_ref, top in ((lo_ref, True), (hi_ref, False)):
        for i, (field, away) in enumerate(y_plan(nfield)[0]):
            row = away - 1 if top else rows - away
            flat, base = (flat_kappa, 0) if field == nfield else (flat_fields, field * depth_len * rows)
            for z in range(0, depth_len, SUB):
                out_ref[i, z : z + SUB, :] = flat[pl.ds(base + z * rows + row, SUB, stride=rows), :]


def pack_edges_kernel(
    fields_ref, kappa_ref, zlo_ref, zhi_ref, ownlo_ref, ownhi_ref, lo_ref, hi_ref, mainlo_ref, mainhi_ref
):
    refs = (fields_ref, kappa_ref, zlo_ref, zhi_ref)
    nfield, depth_len, rows, lanes = fields_ref.shape
    lane = lax.broadcasted_iota(jnp.int32, (1, lanes), 1)
    edges = y_plan(nfield)[1]
    for i, (field, away, k) in enumerate(edges):
        plane = source_plane(refs, field, k if k < 0 else depth_len - 1 + k)
        lo_ref[i : i + 1, :] = plane[away - 1 : away, :]
        hi_ref[i : i + 1, :] = plane[rows - away : rows - away + 1, :]
    for field in range(nfield + 1):
        wide = reach(field, nfield)
        pair = (ownlo_ref[field], ownhi_ref[field])
        for z in list(range(-wide, 0)) + list(range(depth_len, depth_len + wide)):
            pair = take_columns(source_plane(refs, field, z)[...], z + W, lane, *pair)
        mainlo_ref[field], mainhi_ref[field] = pair
        for side in range(2):
            at = len(edges) + (side * (nfield + 1) + field) * W
            lo_ref[at : at + W, :] = pair[side][:W]
            hi_ref[at : at + W, :] = pair[side][rows - W :]


def assemble(refs, halo_rows, pad_ref):
    fields_ref, kappa_ref, zlo_ref, zhi_ref = refs
    nfield, depth_len, rows, lanes = fields_ref.shape
    planes, pitch = depth_len + 2 * W, rows + SUB
    halo = jnp.zeros((SUB, lanes), F32)

    @pl.loop(0, depth_len, unroll=steps(depth_len, 4))
    def _(z):
        for field in range(nfield + 1):
            plane = field * planes + W + z
            pad_ref[plane, :rows, :] = kappa_ref[z] if field == nfield else fields_ref[field, z]
            pad_ref[plane, rows:, :] = halo

    for field, at, wide in z_plan(nfield)[0]:
        for k in range(W):
            below, above = field * planes + W - 1 - k, field * planes + W + depth_len + k
            if k < wide:
                pad_ref[below, :rows, :] = zlo_ref[at + wide - 1 - k]
                pad_ref[above, :rows, :] = zhi_ref[at + k]
            for plane in (below, above):
                if k >= wide:
                    pad_ref[plane, :rows, :] = jnp.zeros((rows, lanes), F32)
                pad_ref[plane, rows:, :] = halo
    place_rows(pad_ref, depth_len, rows, halo_rows)


def place_rows(pad_ref, depth_len, first_row, halo_rows):
    planes = depth_len + 2 * W
    pitch, lanes = pad_ref.shape[1:]
    flat = pad_ref.reshape(pad_ref.shape[0] * pitch, lanes)
    kinds, edges = y_plan(pad_ref.shape[0] // planes - 1)
    for low, (ref, edge_ref) in ((True, halo_rows[:2]), (False, halo_rows[2:])):
        flag = present("gy")[0 if low else 1]
        for i, (field, away) in enumerate(kinds):
            row = pitch - away if low else first_row + away - 1
            for z in range(0, depth_len, SUB):
                flat[pl.ds((field * planes + W + z) * pitch + row, SUB, stride=pitch), :] = (
                    ref[i, z : z + SUB, :] * flag
                )
        for i, (field, away, k) in enumerate(edges):
            row = pitch - away if low else first_row + away - 1
            plane = field * planes + W + (k if k < 0 else depth_len - 1 + k)
            pad_ref[plane, row : row + 1, :] = edge_ref[i : i + 1, :] * flag


def take_columns(value, zi, lane, low, high):
    lanes = value.shape[-1]
    mine = (lane >= W * zi) & (lane < W * zi + W)
    low = jnp.where(mine, pltpu.roll(value, W * zi, 1), low)
    high = jnp.where(mine, pltpu.roll(value, (W * zi + W) % lanes, 1), high)
    return low, high


def pack_own_kernel(fields_ref, kappa_ref, lo_ref, hi_ref):
    nfield, depth_len, rows, lanes = fields_ref.shape
    lane = lax.broadcasted_iota(jnp.int32, (1, lanes), 1)
    for field in range(nfield + 1):
        low = high = jnp.zeros((rows, lanes), F32)
        for z in range(depth_len):
            value = kappa_ref[z] if field == nfield else fields_ref[field, z]
            low, high = take_columns(value, z + W, lane, low, high)
        lo_ref[field] = low
        hi_ref[field] = high


def pack_columns_kernel(
    elo_ref, ehi_ref, mainlo_ref, mainhi_ref, rows_ref, lo_ref, hi_ref
):
    del rows_ref
    count, rows, lanes = mainlo_ref.shape
    low, high = present("gy")
    at = len(y_plan(count - 1)[1])
    for main_ref, out_ref in ((mainlo_ref, lo_ref), (mainhi_ref, hi_ref)):
        for field in range(count):
            out_ref[field, :rows, :] = main_ref[field]
            out_ref[field, rows:, :] = jnp.zeros((SUB, lanes), F32)
            out_ref[field, rows : rows + W, :] = ehi_ref[at : at + W, :] * high
            out_ref[field, rows + SUB - W :, :] = elo_ref[at : at + W, :] * low
            at += W


def stencil(u, coefs, ups, downs, speeds):
    total = (coefs[3] - (speeds[0] + speeds[1] + speeds[2])) * u
    for axis in range(3):
        k_up, k_down = coefs[axis]
        total = total + k_up * ups[axis] + (k_down + speeds[axis]) * downs[axis]
    return total


def weights(k, ups, downs):
    half = 0.5 * k
    coefs = [(half + 0.5 * ups[a], half + 0.5 * downs[a]) for a in range(3)]
    rest = 1.0
    for up, down in coefs:
        rest = rest - (up + down)
    return coefs + [rest]


def side_neighbours(near, own, is_left, lanes, col):
    first, second = (near, own) if is_left else (own, near)
    first_up = jnp.where(col == W - 1, pltpu.roll(second, W - 1, 1), pltpu.roll(first, lanes - 1, 1))
    first_down = pltpu.roll(first, 1, 1)
    second_up = pltpu.roll(second, lanes - 1, 1)
    second_down = jnp.where(col == 0, pltpu.roll(first, lanes - (W - 1), 1), pltpu.roll(second, 1, 1))
    pair = ((first_up, first_down), (second_up, second_down))
    return pair if is_left else (pair[1], pair[0])


def main_kernel(
    courant_ref, center_ref, sharp_ref, gain_ref, color_ref, mask_ref, order_ref,
    fields_ref, kappa_ref, zlo_ref, zhi_ref,
    ylo_ref, elo_ref, yhi_ref, ehi_ref, xlo_ref, xhi_ref, ownlo_ref, ownhi_ref,
    state_ref, out_ref,
    pad_ref, next_ref, last_ref, side_ref, edge_ref, base_ref, tile_ref, coef_ref, held_ref, sem,
):
    nfield, depth_len, rows, lanes = state_ref.shape
    planes, pitch = depth_len + 2 * W, rows + SUB
    lane = lax.broadcasted_iota(jnp.int32, (pitch, lanes), 1)
    r = lax.broadcasted_iota(jnp.int32, (pitch, lanes), 0)
    zi_of = lane // W
    col = lane - zi_of * W
    flag = present("gz") + present("gy") + present("gx")
    speed = [[courant_ref[f, a] for a in range(3)] for f in range(nfield)]
    row_mask = jnp.where(r < rows, 1.0, jnp.where(r < rows + SUB // 2, flag[3], flag[2]))

    def along_y(value):
        return pltpu.roll(value, pitch - 1, 0), pltpu.roll(value, 1, 0)

    sides = ((xlo_ref, ownlo_ref, True, flag[4]), (xhi_ref, ownhi_ref, False, flag[5]))

    def block_of(level, side, block, field):
        if level == 0 or field == nfield:
            return sides[side][block][field]
        return side_ref[level - 1, side, block, field]

    def edges(level, field):
        left, right = block_of(level, 0, 0, field), block_of(level, 1, 0, field)
        edge_ref[level, field] = jnp.where(col == W - 1, left, pltpu.roll(right, 1, 1))

    def side_step(level, count):
        zmask = row_mask * jnp.where(
            zi_of < W, flag[0], jnp.where(zi_of >= W + depth_len, flag[1], 1.0)
        )
        for side, (_, _, is_left, present) in enumerate(sides):
            blocks = (0, 1) if level == 0 else (0,)

            def around(lvl, field):
                pair = [block_of(lvl, side, block, field) for block in (0, 1)]
                x = side_neighbours(pair[0], pair[1], is_left, lanes, col)
                found = []
                for block in blocks:
                    value = pair[block]
                    y_up, y_down = along_y(value)
                    ups = (pltpu.roll(value, lanes - W, 1), y_up, x[block][0])
                    downs = (pltpu.roll(value, W, 1), y_down, x[block][1])
                    found.append((value, ups, downs))
                return found

            coefs = [weights(*found) for found in around(0, nfield)]
            for field in range(count):
                for block, (u, ups, downs) in zip(blocks, around(level, field)):
                    value = stencil(u, coefs[block], ups, downs, speed[field])
                    side_ref[level, side, block, field] = value * (zmask * present if block == 0 else zmask)

    def along_x(value, zi, edge):
        n = value.shape[0]
        turned = pltpu.roll(edge, lax.rem(2 * lanes - 2 - W * zi, lanes), 1)
        up = jnp.where(lane[:n] == lanes - 1, turned, pltpu.roll(value, lanes - 1, 1))
        down = jnp.where(lane[:n] == 0, turned, pltpu.roll(value, 1, 1))
        return up, down

    def around(src_ref, level, field, zi, n):
        plane = field * planes + zi
        whole = src_ref[plane]
        value = whole[:n]
        y_up, y_down = along_y(whole)
        x_up, x_down = along_x(value, zi, edge_ref[level, field, :n, :])
        return (
            value,
            (src_ref[plane + 1, :n, :], y_up[:n], x_up),
            (src_ref[plane - 1, :n, :], y_down[:n], x_down),
        )

    def step_value(src_ref, level, field, zi, n, coefs):
        u, ups, downs = around(src_ref, level, field, zi, n)
        return stencil(u, coefs, ups, downs, speed[field])

    def kept(zi, n):
        found = [coef_ref[i, zi, :n, :] for i in range(7)]
        return [found[0:2], found[2:4], found[4:6], found[6]]

    def depth_mask(zi):
        return jnp.where(zi < W, flag[0], jnp.where(zi >= W + depth_len, flag[1], 1.0))

    halo_rows = (ylo_ref, elo_ref, yhi_ref, ehi_ref)
    assemble((fields_ref, kappa_ref, zlo_ref, zhi_ref), halo_rows, pad_ref)
    for field in range(nfield + 1):
        edges(0, field)
    side_step(0, nfield)
    for field in range(nfield):
        edges(1, field)
    side_step(1, 1)
    edges(2, 0)

    @pl.loop(1, planes - 1, unroll=steps(planes - 2, 6))
    def _(zi):
        mask = row_mask * depth_mask(zi)
        coefs = weights(*around(pad_ref, 0, nfield, zi, pitch))
        for i, value in enumerate(sum(coefs[:3], ()) + (coefs[3],)):
            coef_ref[i, zi] = value
        for field in range(nfield):
            next_ref[field * planes + zi] = mask * step_value(pad_ref, 0, field, zi, pitch, coefs)

    @pl.loop(2, planes - 2, unroll=steps(planes - 4, 17))
    def _(zi):
        coefs = kept(zi, pitch)
        last_ref[zi] = step_value(next_ref, 1, 0, zi, pitch, coefs) * (row_mask * depth_mask(zi))

    @pl.loop(0, depth_len, unroll=steps(depth_len, 8))
    def _(z):
        zi = z + W
        coefs = kept(zi, rows)
        s, ups, downs = around(last_ref, 2, 0, zi, rows)
        held_ref[0, z] = s
        g_z, g_y, g_x = [0.5 * (ups[a] - downs[a]) for a in range(3)]
        shade = 0.35 + 0.65 * jnp.abs(0.64 * g_z + 0.6 * g_y + 0.48 * g_x) * lax.rsqrt(
            g_z * g_z + g_y * g_y + g_x * g_x + 1.0
        )
        for field in range(1, nfield):
            value = step_value(next_ref, 1, field, zi, rows, coefs)
            held_ref[field, z] = value
            if field <= 3:
                base_ref[field, z] = shade * (0.5 + 0.5 * jnp.tanh(0.5 * value))
            if field == 4:
                base_ref[0, z] = 1.0 + 0.5 * jnp.tanh(value)

    keep = pltpu.make_async_copy(held_ref, state_ref, sem)
    keep.start()
    ntf = center_ref.shape[0]
    chunk = 4 if ntf % 4 == 0 else 1
    halves = rows // SUB

    @pl.loop(0, (ntf // chunk) * halves)
    def _(step):
        first = (step // halves) * chunk
        row = pl.multiple_of((step % halves) * SUB, SUB)
        shape = (SUB, lanes)
        mid = [jnp.full(shape, center_ref[first + j], jnp.float32) for j in range(chunk)]
        bend = [jnp.full(shape, sharp_ref[first + j] * -LOG2E, jnp.float32) for j in range(chunk)]
        dense = [jnp.full(shape, gain_ref[first + j] * -LOG2E, jnp.float32) for j in range(chunk)]
        passed = [jnp.ones(shape, jnp.float32)] * chunk
        total = [jnp.zeros(shape, jnp.float32)] * chunk
        acc = [[jnp.zeros(shape, jnp.float32)] * 3 for _ in range(chunk)]
        for z in range(depth_len):
            s = held_ref[0, z, pl.ds(row, SUB), :]
            modul = base_ref[0, z, pl.ds(row, SUB), :]
            base = [base_ref[k + 1, z, pl.ds(row, SUB), :] for k in range(3)]
            for j in range(chunk):
                diff = s - mid[j]
                total[j] = total[j] + modul * jnp.exp2(diff * diff * bend[j])
                after = jnp.exp2(total[j] * dense[j])
                weight = passed[j] - after
                passed[j] = after
                acc[j] = [acc[j][k] + weight * base[k] for k in range(3)]
        for j in range(chunk):
            start = ((first + j) * rows + row) * 4
            for k in range(3):
                tile_ref[pl.ds(start + k, SUB, stride=4), :] = acc[j][k] * color_ref[k, first + j]
            tile_ref[pl.ds(start + 3, SUB, stride=4), :] = 1.0 - passed[j]

    @pl.loop(0, order_ref.shape[0], unroll=steps(order_ref.shape[0], 64))
    def _(slot):
        tile = order_ref[slot]
        cover = mask_ref[lax.div(tile, rows), lax.rem(tile, rows)].astype(F32)
        out_ref[slot] = tile_ref[pl.ds(pl.multiple_of(tile * 4, 4), 4), :] * cover
    keep.wait()


def compose_kernel(part_ref, out_ref):
    slabs, rows, _ = part_ref.shape

    @pl.loop(0, rows // 32, unroll=rows // 32)
    def _(step):
        def load(slab, k):
            return part_ref[slab, pl.ds(step * 32 + k, 8, stride=4), :]

        acc = [load(0, k) for k in range(4)]
        for slab in range(1, slabs):
            clear = 1.0 - acc[3]
            acc = [acc[k] + clear * load(slab, k) for k in range(4)]
        for k in range(4):
            out_ref[pl.ds(step * 32 + k, 8, stride=4), :] = acc[k]


def compose(parts):
    vmem = pl.BlockSpec(memory_space=pltpu.VMEM)
    return pl.pallas_call(
        compose_kernel,
        out_shape=jax.ShapeDtypeStruct(parts.shape[1:], jnp.float32),
        in_specs=[vmem],
        out_specs=vmem,
        compiler_params=pltpu.CompilerParams(vmem_limit_bytes=16 * 1024 * 1024),
        name="compose",
    )(parts)


def is_odd(axis):
    return lax.rem(lax.axis_index(axis), 2) == 1


def swap_pairs(first, second, axis):
    count = lax.axis_size(axis)
    came = []
    for start, message in ((0, first), (1, second)):
        pairs = []
        for i in range(start, count - 1, 2):
            pairs += [(i, i + 1), (i + 1, i)]
        came.append(lax.ppermute(message, axis, pairs) if pairs else jnp.zeros_like(message))
    odd = is_odd(axis)
    return jnp.where(odd, came[0], came[1]), jnp.where(odd, came[1], came[0])


def swap_rows(low, high, axis):
    odd = is_odd(axis)
    first = jnp.where(odd, low, high)
    if lax.axis_size(axis) == 2:
        came = lax.ppermute(first, axis, [(0, 1), (1, 0)])
        return came, came
    return swap_pairs(first, jnp.where(odd, high, low), axis)


def shards(
    fields, diffusivity, courant, tf_center, tf_sharp, tf_gain, tf_color, tile_mask, tile_perm
):
    nfield, depth_len, rows_len, cols_len = fields.shape
    planes, pitch = depth_len + 2 * W, rows_len + SUB
    smem = pl.BlockSpec(memory_space=pltpu.SMEM)
    vmem = pl.BlockSpec(memory_space=pltpu.VMEM)
    params = pltpu.CompilerParams(vmem_limit_bytes=16 * 1024 * 1024)

    def array(*shape):
        return jax.ShapeDtypeStruct(shape, F32)

    faces = z_plan(nfield)[1]
    first, second = pl.pallas_call(
        pack_planes_kernel,
        out_shape=(array(faces, rows_len, cols_len),) * 2,
        in_specs=[pl.BlockSpec(memory_space=pl.ANY)] * 2,
        out_specs=(vmem, vmem),
        scratch_shapes=[pltpu.SemaphoreType.DMA((2 * nfield + 2,))],
        compiler_params=pltpu.CompilerParams(vmem_limit_bytes=60 * 1024 * 1024),
        name="pack_planes",
    )(fields, diffusivity)
    zlo, zhi = swap_pairs(first, second, "gz")
    kinds, outer = y_plan(nfield)
    send_lo, send_hi = pl.pallas_call(
        pack_rows_kernel,
        out_shape=(array(len(kinds), depth_len, cols_len),) * 2,
        in_specs=[vmem] * 2,
        out_specs=(vmem, vmem),
        compiler_params=params,
        name="pack_rows",
    )(fields, diffusivity)
    ylo, yhi = swap_rows(send_lo, send_hi, "gy")
    part_lo, part_hi = pl.pallas_call(
        pack_own_kernel,
        out_shape=(array(nfield + 1, rows_len, cols_len),) * 2,
        in_specs=[vmem] * 2,
        out_specs=(vmem,) * 2,
        compiler_params=params,
        cost_estimate=pl.CostEstimate(flops=10**7, bytes_accessed=4 * 10**6, transcendentals=0),
        name="pack_own",
    )(fields, diffusivity)
    extra = len(outer) + 2 * (nfield + 1) * W
    send_lo, send_hi, main_lo, main_hi = pl.pallas_call(
        pack_edges_kernel,
        out_shape=(array(extra, cols_len),) * 2 + (array(nfield + 1, rows_len, cols_len),) * 2,
        in_specs=[vmem] * 6,
        out_specs=(vmem,) * 4,
        compiler_params=params,
        name="pack_edges",
    )(fields, diffusivity, zlo, zhi, part_lo, part_hi)
    elo, ehi = swap_rows(send_lo, send_hi, "gy")
    pad = pltpu.VMEM(((nfield + 1) * planes, pitch, cols_len), F32)
    own_lo, own_hi = pl.pallas_call(
        pack_columns_kernel,
        out_shape=(array(nfield + 1, pitch, cols_len),) * 2,
        in_specs=[vmem] * 4 + [pl.BlockSpec(memory_space=pl.ANY)],
        out_specs=(vmem,) * 2,
        compiler_params=params,
        name="pack_columns",
    )(elo, ehi, main_lo, main_hi, ylo)
    odd = is_odd("gx")
    xlo, xhi = swap_pairs(jnp.where(odd, own_lo, own_hi), jnp.where(odd, own_hi, own_lo), "gx")
    count = lax.axis_size("gz")
    order = tile_perm[0, 0]
    per_owner = order.shape[0] // count
    state, tiles = pl.pallas_call(
        main_kernel,
        out_shape=(array(*fields.shape), array(order.shape[0], 4, cols_len)),
        in_specs=[smem] * 7 + [vmem] * 12,
        out_specs=(pl.BlockSpec(memory_space=pl.ANY), vmem),
        scratch_shapes=[
            pad,
            pltpu.VMEM((nfield * planes, pitch, cols_len), F32),
            pltpu.VMEM((planes, pitch, cols_len), F32),
            pltpu.VMEM((2, 2, 2, nfield, pitch, cols_len), F32),
            pltpu.VMEM((3, nfield + 1, pitch, cols_len), F32),
            pltpu.VMEM((4, depth_len, rows_len, cols_len), F32),
            pltpu.VMEM((order.shape[0] * 4, cols_len), F32),
            pltpu.VMEM((7, planes, pitch, cols_len), F32),
            pltpu.VMEM(fields.shape, F32),
            pltpu.SemaphoreType.DMA(()),
        ],
        compiler_params=pltpu.CompilerParams(vmem_limit_bytes=24 * 1024 * 1024),
        name="step_and_march",
    )(
        courant, tf_center, tf_sharp, tf_gain, tf_color, tile_mask[0, :, :, 0], order,
        fields, diffusivity, zlo, zhi, ylo, elo, yhi, ehi, xlo, xhi, own_lo, own_hi,
    )
    grouped = tiles.reshape(count, per_owner * 4, cols_len)
    composed = compose(lax.all_to_all(grouped, "gz", split_axis=0, concat_axis=0, tiled=True))
    picture = composed.reshape(1, 1, per_owner, 4, cols_len)
    return (state, picture)


def solution(mesh):
    return jax.shard_map(
        shards,
        mesh=mesh,
        in_specs=(
            P(None, "gz", "gy", "gx"),
            P("gz", "gy", "gx"),
            P(),
            P(),
            P(),
            P(),
            P(),
            P("gz", None, "gy", "gx"),
            P("gy", "gx", None),
        ),
        out_specs=(P(None, "gz", "gy", "gx"), P("gy", "gx", "gz", None, None)),
        check_vma=False,
    )
```

```python
import jax
import jax.numpy as jnp
from jax import lax
from jax.experimental import pallas as pl
from jax.experimental.pallas import tpu as pltpu
from jax.sharding import PartitionSpec as P

LOG2E = 1.4426950408889634
W = 3
SUB = 8
F32 = jnp.float32


def reach(field, nfield):
    return W if field in (0, nfield) else W - 1


def tiles_of(first, last):
    return [min(start, last - SUB) for start in range(first, last, SUB)]


def z_plan(nfield):
    plan, at = [], 0
    for field in range(nfield + 1):
        plan.append((field, at, reach(field, nfield)))
        at += reach(field, nfield)
    return plan, at


def y_plan(nfield):
    kinds, edges = [], []
    for field in range(nfield + 1):
        wide = reach(field, nfield)
        for away in range(1, wide + 1):
            kinds.append((field, away))
            for k in range(1, wide - away + 1):
                edges.append((field, away, -k))
                edges.append((field, away, k))
    return kinds, edges


def pack_planes_kernel(fields_ref, kappa_ref, first_ref, second_ref, sems):
    nfield, depth_len = fields_ref.shape[:2]
    odd = lax.rem(lax.axis_index("gz"), 2)
    copies = []
    for field, at, wide in z_plan(nfield)[0]:
        source = kappa_ref if field == nfield else fields_ref.at[field]
        for place, target in ((1 - odd, first_ref), (odd, second_ref)):
            copies.append(
                pltpu.make_async_copy(
                    source.at[pl.ds(place * (depth_len - wide), wide)], target.at[pl.ds(at, wide)], sems.at[len(copies)]
                )
            )
    for copy in copies:
        copy.start()
    for copy in copies:
        copy.wait()


def present(axis):
    here = lax.axis_index(axis)
    return jnp.where(here > 0, 1.0, 0.0), jnp.where(here < lax.axis_size(axis) - 1, 1.0, 0.0)


def steps(count, most):
    return max(k for k in range(1, most + 1) if count % k == 0)


def source_plane(refs, field, z):
    fields_ref, kappa_ref, zlo_ref, zhi_ref = refs
    nfield, depth_len = fields_ref.shape[:2]
    _, at, wide = z_plan(nfield)[0][field]
    if z < 0:
        return zlo_ref.at[at + wide + z]
    if z >= depth_len:
        return zhi_ref.at[at + z - depth_len]
    return kappa_ref.at[z] if field == nfield else fields_ref.at[field, z]


def pack_rows_kernel(fields_ref, kappa_ref, lo_ref, hi_ref):
    nfield, depth_len, rows, lanes = fields_ref.shape
    flat_fields = fields_ref.reshape(nfield * depth_len * rows, lanes)
    flat_kappa = kappa_ref.reshape(depth_len * rows, lanes)
    for out_ref, top in ((lo_ref, True), (hi_ref, False)):
        for i, (field, away) in enumerate(y_plan(nfield)[0]):
            row = away - 1 if top else rows - away
            flat, base = (flat_kappa, 0) if field == nfield else (flat_fields, field * depth_len * rows)
            for z in range(0, depth_len, SUB):
                out_ref[i, z : z + SUB, :] = flat[pl.ds(base + z * rows + row, SUB, stride=rows), :]


def pack_edges_kernel(
    fields_ref, kappa_ref, zlo_ref, zhi_ref, ownlo_ref, ownhi_ref, lo_ref, hi_ref, mainlo_ref, mainhi_ref
):
    refs = (fields_ref, kappa_ref, zlo_ref, zhi_ref)
    nfield, depth_len, rows, lanes = fields_ref.shape
    lane = lax.broadcasted_iota(jnp.int32, (1, lanes), 1)
    edges = y_plan(nfield)[1]
    for i, (field, away, k) in enumerate(edges):
        plane = source_plane(refs, field, k if k < 0 else depth_len - 1 + k)
        lo_ref[i : i + 1, :] = plane[away - 1 : away, :]
        hi_ref[i : i + 1, :] = plane[rows - away : rows - away + 1, :]
    for field in range(nfield + 1):
        wide = reach(field, nfield)
        pair = (ownlo_ref[field], ownhi_ref[field])
        for z in list(range(-wide, 0)) + list(range(depth_len, depth_len + wide)):
            pair = take_columns(source_plane(refs, field, z)[...], z + W, lane, *pair)
        mainlo_ref[field], mainhi_ref[field] = pair
        for side in range(2):
            at = len(edges) + (side * (nfield + 1) + field) * W
            lo_ref[at : at + W, :] = pair[side][:W]
            hi_ref[at : at + W, :] = pair[side][rows - W :]


def assemble(refs, halo_rows, pad_ref, chosen):
    fields_ref, kappa_ref, zlo_ref, zhi_ref = refs
    nfield, depth_len, rows, lanes = fields_ref.shape
    planes, pitch = depth_len + 2 * W, rows + SUB
    halo = jnp.zeros((SUB, lanes), F32)

    @pl.loop(0, depth_len, unroll=steps(depth_len, 4))
    def _(z):
        for slot, field in enumerate(chosen):
            plane = slot * planes + W + z
            pad_ref[plane, :rows, :] = kappa_ref[z] if field == nfield else fields_ref[field, z]
            pad_ref[plane, rows:, :] = halo

    for slot, field in enumerate(chosen):
        _, at, wide = z_plan(nfield)[0][field]
        for k in range(W):
            below, above = slot * planes + W - 1 - k, slot * planes + W + depth_len + k
            if k < wide:
                pad_ref[below, :rows, :] = zlo_ref[at + wide - 1 - k]
                pad_ref[above, :rows, :] = zhi_ref[at + k]
            for plane in (below, above):
                if k >= wide:
                    pad_ref[plane, :rows, :] = jnp.zeros((rows, lanes), F32)
                pad_ref[plane, rows:, :] = halo
    pitch, lanes = pad_ref.shape[1:]
    flat = pad_ref.reshape(pad_ref.shape[0] * pitch, lanes)
    kinds, edges = y_plan(nfield)
    for low, (ref, edge_ref) in ((True, halo_rows[:2]), (False, halo_rows[2:])):
        flag = present("gy")[0 if low else 1]
        for i, (field, away) in enumerate(kinds):
            if field not in chosen:
                continue
            row = pitch - away if low else rows + away - 1
            for z in range(0, depth_len, SUB):
                flat[pl.ds((chosen.index(field) * planes + W + z) * pitch + row, SUB, stride=pitch), :] = (
                    ref[i, z : z + SUB, :] * flag
                )
        for i, (field, away, k) in enumerate(edges):
            if field not in chosen:
                continue
            row = pitch - away if low else rows + away - 1
            plane = chosen.index(field) * planes + W + (k if k < 0 else depth_len - 1 + k)
            pad_ref[plane, row : row + 1, :] = edge_ref[i : i + 1, :] * flag


def take_columns(value, zi, lane, low, high):
    lanes = value.shape[-1]
    mine = (lane >= W * zi) & (lane < W * zi + W)
    low = jnp.where(mine, pltpu.roll(value, W * zi, 1), low)
    high = jnp.where(mine, pltpu.roll(value, (W * zi + W) % lanes, 1), high)
    return low, high


def pack_own_kernel(fields_ref, kappa_ref, lo_ref, hi_ref):
    nfield, depth_len, rows, lanes = fields_ref.shape
    lane = lax.broadcasted_iota(jnp.int32, (1, lanes), 1)
    for field in range(nfield + 1):
        low = high = jnp.zeros((rows, lanes), F32)
        for z in range(depth_len):
            value = kappa_ref[z] if field == nfield else fields_ref[field, z]
            low, high = take_columns(value, z + W, lane, low, high)
        lo_ref[field] = low
        hi_ref[field] = high


def pack_columns_kernel(
    elo_ref, ehi_ref, mainlo_ref, mainhi_ref, rows_ref, lo_ref, hi_ref
):
    del rows_ref
    count, rows, lanes = mainlo_ref.shape
    low, high = present("gy")
    at = len(y_plan(count - 1)[1])
    for main_ref, out_ref in ((mainlo_ref, lo_ref), (mainhi_ref, hi_ref)):
        for field in range(count):
            out_ref[field, :rows, :] = main_ref[field]
            out_ref[field, rows:, :] = jnp.zeros((SUB, lanes), F32)
            out_ref[field, rows : rows + W, :] = ehi_ref[at : at + W, :] * high
            out_ref[field, rows + SUB - W :, :] = elo_ref[at : at + W, :] * low
            at += W


def stencil(u, coefs, ups, downs, speeds):
    total = (coefs[3] - (speeds[0] + speeds[1] + speeds[2])) * u
    for axis in range(3):
        k_up, k_down = coefs[axis]
        total = total + k_up * ups[axis] + (k_down + speeds[axis]) * downs[axis]
    return total


def weights(k, ups, downs):
    half = 0.5 * k
    coefs = [(half + 0.5 * ups[a], half + 0.5 * downs[a]) for a in range(3)]
    rest = 1.0
    for up, down in coefs:
        rest = rest - (up + down)
    return coefs + [rest]


def row_flags(shape, rows):
    r = lax.broadcasted_iota(jnp.int32, shape, 0)
    low, high = present("gy")
    return jnp.where(r < rows, 1.0, jnp.where(r < rows + SUB // 2, high, low))


def plane_flag(zi, depth_len):
    low, high = present("gz")
    return jnp.where(zi < W, low, jnp.where(zi >= W + depth_len, high, 1.0))


def first_step_kernel(
    courant_ref, fields_ref, kappa_ref, zlo_ref, zhi_ref, ylo_ref, elo_ref, yhi_ref, ehi_ref, *rest
):
    out_refs, pad_ref = rest[:-1], rest[-1]
    nfield, depth_len, rows, lanes = fields_ref.shape
    planes, pitch = depth_len + 2 * W, rows + SUB
    refs, halo_rows = (fields_ref, kappa_ref, zlo_ref, zhi_ref), (ylo_ref, elo_ref, yhi_ref, ehi_ref)
    assemble(refs, halo_rows, pad_ref, list(range(nfield + 1)))
    lane = lax.broadcasted_iota(jnp.int32, (pitch, lanes), 1)
    row_mask = row_flags((pitch, lanes), rows)
    speed = [[courant_ref[f, a] for a in range(3)] for f in range(nfield)]

    def around(field, zi):
        plane = field * planes + zi
        value = pad_ref[plane]
        x_up = jnp.where(lane == lanes - 1, value, pltpu.roll(value, lanes - 1, 1))
        x_down = jnp.where(lane == 0, value, pltpu.roll(value, 1, 1))
        ups = (pad_ref[plane + 1], pltpu.roll(value, pitch - 1, 0), x_up)
        downs = (pad_ref[plane - 1], pltpu.roll(value, 1, 0), x_down)
        return value, ups, downs

    @pl.loop(1, planes - 1, unroll=steps(planes - 2, 6))
    def _(zi):
        mask = row_mask * plane_flag(zi, depth_len)
        coefs = weights(*around(nfield, zi))
        for field in range(nfield):
            u, ups, downs = around(field, zi)
            out_refs[field][zi] = mask * stencil(u, coefs, ups, downs, speed[field])


def side_neighbours(near, own, is_left, lanes, col):
    first, second = (near, own) if is_left else (own, near)
    first_up = jnp.where(col == W - 1, pltpu.roll(second, W - 1, 1), pltpu.roll(first, lanes - 1, 1))
    first_down = pltpu.roll(first, 1, 1)
    second_up = pltpu.roll(second, lanes - 1, 1)
    second_down = jnp.where(col == 0, pltpu.roll(first, lanes - (W - 1), 1), pltpu.roll(second, 1, 1))
    pair = ((first_up, first_down), (second_up, second_down))
    return pair if is_left else (pair[1], pair[0])


def main_kernel(
    courant_ref, center_ref, sharp_ref, gain_ref, color_ref, mask_ref, order_ref,
    fields_ref, kappa_ref, zlo_ref, zhi_ref,
    ylo_ref, elo_ref, yhi_ref, ehi_ref, xlo_ref, xhi_ref, ownlo_ref, ownhi_ref, *rest,
):
    nfield, depth_len, rows, lanes = fields_ref.shape
    step_refs = rest[:nfield]
    (
        state_ref, out_ref, kpad_ref, next_ref, last_ref, side_ref, edge_ref, base_ref,
        tile_ref, coef_ref, held_ref, flux_ref, sem,
    ) = rest[nfield:]
    nfield, depth_len, rows, lanes = state_ref.shape
    planes, pitch = depth_len + 2 * W, rows + SUB
    lane = lax.broadcasted_iota(jnp.int32, (pitch, lanes), 1)
    zi_of = lane // W
    col = lane - zi_of * W
    flag = present("gz") + present("gy") + present("gx")
    speed = [[courant_ref[f, a] for a in range(3)] for f in range(nfield)]
    row_mask = row_flags((pitch, lanes), rows)

    def along_y(value):
        return pltpu.roll(value, pitch - 1, 0), pltpu.roll(value, 1, 0)

    sides = ((xlo_ref, ownlo_ref, True, flag[4]), (xhi_ref, ownhi_ref, False, flag[5]))

    def block_of(level, side, block, field):
        if level == 0 or field == nfield:
            return sides[side][block][field]
        return side_ref[level - 1, side, block, field]

    def edges(level, field):
        left, right = block_of(level, 0, 0, field), block_of(level, 1, 0, field)
        edge_ref[level, field] = jnp.where(col == W - 1, left, pltpu.roll(right, 1, 1))

    def side_step(level, count):
        zmask = row_mask * jnp.where(
            zi_of < W, flag[0], jnp.where(zi_of >= W + depth_len, flag[1], 1.0)
        )
        for side, (_, _, is_left, present) in enumerate(sides):
            blocks = (0, 1) if level == 0 else (0,)

            def around(lvl, field):
                pair = [block_of(lvl, side, block, field) for block in (0, 1)]
                x = side_neighbours(pair[0], pair[1], is_left, lanes, col)
                found = []
                for block in blocks:
                    value = pair[block]
                    y_up, y_down = along_y(value)
                    ups = (pltpu.roll(value, lanes - W, 1), y_up, x[block][0])
                    downs = (pltpu.roll(value, W, 1), y_down, x[block][1])
                    found.append((value, ups, downs))
                return found

            coefs = [weights(*found) for found in around(0, nfield)]
            for field in range(count):
                for block, (u, ups, downs) in zip(blocks, around(level, field)):
                    value = stencil(u, coefs[block], ups, downs, speed[field])
                    side_ref[level, side, block, field] = value * (zmask * present if block == 0 else zmask)

    def along_x(value, zi, edge):
        n = value.shape[0]
        turned = pltpu.roll(edge, lax.rem(2 * lanes - 2 - W * zi, lanes), 1)
        up = jnp.where(lane[:n] == lanes - 1, turned, pltpu.roll(value, lanes - 1, 1))
        down = jnp.where(lane[:n] == 0, turned, pltpu.roll(value, 1, 1))
        return up, down

    def around(src_ref, level, field, zi, n, slot=None):
        plane = (field if slot is None else slot) * planes + zi
        whole = src_ref[plane]
        value = whole[:n]
        y_up, y_down = along_y(whole)
        x_up, x_down = along_x(value, zi, edge_ref[level, field, :n, :])
        return (
            value,
            (src_ref[plane + 1, :n, :], y_up[:n], x_up),
            (src_ref[plane - 1, :n, :], y_down[:n], x_down),
        )

    def step_value(src_ref, level, field, zi, n, coefs):
        u, ups, downs = around(src_ref, level, field, zi, n)
        return stencil(u, coefs, ups, downs, speed[field])

    def kept(zi, n):
        found = [coef_ref[i, zi, :n, :] for i in range(7)]
        return [found[0:2], found[2:4], found[4:6], found[6]]

    halo_rows = (ylo_ref, elo_ref, yhi_ref, ehi_ref)
    assemble((fields_ref, kappa_ref, zlo_ref, zhi_ref), halo_rows, kpad_ref, [nfield])
    edges(0, nfield)
    lane_mask = row_mask * jnp.where(
        zi_of < W, flag[0], jnp.where(zi_of >= W + depth_len, flag[1], 1.0)
    )
    k_left = 0.5 * (xlo_ref[nfield] + pltpu.roll(ownlo_ref[nfield], W - 1, 1))
    k_right = 0.5 * (xhi_ref[nfield] + pltpu.roll(ownhi_ref[nfield], lanes - (W - 1), 1))
    for field in range(nfield):
        left = (k_left + speed[field][2]) * (xlo_ref[field] - pltpu.roll(ownlo_ref[field], W - 1, 1))
        right = k_right * (xhi_ref[field] - pltpu.roll(ownhi_ref[field], lanes - (W - 1), 1))
        flux_ref[field] = lane_mask * jnp.where(col == W - 1, left, pltpu.roll(right, 1, 1))
    side_step(0, nfield)
    for field in range(nfield):
        edges(1, field)
    side_step(1, 1)
    edges(2, 0)

    @pl.loop(1, planes - 1, unroll=steps(planes - 2, 6))
    def _(zi):
        coefs = weights(*around(kpad_ref, 0, nfield, zi, pitch, 0))
        for i, value in enumerate(sum(coefs[:3], ()) + (coefs[3],)):
            coef_ref[i, zi] = value
        outer = (lane == 0) | (lane == lanes - 1)
        for field in range(nfield):
            turned = pltpu.roll(flux_ref[field], lax.rem(2 * lanes - 2 - W * zi, lanes), 1)
            next_ref[field * planes + zi] = step_refs[field][zi] + jnp.where(outer, turned, 0.0)

    @pl.loop(2, planes - 2, unroll=steps(planes - 4, 17))
    def _(zi):
        coefs = kept(zi, pitch)
        last_ref[zi] = step_value(next_ref, 1, 0, zi, pitch, coefs) * (row_mask * plane_flag(zi, depth_len))

    @pl.loop(0, depth_len, unroll=steps(depth_len, 8))
    def _(z):
        zi = z + W
        coefs = kept(zi, rows)
        s, ups, downs = around(last_ref, 2, 0, zi, rows)
        held_ref[0, z] = s
        g_z, g_y, g_x = [0.5 * (ups[a] - downs[a]) for a in range(3)]
        shade = 0.35 + 0.65 * jnp.abs(0.64 * g_z + 0.6 * g_y + 0.48 * g_x) * lax.rsqrt(
            g_z * g_z + g_y * g_y + g_x * g_x + 1.0
        )
        for field in range(1, nfield):
            value = step_value(next_ref, 1, field, zi, rows, coefs)
            held_ref[field, z] = value
            if field <= 3:
                base_ref[field, z] = shade * (0.5 + 0.5 * jnp.tanh(0.5 * value))
            if field == 4:
                base_ref[0, z] = 1.0 + 0.5 * jnp.tanh(value)

    keep = pltpu.make_async_copy(held_ref, state_ref, sem)
    keep.start()
    ntf = center_ref.shape[0]
    chunk = 4 if ntf % 4 == 0 else 1
    halves = rows // SUB

    @pl.loop(0, (ntf // chunk) * halves)
    def _(step):
        first = (step // halves) * chunk
        row = pl.multiple_of((step % halves) * SUB, SUB)
        shape = (SUB, lanes)
        mid = [jnp.full(shape, center_ref[first + j], jnp.float32) for j in range(chunk)]
        bend = [jnp.full(shape, sharp_ref[first + j] * -LOG2E, jnp.float32) for j in range(chunk)]
        dense = [jnp.full(shape, gain_ref[first + j] * -LOG2E, jnp.float32) for j in range(chunk)]
        passed = [jnp.ones(shape, jnp.float32)] * chunk
        total = [jnp.zeros(shape, jnp.float32)] * chunk
        acc = [[jnp.zeros(shape, jnp.float32)] * 3 for _ in range(chunk)]
        for z in range(depth_len):
            s = held_ref[0, z, pl.ds(row, SUB), :]
            modul = base_ref[0, z, pl.ds(row, SUB), :]
            base = [base_ref[k + 1, z, pl.ds(row, SUB), :] for k in range(3)]
            for j in range(chunk):
                diff = s - mid[j]
                total[j] = total[j] + modul * jnp.exp2(diff * diff * bend[j])
                after = jnp.exp2(total[j] * dense[j])
                weight = passed[j] - after
                passed[j] = after
                acc[j] = [acc[j][k] + weight * base[k] for k in range(3)]
        for j in range(chunk):
            start = ((first + j) * rows + row) * 4
            for k in range(3):
                tile_ref[pl.ds(start + k, SUB, stride=4), :] = acc[j][k] * color_ref[k, first + j]
            tile_ref[pl.ds(start + 3, SUB, stride=4), :] = 1.0 - passed[j]

    @pl.loop(0, order_ref.shape[0], unroll=steps(order_ref.shape[0], 64))
    def _(slot):
        tile = order_ref[slot]
        cover = mask_ref[lax.div(tile, rows), lax.rem(tile, rows)].astype(F32)
        out_ref[slot] = tile_ref[pl.ds(pl.multiple_of(tile * 4, 4), 4), :] * cover
    keep.wait()


def compose_kernel(part_ref, out_ref):
    slabs, rows, _ = part_ref.shape

    @pl.loop(0, rows // 32, unroll=rows // 32)
    def _(step):
        def load(slab, k):
            return part_ref[slab, pl.ds(step * 32 + k, 8, stride=4), :]

        acc = [load(0, k) for k in range(4)]
        for slab in range(1, slabs):
            clear = 1.0 - acc[3]
            acc = [acc[k] + clear * load(slab, k) for k in range(4)]
        for k in range(4):
            out_ref[pl.ds(step * 32 + k, 8, stride=4), :] = acc[k]


def compose(parts):
    vmem = pl.BlockSpec(memory_space=pltpu.VMEM)
    return pl.pallas_call(
        compose_kernel,
        out_shape=jax.ShapeDtypeStruct(parts.shape[1:], jnp.float32),
        in_specs=[vmem],
        out_specs=vmem,
        compiler_params=pltpu.CompilerParams(vmem_limit_bytes=16 * 1024 * 1024),
        name="compose",
    )(parts)


def is_odd(axis):
    return lax.rem(lax.axis_index(axis), 2) == 1


def swap_pairs(first, second, axis):
    count = lax.axis_size(axis)
    came = []
    for start, message in ((0, first), (1, second)):
        pairs = []
        for i in range(start, count - 1, 2):
            pairs += [(i, i + 1), (i + 1, i)]
        came.append(lax.ppermute(message, axis, pairs) if pairs else jnp.zeros_like(message))
    odd = is_odd(axis)
    return jnp.where(odd, came[0], came[1]), jnp.where(odd, came[1], came[0])


def swap_rows(low, high, axis):
    odd = is_odd(axis)
    first = jnp.where(odd, low, high)
    if lax.axis_size(axis) == 2:
        came = lax.ppermute(first, axis, [(0, 1), (1, 0)])
        return came, came
    return swap_pairs(first, jnp.where(odd, high, low), axis)


def shards(
    fields, diffusivity, courant, tf_center, tf_sharp, tf_gain, tf_color, tile_mask, tile_perm
):
    nfield, depth_len, rows_len, cols_len = fields.shape
    planes, pitch = depth_len + 2 * W, rows_len + SUB
    smem = pl.BlockSpec(memory_space=pltpu.SMEM)
    vmem = pl.BlockSpec(memory_space=pltpu.VMEM)
    params = pltpu.CompilerParams(vmem_limit_bytes=16 * 1024 * 1024)

    def array(*shape):
        return jax.ShapeDtypeStruct(shape, F32)

    faces = z_plan(nfield)[1]
    first, second = pl.pallas_call(
        pack_planes_kernel,
        out_shape=(array(faces, rows_len, cols_len),) * 2,
        in_specs=[pl.BlockSpec(memory_space=pl.ANY)] * 2,
        out_specs=(vmem, vmem),
        scratch_shapes=[pltpu.SemaphoreType.DMA((2 * nfield + 2,))],
        compiler_params=pltpu.CompilerParams(vmem_limit_bytes=60 * 1024 * 1024),
        name="pack_planes",
    )(fields, diffusivity)
    zlo, zhi = swap_pairs(first, second, "gz")
    kinds, outer = y_plan(nfield)
    send_lo, send_hi = pl.pallas_call(
        pack_rows_kernel,
        out_shape=(array(len(kinds), depth_len, cols_len),) * 2,
        in_specs=[vmem] * 2,
        out_specs=(vmem, vmem),
        compiler_params=params,
        name="pack_rows",
    )(fields, diffusivity)
    ylo, yhi = swap_rows(send_lo, send_hi, "gy")
    part_lo, part_hi = pl.pallas_call(
        pack_own_kernel,
        out_shape=(array(nfield + 1, rows_len, cols_len),) * 2,
        in_specs=[vmem] * 2,
        out_specs=(vmem,) * 2,
        compiler_params=params,
        cost_estimate=pl.CostEstimate(flops=10**7, bytes_accessed=4 * 10**6, transcendentals=0),
        name="pack_own",
    )(fields, diffusivity)
    extra = len(outer) + 2 * (nfield + 1) * W
    send_lo, send_hi, main_lo, main_hi = pl.pallas_call(
        pack_edges_kernel,
        out_shape=(array(extra, cols_len),) * 2 + (array(nfield + 1, rows_len, cols_len),) * 2,
        in_specs=[vmem] * 6,
        out_specs=(vmem,) * 4,
        compiler_params=params,
        name="pack_edges",
    )(fields, diffusivity, zlo, zhi, part_lo, part_hi)
    elo, ehi = swap_rows(send_lo, send_hi, "gy")
    pad = pltpu.VMEM(((nfield + 1) * planes, pitch, cols_len), F32)
    own_lo, own_hi = pl.pallas_call(
        pack_columns_kernel,
        out_shape=(array(nfield + 1, pitch, cols_len),) * 2,
        in_specs=[vmem] * 4 + [pl.BlockSpec(memory_space=pl.ANY)],
        out_specs=(vmem,) * 2,
        compiler_params=params,
        name="pack_columns",
    )(elo, ehi, main_lo, main_hi, ylo)
    odd = is_odd("gx")
    xlo, xhi = swap_pairs(jnp.where(odd, own_lo, own_hi), jnp.where(odd, own_hi, own_lo), "gx")
    stepped = pl.pallas_call(
        first_step_kernel,
        out_shape=(array(planes, pitch, cols_len),) * nfield,
        in_specs=[smem] + [vmem] * 8,
        out_specs=(vmem,) * nfield,
        scratch_shapes=[pad],
        compiler_params=params,
        cost_estimate=pl.CostEstimate(flops=10**8, bytes_accessed=8 * 10**6, transcendentals=0),
        name="first_step",
    )(courant, fields, diffusivity, zlo, zhi, ylo, elo, yhi, ehi)
    count = lax.axis_size("gz")
    order = tile_perm[0, 0]
    per_owner = order.shape[0] // count
    state, tiles = pl.pallas_call(
        main_kernel,
        out_shape=(array(*fields.shape), array(order.shape[0], 4, cols_len)),
        in_specs=[smem] * 7 + [vmem] * (12 + nfield),
        out_specs=(pl.BlockSpec(memory_space=pl.ANY), vmem),
        scratch_shapes=[
            pltpu.VMEM((planes, pitch, cols_len), F32),
            pltpu.VMEM((nfield * planes, pitch, cols_len), F32),
            pltpu.VMEM((planes, pitch, cols_len), F32),
            pltpu.VMEM((2, 2, 2, nfield, pitch, cols_len), F32),
            pltpu.VMEM((3, nfield + 1, pitch, cols_len), F32),
            pltpu.VMEM((4, depth_len, rows_len, cols_len), F32),
            pltpu.VMEM((order.shape[0] * 4, cols_len), F32),
            pltpu.VMEM((7, planes, pitch, cols_len), F32),
            pltpu.VMEM(fields.shape, F32),
            pltpu.VMEM((nfield, pitch, cols_len), F32),
            pltpu.SemaphoreType.DMA(()),
        ],
        compiler_params=pltpu.CompilerParams(vmem_limit_bytes=24 * 1024 * 1024),
        name="step_and_march",
    )(
        courant, tf_center, tf_sharp, tf_gain, tf_color, tile_mask[0, :, :, 0], order,
        fields, diffusivity, zlo, zhi, ylo, elo, yhi, ehi, xlo, xhi, own_lo, own_hi,
        *stepped,
    )
    grouped = tiles.reshape(count, per_owner * 4, cols_len)
    composed = compose(lax.all_to_all(grouped, "gz", split_axis=0, concat_axis=0, tiled=True))
    picture = composed.reshape(1, 1, per_owner, 4, cols_len)
    return (state, picture)


def solution(mesh):
    return jax.shard_map(
        shards,
        mesh=mesh,
        in_specs=(
            P(None, "gz", "gy", "gx"),
            P("gz", "gy", "gx"),
            P(),
            P(),
            P(),
            P(),
            P(),
            P("gz", None, "gy", "gx"),
            P("gy", "gx", None),
        ),
        out_specs=(P(None, "gz", "gy", "gx"), P("gy", "gx", "gz", None, None)),
        check_vma=False,
    )
```

```python
import jax
import jax.numpy as jnp
from jax import lax
from jax.experimental import pallas as pl
from jax.experimental.pallas import tpu as pltpu
from jax.sharding import PartitionSpec as P

LOG2E = 1.4426950408889634
W = 3
SUB = 8
F32 = jnp.float32


def reach(field, nfield):
    return W if field in (0, nfield) else W - 1


def tiles_of(first, last):
    return [min(start, last - SUB) for start in range(first, last, SUB)]


def z_plan(nfield):
    plan, at = [], 0
    for field in range(nfield + 1):
        plan.append((field, at, reach(field, nfield)))
        at += reach(field, nfield)
    return plan, at


def y_plan(nfield):
    kinds, edges = [], []
    for field in range(nfield + 1):
        wide = reach(field, nfield)
        for away in range(1, wide + 1):
            kinds.append((field, away))
            for k in range(1, wide - away + 1):
                edges.append((field, away, -k))
                edges.append((field, away, k))
    return kinds, edges


def pack_planes_kernel(fields_ref, kappa_ref, first_ref, second_ref, sems):
    nfield, depth_len = fields_ref.shape[:2]
    odd = lax.rem(lax.axis_index("gz"), 2)
    copies = []
    for field, at, wide in z_plan(nfield)[0]:
        source = kappa_ref if field == nfield else fields_ref.at[field]
        for place, target in ((1 - odd, first_ref), (odd, second_ref)):
            copies.append(
                pltpu.make_async_copy(
                    source.at[pl.ds(place * (depth_len - wide), wide)], target.at[pl.ds(at, wide)], sems.at[len(copies)]
                )
            )
    for copy in copies:
        copy.start()
    for copy in copies:
        copy.wait()


def present(axis):
    here = lax.axis_index(axis)
    return jnp.where(here > 0, 1.0, 0.0), jnp.where(here < lax.axis_size(axis) - 1, 1.0, 0.0)


def steps(count, most):
    return max(k for k in range(1, most + 1) if count % k == 0)


def source_plane(refs, field, z):
    fields_ref, kappa_ref, zlo_ref, zhi_ref = refs
    nfield, depth_len = fields_ref.shape[:2]
    _, at, wide = z_plan(nfield)[0][field]
    if z < 0:
        return zlo_ref.at[at + wide + z]
    if z >= depth_len:
        return zhi_ref.at[at + z - depth_len]
    return kappa_ref.at[z] if field == nfield else fields_ref.at[field, z]


def pack_rows_kernel(fields_ref, kappa_ref, lo_ref, hi_ref):
    nfield, depth_len, rows, lanes = fields_ref.shape
    flat_fields = fields_ref.reshape(nfield * depth_len * rows, lanes)
    flat_kappa = kappa_ref.reshape(depth_len * rows, lanes)
    for out_ref, top in ((lo_ref, True), (hi_ref, False)):
        for i, (field, away) in enumerate(y_plan(nfield)[0]):
            row = away - 1 if top else rows - away
            flat, base = (flat_kappa, 0) if field == nfield else (flat_fields, field * depth_len * rows)
            for z in range(0, depth_len, SUB):
                out_ref[i, z : z + SUB, :] = flat[pl.ds(base + z * rows + row, SUB, stride=rows), :]


def pack_edges_kernel(
    fields_ref, kappa_ref, zlo_ref, zhi_ref, ownlo_ref, ownhi_ref, lo_ref, hi_ref, mainlo_ref, mainhi_ref
):
    refs = (fields_ref, kappa_ref, zlo_ref, zhi_ref)
    nfield, depth_len, rows, lanes = fields_ref.shape
    lane = lax.broadcasted_iota(jnp.int32, (1, lanes), 1)
    edges = y_plan(nfield)[1]
    for i, (field, away, k) in enumerate(edges):
        plane = source_plane(refs, field, k if k < 0 else depth_len - 1 + k)
        lo_ref[i : i + 1, :] = plane[away - 1 : away, :]
        hi_ref[i : i + 1, :] = plane[rows - away : rows - away + 1, :]
    for field in range(nfield + 1):
        wide = reach(field, nfield)
        pair = (ownlo_ref[field], ownhi_ref[field])
        for z in list(range(-wide, 0)) + list(range(depth_len, depth_len + wide)):
            pair = take_columns(source_plane(refs, field, z)[...], z + W, lane, *pair)
        mainlo_ref[field], mainhi_ref[field] = pair
        for side in range(2):
            at = len(edges) + (side * (nfield + 1) + field) * W
            lo_ref[at : at + W, :] = pair[side][:W]
            hi_ref[at : at + W, :] = pair[side][rows - W :]


def assemble(refs, halo_rows, pad_ref, chosen):
    fields_ref, kappa_ref, zlo_ref, zhi_ref = refs
    nfield, depth_len, rows, lanes = fields_ref.shape
    planes, pitch = depth_len + 2 * W, rows + SUB
    halo = jnp.zeros((SUB, lanes), F32)

    @pl.loop(0, depth_len, unroll=steps(depth_len, 4))
    def _(z):
        for slot, field in enumerate(chosen):
            plane = slot * planes + W + z
            pad_ref[plane, :rows, :] = kappa_ref[z] if field == nfield else fields_ref[field, z]
            pad_ref[plane, rows:, :] = halo

    for slot, field in enumerate(chosen):
        _, at, wide = z_plan(nfield)[0][field]
        for k in range(W):
            below, above = slot * planes + W - 1 - k, slot * planes + W + depth_len + k
            if k < wide:
                pad_ref[below, :rows, :] = zlo_ref[at + wide - 1 - k]
                pad_ref[above, :rows, :] = zhi_ref[at + k]
            for plane in (below, above):
                if k >= wide:
                    pad_ref[plane, :rows, :] = jnp.zeros((rows, lanes), F32)
                pad_ref[plane, rows:, :] = halo
    pitch, lanes = pad_ref.shape[1:]
    flat = pad_ref.reshape(pad_ref.shape[0] * pitch, lanes)
    kinds, edges = y_plan(nfield)
    for low, (ref, edge_ref) in ((True, halo_rows[:2]), (False, halo_rows[2:])):
        flag = present("gy")[0 if low else 1]
        for i, (field, away) in enumerate(kinds):
            if field not in chosen:
                continue
            row = pitch - away if low else rows + away - 1
            for z in range(0, depth_len, SUB):
                flat[pl.ds((chosen.index(field) * planes + W + z) * pitch + row, SUB, stride=pitch), :] = (
                    ref[i, z : z + SUB, :] * flag
                )
        for i, (field, away, k) in enumerate(edges):
            if field not in chosen:
                continue
            row = pitch - away if low else rows + away - 1
            plane = chosen.index(field) * planes + W + (k if k < 0 else depth_len - 1 + k)
            pad_ref[plane, row : row + 1, :] = edge_ref[i : i + 1, :] * flag


def take_columns(value, zi, lane, low, high):
    lanes = value.shape[-1]
    mine = (lane >= W * zi) & (lane < W * zi + W)
    low = jnp.where(mine, pltpu.roll(value, W * zi, 1), low)
    high = jnp.where(mine, pltpu.roll(value, (W * zi + W) % lanes, 1), high)
    return low, high


def pack_own_kernel(fields_ref, kappa_ref, lo_ref, hi_ref):
    nfield, depth_len, rows, lanes = fields_ref.shape
    lane = lax.broadcasted_iota(jnp.int32, (1, lanes), 1)
    for field in range(nfield + 1):
        low = high = jnp.zeros((rows, lanes), F32)
        for z in range(depth_len):
            value = kappa_ref[z] if field == nfield else fields_ref[field, z]
            low, high = take_columns(value, z + W, lane, low, high)
        lo_ref[field] = low
        hi_ref[field] = high


def pack_columns_kernel(
    elo_ref, ehi_ref, mainlo_ref, mainhi_ref, rows_ref, lo_ref, hi_ref
):
    del rows_ref
    count, rows, lanes = mainlo_ref.shape
    low, high = present("gy")
    at = len(y_plan(count - 1)[1])
    for main_ref, out_ref in ((mainlo_ref, lo_ref), (mainhi_ref, hi_ref)):
        for field in range(count):
            out_ref[field, :rows, :] = main_ref[field]
            out_ref[field, rows:, :] = jnp.zeros((SUB, lanes), F32)
            out_ref[field, rows : rows + W, :] = ehi_ref[at : at + W, :] * high
            out_ref[field, rows + SUB - W :, :] = elo_ref[at : at + W, :] * low
            at += W


def stencil(u, coefs, ups, downs, speeds):
    total = (coefs[3] - (speeds[0] + speeds[1] + speeds[2])) * u
    for axis in range(3):
        k_up, k_down = coefs[axis]
        total = total + k_up * ups[axis] + (k_down + speeds[axis]) * downs[axis]
    return total


def weights(k, ups, downs):
    half = 0.5 * k
    coefs = [(half + 0.5 * ups[a], half + 0.5 * downs[a]) for a in range(3)]
    rest = 1.0
    for up, down in coefs:
        rest = rest - (up + down)
    return coefs + [rest]


def row_flags(shape, rows):
    r = lax.broadcasted_iota(jnp.int32, shape, 0)
    low, high = present("gy")
    return jnp.where(r < rows, 1.0, jnp.where(r < rows + SUB // 2, high, low))


def plane_flag(zi, depth_len):
    low, high = present("gz")
    return jnp.where(zi < W, low, jnp.where(zi >= W + depth_len, high, 1.0))


def first_step_kernel(
    courant_ref, fields_ref, kappa_ref, zlo_ref, zhi_ref, ylo_ref, elo_ref, yhi_ref, ehi_ref, *rest
):
    out_refs, coef_ref, pad_ref = rest[:-2], rest[-2], rest[-1]
    nfield, depth_len, rows, lanes = fields_ref.shape
    planes, pitch = depth_len + 2 * W, rows + SUB
    refs, halo_rows = (fields_ref, kappa_ref, zlo_ref, zhi_ref), (ylo_ref, elo_ref, yhi_ref, ehi_ref)
    assemble(refs, halo_rows, pad_ref, list(range(nfield + 1)))
    lane = lax.broadcasted_iota(jnp.int32, (pitch, lanes), 1)
    row_mask = row_flags((pitch, lanes), rows)
    speed = [[courant_ref[f, a] for a in range(3)] for f in range(nfield)]

    def around(field, zi):
        plane = field * planes + zi
        value = pad_ref[plane]
        x_up = jnp.where(lane == lanes - 1, value, pltpu.roll(value, lanes - 1, 1))
        x_down = jnp.where(lane == 0, value, pltpu.roll(value, 1, 1))
        ups = (pad_ref[plane + 1], pltpu.roll(value, pitch - 1, 0), x_up)
        downs = (pad_ref[plane - 1], pltpu.roll(value, 1, 0), x_down)
        return value, ups, downs

    @pl.loop(1, planes - 1, unroll=steps(planes - 2, 6))
    def _(zi):
        mask = row_mask * plane_flag(zi, depth_len)
        coefs = weights(*around(nfield, zi))
        for i, value in enumerate(sum(coefs[:3], ()) + (coefs[3],)):
            coef_ref[i, zi] = value
        for field in range(nfield):
            u, ups, downs = around(field, zi)
            out_refs[field][zi] = mask * stencil(u, coefs, ups, downs, speed[field])


def side_neighbours(near, own, is_left, lanes, col):
    first, second = (near, own) if is_left else (own, near)
    first_up = jnp.where(col == W - 1, pltpu.roll(second, W - 1, 1), pltpu.roll(first, lanes - 1, 1))
    first_down = pltpu.roll(first, 1, 1)
    second_up = pltpu.roll(second, lanes - 1, 1)
    second_down = jnp.where(col == 0, pltpu.roll(first, lanes - (W - 1), 1), pltpu.roll(second, 1, 1))
    pair = ((first_up, first_down), (second_up, second_down))
    return pair if is_left else (pair[1], pair[0])


def main_kernel(
    courant_ref, center_ref, sharp_ref, gain_ref, color_ref, mask_ref, order_ref,
    xlo_ref, xhi_ref, ownlo_ref, ownhi_ref, coef_ref, *rest,
):
    nfield = courant_ref.shape[0]
    step_refs = rest[:nfield]
    (
        state_ref, out_ref, next_ref, last_ref, side_ref, edge_ref, base_ref, tile_ref, held_ref,
        flux_ref, sem,
    ) = rest[nfield:]
    _, depth_len, rows, lanes = held_ref.shape
    planes, pitch = depth_len + 2 * W, rows + SUB
    lane = lax.broadcasted_iota(jnp.int32, (pitch, lanes), 1)
    zi_of = lane // W
    col = lane - zi_of * W
    flag = present("gz") + present("gy") + present("gx")
    speed = [[courant_ref[f, a] for a in range(3)] for f in range(nfield)]
    row_mask = row_flags((pitch, lanes), rows)

    def along_y(value):
        return pltpu.roll(value, pitch - 1, 0), pltpu.roll(value, 1, 0)

    sides = ((xlo_ref, ownlo_ref, True, flag[4]), (xhi_ref, ownhi_ref, False, flag[5]))

    def block_of(level, side, block, field):
        if level == 0 or field == nfield:
            return sides[side][block][field]
        return side_ref[level - 1, side, block, field]

    def fluxes(level, field, masks):
        near, own = [[block_of(level, side, block, field) for side in (0, 1)] for block in (0, 1)]
        left = (k_left + speed[field][2]) * (near[0] - pltpu.roll(own[0], W - 1, 1))
        right = k_right * (near[1] - pltpu.roll(own[1], lanes - (W - 1), 1))
        flux_ref[level, field] = masks * jnp.where(col == W - 1, left, pltpu.roll(right, 1, 1))

    def side_step(level, count):
        zmask = row_mask * jnp.where(
            zi_of < W, flag[0], jnp.where(zi_of >= W + depth_len, flag[1], 1.0)
        )
        for side, (_, _, is_left, present) in enumerate(sides):
            blocks = (0, 1) if level == 0 else (0,)

            def around(lvl, field):
                pair = [block_of(lvl, side, block, field) for block in (0, 1)]
                x = side_neighbours(pair[0], pair[1], is_left, lanes, col)
                found = []
                for block in blocks:
                    value = pair[block]
                    y_up, y_down = along_y(value)
                    ups = (pltpu.roll(value, lanes - W, 1), y_up, x[block][0])
                    downs = (pltpu.roll(value, W, 1), y_down, x[block][1])
                    found.append((value, ups, downs))
                return found

            coefs = [weights(*found) for found in around(0, nfield)]
            for field in range(count):
                for block, (u, ups, downs) in zip(blocks, around(level, field)):
                    value = stencil(u, coefs[block], ups, downs, speed[field])
                    side_ref[level, side, block, field] = value * (zmask * present if block == 0 else zmask)

    def turned(packed, zi, n):
        return pltpu.roll(packed[:n], lax.rem(2 * lanes - 2 - W * zi, lanes), 1)

    def step_value(field, zi, n, coefs):
        plane = field * planes + zi
        whole = next_ref[plane]
        u = whole[:n]
        y_up, y_down = along_y(whole)
        x_up = jnp.where(lane[:n] == lanes - 1, u, pltpu.roll(u, lanes - 1, 1))
        x_down = jnp.where(lane[:n] == 0, u, pltpu.roll(u, 1, 1))
        ups = (next_ref[plane + 1, :n, :], y_up[:n], x_up)
        downs = (next_ref[plane - 1, :n, :], y_down[:n], x_down)
        inner = stencil(u, coefs, ups, downs, speed[field])
        return inner + jnp.where(outer[:n], turned(flux_ref[1, field], zi, n), 0.0)

    def kept(zi, n):
        found = [coef_ref[i, zi, :n, :] for i in range(7)]
        return [found[0:2], found[2:4], found[4:6], found[6]]

    outer = (lane == 0) | (lane == lanes - 1)
    lane_mask = row_mask * jnp.where(
        zi_of < W, flag[0], jnp.where(zi_of >= W + depth_len, flag[1], 1.0)
    )
    k_left = 0.5 * (xlo_ref[nfield] + pltpu.roll(ownlo_ref[nfield], W - 1, 1))
    k_right = 0.5 * (xhi_ref[nfield] + pltpu.roll(ownhi_ref[nfield], lanes - (W - 1), 1))
    for field in range(nfield):
        fluxes(0, field, lane_mask)
    side_step(0, nfield)
    for field in range(nfield):
        fluxes(1, field, lane_mask)
    side_step(1, 1)
    left, right = block_of(2, 0, 0, 0), block_of(2, 1, 0, 0)
    edge_ref[...] = jnp.where(col == W - 1, left, pltpu.roll(right, 1, 1))

    @pl.loop(1, planes - 1, unroll=steps(planes - 2, 6))
    def _(zi):
        for field in range(nfield):
            next_ref[field * planes + zi] = step_refs[field][zi] + jnp.where(
                outer, turned(flux_ref[0, field], zi, pitch), 0.0
            )

    @pl.loop(2, planes - 2, unroll=steps(planes - 4, 17))
    def _(zi):
        coefs = kept(zi, pitch)
        last_ref[zi] = step_value(0, zi, pitch, coefs) * (row_mask * plane_flag(zi, depth_len))

    @pl.loop(0, depth_len, unroll=steps(depth_len, 8))
    def _(z):
        zi = z + W
        coefs = kept(zi, rows)
        whole = last_ref[zi]
        s = whole[:rows]
        held_ref[0, z] = s
        y_up, y_down = along_y(whole)
        beside = turned(edge_ref[...], zi, rows)
        x_up = jnp.where(lane[:rows] == lanes - 1, beside, pltpu.roll(s, lanes - 1, 1))
        x_down = jnp.where(lane[:rows] == 0, beside, pltpu.roll(s, 1, 1))
        g_z = 0.5 * (last_ref[zi + 1, :rows, :] - last_ref[zi - 1, :rows, :])
        g_y = 0.5 * (y_up[:rows] - y_down[:rows])
        g_x = 0.5 * (x_up - x_down)
        shade = 0.35 + 0.65 * jnp.abs(0.64 * g_z + 0.6 * g_y + 0.48 * g_x) * lax.rsqrt(
            g_z * g_z + g_y * g_y + g_x * g_x + 1.0
        )
        for field in range(1, nfield):
            value = step_value(field, zi, rows, coefs)
            held_ref[field, z] = value
            if field <= 3:
                base_ref[field, z] = shade * (0.5 + 0.5 * jnp.tanh(0.5 * value))
            if field == 4:
                base_ref[0, z] = 1.0 + 0.5 * jnp.tanh(value)

    keep = pltpu.make_async_copy(held_ref, state_ref, sem)
    keep.start()
    ntf = center_ref.shape[0]
    chunk = 4 if ntf % 4 == 0 else 1
    halves = rows // SUB

    @pl.loop(0, (ntf // chunk) * halves)
    def _(step):
        first = (step // halves) * chunk
        row = pl.multiple_of((step % halves) * SUB, SUB)
        shape = (SUB, lanes)
        mid = [jnp.full(shape, center_ref[first + j], jnp.float32) for j in range(chunk)]
        bend = [jnp.full(shape, sharp_ref[first + j] * -LOG2E, jnp.float32) for j in range(chunk)]
        dense = [jnp.full(shape, gain_ref[first + j] * -LOG2E, jnp.float32) for j in range(chunk)]
        passed = [jnp.ones(shape, jnp.float32)] * chunk
        total = [jnp.zeros(shape, jnp.float32)] * chunk
        acc = [[jnp.zeros(shape, jnp.float32)] * 3 for _ in range(chunk)]
        for z in range(depth_len):
            s = held_ref[0, z, pl.ds(row, SUB), :]
            modul = base_ref[0, z, pl.ds(row, SUB), :]
            base = [base_ref[k + 1, z, pl.ds(row, SUB), :] for k in range(3)]
            for j in range(chunk):
                diff = s - mid[j]
                total[j] = total[j] + modul * jnp.exp2(diff * diff * bend[j])
                after = jnp.exp2(total[j] * dense[j])
                weight = passed[j] - after
                passed[j] = after
                acc[j] = [acc[j][k] + weight * base[k] for k in range(3)]
        for j in range(chunk):
            start = ((first + j) * rows + row) * 4
            for k in range(3):
                tile_ref[pl.ds(start + k, SUB, stride=4), :] = acc[j][k] * color_ref[k, first + j]
            tile_ref[pl.ds(start + 3, SUB, stride=4), :] = 1.0 - passed[j]

    @pl.loop(0, order_ref.shape[0], unroll=steps(order_ref.shape[0], 64))
    def _(slot):
        tile = order_ref[slot]
        cover = mask_ref[lax.div(tile, rows), lax.rem(tile, rows)].astype(F32)
        out_ref[slot] = tile_ref[pl.ds(pl.multiple_of(tile * 4, 4), 4), :] * cover
    keep.wait()


def compose_kernel(part_ref, out_ref):
    slabs, rows, _ = part_ref.shape

    @pl.loop(0, rows // 32, unroll=rows // 32)
    def _(step):
        def load(slab, k):
            return part_ref[slab, pl.ds(step * 32 + k, 8, stride=4), :]

        acc = [load(0, k) for k in range(4)]
        for slab in range(1, slabs):
            clear = 1.0 - acc[3]
            acc = [acc[k] + clear * load(slab, k) for k in range(4)]
        for k in range(4):
            out_ref[pl.ds(step * 32 + k, 8, stride=4), :] = acc[k]


def compose(parts):
    vmem = pl.BlockSpec(memory_space=pltpu.VMEM)
    return pl.pallas_call(
        compose_kernel,
        out_shape=jax.ShapeDtypeStruct(parts.shape[1:], jnp.float32),
        in_specs=[vmem],
        out_specs=vmem,
        compiler_params=pltpu.CompilerParams(vmem_limit_bytes=16 * 1024 * 1024),
        name="compose",
    )(parts)


def is_odd(axis):
    return lax.rem(lax.axis_index(axis), 2) == 1


def swap_pairs(first, second, axis):
    count = lax.axis_size(axis)
    came = []
    for start, message in ((0, first), (1, second)):
        pairs = []
        for i in range(start, count - 1, 2):
            pairs += [(i, i + 1), (i + 1, i)]
        came.append(lax.ppermute(message, axis, pairs) if pairs else jnp.zeros_like(message))
    odd = is_odd(axis)
    return jnp.where(odd, came[0], came[1]), jnp.where(odd, came[1], came[0])


def swap_rows(low, high, axis):
    odd = is_odd(axis)
    first = jnp.where(odd, low, high)
    if lax.axis_size(axis) == 2:
        came = lax.ppermute(first, axis, [(0, 1), (1, 0)])
        return came, came
    return swap_pairs(first, jnp.where(odd, high, low), axis)


def shards(
    fields, diffusivity, courant, tf_center, tf_sharp, tf_gain, tf_color, tile_mask, tile_perm
):
    nfield, depth_len, rows_len, cols_len = fields.shape
    planes, pitch = depth_len + 2 * W, rows_len + SUB
    smem = pl.BlockSpec(memory_space=pltpu.SMEM)
    vmem = pl.BlockSpec(memory_space=pltpu.VMEM)
    params = pltpu.CompilerParams(vmem_limit_bytes=16 * 1024 * 1024)

    def array(*shape):
        return jax.ShapeDtypeStruct(shape, F32)

    faces = z_plan(nfield)[1]
    first, second = pl.pallas_call(
        pack_planes_kernel,
        out_shape=(array(faces, rows_len, cols_len),) * 2,
        in_specs=[pl.BlockSpec(memory_space=pl.ANY)] * 2,
        out_specs=(vmem, vmem),
        scratch_shapes=[pltpu.SemaphoreType.DMA((2 * nfield + 2,))],
        compiler_params=pltpu.CompilerParams(vmem_limit_bytes=60 * 1024 * 1024),
        name="pack_planes",
    )(fields, diffusivity)
    zlo, zhi = swap_pairs(first, second, "gz")
    kinds, outer = y_plan(nfield)
    send_lo, send_hi = pl.pallas_call(
        pack_rows_kernel,
        out_shape=(array(len(kinds), depth_len, cols_len),) * 2,
        in_specs=[vmem] * 2,
        out_specs=(vmem, vmem),
        compiler_params=params,
        name="pack_rows",
    )(fields, diffusivity)
    ylo, yhi = swap_rows(send_lo, send_hi, "gy")
    part_lo, part_hi = pl.pallas_call(
        pack_own_kernel,
        out_shape=(array(nfield + 1, rows_len, cols_len),) * 2,
        in_specs=[vmem] * 2,
        out_specs=(vmem,) * 2,
        compiler_params=params,
        cost_estimate=pl.CostEstimate(flops=10**7, bytes_accessed=4 * 10**6, transcendentals=0),
        name="pack_own",
    )(fields, diffusivity)
    extra = len(outer) + 2 * (nfield + 1) * W
    send_lo, send_hi, main_lo, main_hi = pl.pallas_call(
        pack_edges_kernel,
        out_shape=(array(extra, cols_len),) * 2 + (array(nfield + 1, rows_len, cols_len),) * 2,
        in_specs=[vmem] * 6,
        out_specs=(vmem,) * 4,
        compiler_params=params,
        name="pack_edges",
    )(fields, diffusivity, zlo, zhi, part_lo, part_hi)
    elo, ehi = swap_rows(send_lo, send_hi, "gy")
    pad = pltpu.VMEM(((nfield + 1) * planes, pitch, cols_len), F32)
    own_lo, own_hi = pl.pallas_call(
        pack_columns_kernel,
        out_shape=(array(nfield + 1, pitch, cols_len),) * 2,
        in_specs=[vmem] * 4 + [pl.BlockSpec(memory_space=pl.ANY)],
        out_specs=(vmem,) * 2,
        compiler_params=params,
        name="pack_columns",
    )(elo, ehi, main_lo, main_hi, ylo)
    odd = is_odd("gx")
    xlo, xhi = swap_pairs(jnp.where(odd, own_lo, own_hi), jnp.where(odd, own_hi, own_lo), "gx")
    *stepped, coefs = pl.pallas_call(
        first_step_kernel,
        out_shape=(array(planes, pitch, cols_len),) * nfield + (array(7, planes, pitch, cols_len),),
        in_specs=[smem] + [vmem] * 8,
        out_specs=(vmem,) * (nfield + 1),
        scratch_shapes=[pad],
        compiler_params=params,
        cost_estimate=pl.CostEstimate(flops=10**8, bytes_accessed=8 * 10**6, transcendentals=0),
        name="first_step",
    )(courant, fields, diffusivity, zlo, zhi, ylo, elo, yhi, ehi)
    count = lax.axis_size("gz")
    order = tile_perm[0, 0]
    per_owner = order.shape[0] // count
    state, tiles = pl.pallas_call(
        main_kernel,
        out_shape=(array(*fields.shape), array(order.shape[0], 4, cols_len)),
        in_specs=[smem] * 7 + [vmem] * (5 + nfield),
        out_specs=(pl.BlockSpec(memory_space=pl.ANY), vmem),
        scratch_shapes=[
            pltpu.VMEM((nfield * planes, pitch, cols_len), F32),
            pltpu.VMEM((planes, pitch, cols_len), F32),
            pltpu.VMEM((2, 2, 2, nfield, pitch, cols_len), F32),
            pltpu.VMEM((pitch, cols_len), F32),
            pltpu.VMEM((4, depth_len, rows_len, cols_len), F32),
            pltpu.VMEM((order.shape[0] * 4, cols_len), F32),
            pltpu.VMEM(fields.shape, F32),
            pltpu.VMEM((2, nfield, pitch, cols_len), F32),
            pltpu.SemaphoreType.DMA(()),
        ],
        compiler_params=pltpu.CompilerParams(vmem_limit_bytes=24 * 1024 * 1024),
        name="step_and_march",
    )(
        courant, tf_center, tf_sharp, tf_gain, tf_color, tile_mask[0, :, :, 0], order,
        xlo, xhi, own_lo, own_hi, coefs,
        *stepped,
    )
    grouped = tiles.reshape(count, per_owner * 4, cols_len)
    composed = compose(lax.all_to_all(grouped, "gz", split_axis=0, concat_axis=0, tiled=True))
    picture = composed.reshape(1, 1, per_owner, 4, cols_len)
    return (state, picture)


def solution(mesh):
    return jax.shard_map(
        shards,
        mesh=mesh,
        in_specs=(
            P(None, "gz", "gy", "gx"),
            P("gz", "gy", "gx"),
            P(),
            P(),
            P(),
            P(),
            P(),
            P("gz", None, "gy", "gx"),
            P("gy", "gx", None),
        ),
        out_specs=(P(None, "gz", "gy", "gx"), P("gy", "gx", "gz", None, None)),
        check_vma=False,
    )
```

```python
import jax
import jax.numpy as jnp
from jax import lax
from jax.experimental import pallas as pl
from jax.experimental.pallas import tpu as pltpu
from jax.sharding import PartitionSpec as P

LOG2E = 1.4426950408889634
W = 3
SUB = 8
F32 = jnp.float32


def reach(field, nfield):
    return W if field in (0, nfield) else W - 1


def tiles_of(first, last):
    return [min(start, last - SUB) for start in range(first, last, SUB)]


def z_plan(nfield):
    plan, at = [], 0
    for field in range(nfield + 1):
        plan.append((field, at, reach(field, nfield)))
        at += reach(field, nfield)
    return plan, at


def y_plan(nfield):
    kinds, edges = [], []
    for field in range(nfield + 1):
        wide = reach(field, nfield)
        for away in range(1, wide + 1):
            kinds.append((field, away))
            for k in range(1, wide - away + 1):
                edges.append((field, away, -k))
                edges.append((field, away, k))
    return kinds, edges


def pack_planes_kernel(fields_ref, kappa_ref, first_ref, second_ref, sems):
    nfield, depth_len = fields_ref.shape[:2]
    odd = lax.rem(lax.axis_index("gz"), 2)
    copies = []
    for field, at, wide in z_plan(nfield)[0]:
        source = kappa_ref if field == nfield else fields_ref.at[field]
        for place, target in ((1 - odd, first_ref), (odd, second_ref)):
            copies.append(
                pltpu.make_async_copy(
                    source.at[pl.ds(place * (depth_len - wide), wide)], target.at[pl.ds(at, wide)], sems.at[len(copies)]
                )
            )
    for copy in copies:
        copy.start()
    for copy in copies:
        copy.wait()


def present(axis):
    here = lax.axis_index(axis)
    return jnp.where(here > 0, 1.0, 0.0), jnp.where(here < lax.axis_size(axis) - 1, 1.0, 0.0)


def steps(count, most):
    return max(k for k in range(1, most + 1) if count % k == 0)


def source_plane(refs, field, z):
    fields_ref, kappa_ref, zlo_ref, zhi_ref = refs
    nfield, depth_len = fields_ref.shape[:2]
    _, at, wide = z_plan(nfield)[0][field]
    if z < 0:
        return zlo_ref.at[at + wide + z]
    if z >= depth_len:
        return zhi_ref.at[at + z - depth_len]
    return kappa_ref.at[z] if field == nfield else fields_ref.at[field, z]


def pack_rows_kernel(fields_ref, kappa_ref, lo_ref, hi_ref):
    nfield, depth_len, rows, lanes = fields_ref.shape
    flat_fields = fields_ref.reshape(nfield * depth_len * rows, lanes)
    flat_kappa = kappa_ref.reshape(depth_len * rows, lanes)
    for out_ref, top in ((lo_ref, True), (hi_ref, False)):
        for i, (field, away) in enumerate(y_plan(nfield)[0]):
            row = away - 1 if top else rows - away
            flat, base = (flat_kappa, 0) if field == nfield else (flat_fields, field * depth_len * rows)
            for z in range(0, depth_len, SUB):
                out_ref[i, z : z + SUB, :] = flat[pl.ds(base + z * rows + row, SUB, stride=rows), :]


def pack_edges_kernel(
    fields_ref, kappa_ref, zlo_ref, zhi_ref, ownlo_ref, ownhi_ref, lo_ref, hi_ref, mainlo_ref, mainhi_ref
):
    refs = (fields_ref, kappa_ref, zlo_ref, zhi_ref)
    nfield, depth_len, rows, lanes = fields_ref.shape
    lane = lax.broadcasted_iota(jnp.int32, (1, lanes), 1)
    edges = y_plan(nfield)[1]
    for i, (field, away, k) in enumerate(edges):
        plane = source_plane(refs, field, k if k < 0 else depth_len - 1 + k)
        lo_ref[i : i + 1, :] = plane[away - 1 : away, :]
        hi_ref[i : i + 1, :] = plane[rows - away : rows - away + 1, :]
    for field in range(nfield + 1):
        wide = reach(field, nfield)
        pair = (ownlo_ref[field], ownhi_ref[field])
        for z in list(range(-wide, 0)) + list(range(depth_len, depth_len + wide)):
            pair = take_columns(source_plane(refs, field, z)[...], z + W, lane, *pair)
        mainlo_ref[field], mainhi_ref[field] = pair
        for side in range(2):
            at = len(edges) + (side * (nfield + 1) + field) * W
            lo_ref[at : at + W, :] = pair[side][:W]
            hi_ref[at : at + W, :] = pair[side][rows - W :]


def assemble(refs, halo_rows, pad_ref, chosen):
    fields_ref, kappa_ref, zlo_ref, zhi_ref = refs
    nfield, depth_len, rows, lanes = fields_ref.shape
    planes, pitch = depth_len + 2 * W, rows + SUB
    halo = jnp.zeros((SUB, lanes), F32)

    @pl.loop(0, depth_len, unroll=steps(depth_len, 4))
    def _(z):
        for slot, field in enumerate(chosen):
            plane = slot * planes + W + z
            pad_ref[plane, :rows, :] = kappa_ref[z] if field == nfield else fields_ref[field, z]
            pad_ref[plane, rows:, :] = halo

    for slot, field in enumerate(chosen):
        _, at, wide = z_plan(nfield)[0][field]
        for k in range(W):
            below, above = slot * planes + W - 1 - k, slot * planes + W + depth_len + k
            if k < wide:
                pad_ref[below, :rows, :] = zlo_ref[at + wide - 1 - k]
                pad_ref[above, :rows, :] = zhi_ref[at + k]
            for plane in (below, above):
                if k >= wide:
                    pad_ref[plane, :rows, :] = jnp.zeros((rows, lanes), F32)
                pad_ref[plane, rows:, :] = halo
    pitch, lanes = pad_ref.shape[1:]
    flat = pad_ref.reshape(pad_ref.shape[0] * pitch, lanes)
    kinds, edges = y_plan(nfield)
    for low, (ref, edge_ref) in ((True, halo_rows[:2]), (False, halo_rows[2:])):
        flag = present("gy")[0 if low else 1]
        for i, (field, away) in enumerate(kinds):
            if field not in chosen:
                continue
            row = pitch - away if low else rows + away - 1
            for z in range(0, depth_len, SUB):
                flat[pl.ds((chosen.index(field) * planes + W + z) * pitch + row, SUB, stride=pitch), :] = (
                    ref[i, z : z + SUB, :] * flag
                )
        for i, (field, away, k) in enumerate(edges):
            if field not in chosen:
                continue
            row = pitch - away if low else rows + away - 1
            plane = chosen.index(field) * planes + W + (k if k < 0 else depth_len - 1 + k)
            pad_ref[plane, row : row + 1, :] = edge_ref[i : i + 1, :] * flag


def take_columns(value, zi, lane, low, high):
    lanes = value.shape[-1]
    mine = (lane >= W * zi) & (lane < W * zi + W)
    low = jnp.where(mine, pltpu.roll(value, W * zi, 1), low)
    high = jnp.where(mine, pltpu.roll(value, (W * zi + W) % lanes, 1), high)
    return low, high


def pack_own_kernel(fields_ref, kappa_ref, lo_ref, hi_ref):
    nfield, depth_len, rows, lanes = fields_ref.shape
    lane = lax.broadcasted_iota(jnp.int32, (1, lanes), 1)
    for field in range(nfield + 1):
        low = high = jnp.zeros((rows, lanes), F32)
        for z in range(depth_len):
            value = kappa_ref[z] if field == nfield else fields_ref[field, z]
            low, high = take_columns(value, z + W, lane, low, high)
        lo_ref[field] = low
        hi_ref[field] = high


def pack_columns_kernel(
    elo_ref, ehi_ref, mainlo_ref, mainhi_ref, rows_ref, lo_ref, hi_ref
):
    del rows_ref
    count, rows, lanes = mainlo_ref.shape
    low, high = present("gy")
    at = len(y_plan(count - 1)[1])
    for main_ref, out_ref in ((mainlo_ref, lo_ref), (mainhi_ref, hi_ref)):
        for field in range(count):
            out_ref[field, :rows, :] = main_ref[field]
            out_ref[field, rows:, :] = jnp.zeros((SUB, lanes), F32)
            out_ref[field, rows : rows + W, :] = ehi_ref[at : at + W, :] * high
            out_ref[field, rows + SUB - W :, :] = elo_ref[at : at + W, :] * low
            at += W


def stencil(u, coefs, ups, downs, speeds):
    total = (coefs[3] - (speeds[0] + speeds[1] + speeds[2])) * u
    for axis in range(3):
        k_up, k_down = coefs[axis]
        total = total + k_up * ups[axis] + (k_down + speeds[axis]) * downs[axis]
    return total


def weights(k, ups, downs):
    half = 0.5 * k
    coefs = [(half + 0.5 * ups[a], half + 0.5 * downs[a]) for a in range(3)]
    rest = 1.0
    for up, down in coefs:
        rest = rest - (up + down)
    return coefs + [rest]


def row_flags(shape, rows):
    r = lax.broadcasted_iota(jnp.int32, shape, 0)
    low, high = present("gy")
    return jnp.where(r < rows, 1.0, jnp.where(r < rows + SUB // 2, high, low))


def plane_flag(zi, depth_len):
    low, high = present("gz")
    return jnp.where(zi < W, low, jnp.where(zi >= W + depth_len, high, 1.0))


def first_step_kernel(
    courant_ref, fields_ref, kappa_ref, zlo_ref, zhi_ref, ylo_ref, elo_ref, yhi_ref, ehi_ref, *rest
):
    out_refs, pad_ref = rest[:-1], rest[-1]
    nfield, depth_len, rows, lanes = fields_ref.shape
    planes, pitch = depth_len + 2 * W, rows + SUB
    refs, halo_rows = (fields_ref, kappa_ref, zlo_ref, zhi_ref), (ylo_ref, elo_ref, yhi_ref, ehi_ref)
    assemble(refs, halo_rows, pad_ref, list(range(nfield + 1)))
    lane = lax.broadcasted_iota(jnp.int32, (pitch, lanes), 1)
    row_mask = row_flags((pitch, lanes), rows)
    speed = [[courant_ref[f, a] for a in range(3)] for f in range(nfield)]

    def around(field, zi):
        plane = field * planes + zi
        value = pad_ref[plane]
        x_up = jnp.where(lane == lanes - 1, value, pltpu.roll(value, lanes - 1, 1))
        x_down = jnp.where(lane == 0, value, pltpu.roll(value, 1, 1))
        ups = (pad_ref[plane + 1], pltpu.roll(value, pitch - 1, 0), x_up)
        downs = (pad_ref[plane - 1], pltpu.roll(value, 1, 0), x_down)
        return value, ups, downs

    @pl.loop(1, planes - 1, unroll=steps(planes - 2, 6))
    def _(zi):
        mask = row_mask * plane_flag(zi, depth_len)
        coefs = weights(*around(nfield, zi))
        for field in range(nfield):
            u, ups, downs = around(field, zi)
            out_refs[field][zi] = mask * stencil(u, coefs, ups, downs, speed[field])


def side_neighbours(near, own, is_left, lanes, col):
    first, second = (near, own) if is_left else (own, near)
    first_up = jnp.where(col == W - 1, pltpu.roll(second, W - 1, 1), pltpu.roll(first, lanes - 1, 1))
    first_down = pltpu.roll(first, 1, 1)
    second_up = pltpu.roll(second, lanes - 1, 1)
    second_down = jnp.where(col == 0, pltpu.roll(first, lanes - (W - 1), 1), pltpu.roll(second, 1, 1))
    pair = ((first_up, first_down), (second_up, second_down))
    return pair if is_left else (pair[1], pair[0])


def main_kernel(
    courant_ref, center_ref, sharp_ref, gain_ref, color_ref, mask_ref, order_ref,
    fields_ref, kappa_ref, zlo_ref, zhi_ref,
    ylo_ref, elo_ref, yhi_ref, ehi_ref, xlo_ref, xhi_ref, ownlo_ref, ownhi_ref, *rest,
):
    nfield, depth_len, rows, lanes = fields_ref.shape
    step_refs = rest[:nfield]
    count = lax.axis_size("gz")
    state_ref, out_refs = rest[nfield], rest[nfield + 1 : nfield + 1 + count]
    (
        kpad_ref, next_ref, last_ref, side_ref, edge_ref, base_ref,
        tile_ref, coef_ref, held_ref, flux_ref, sem,
    ) = rest[nfield + 1 + count :]
    nfield, depth_len, rows, lanes = state_ref.shape
    planes, pitch = depth_len + 2 * W, rows + SUB
    lane = lax.broadcasted_iota(jnp.int32, (pitch, lanes), 1)
    zi_of = lane // W
    col = lane - zi_of * W
    flag = present("gz") + present("gy") + present("gx")
    speed = [[courant_ref[f, a] for a in range(3)] for f in range(nfield)]
    row_mask = row_flags((pitch, lanes), rows)

    def along_y(value):
        return pltpu.roll(value, pitch - 1, 0), pltpu.roll(value, 1, 0)

    sides = ((xlo_ref, ownlo_ref, True, flag[4]), (xhi_ref, ownhi_ref, False, flag[5]))

    def block_of(level, side, block, field):
        if level == 0 or field == nfield:
            return sides[side][block][field]
        return side_ref[level - 1, side, block, field]

    def edges(level, field):
        left, right = block_of(level, 0, 0, field), block_of(level, 1, 0, field)
        edge_ref[level, field] = jnp.where(col == W - 1, left, pltpu.roll(right, 1, 1))

    def side_step(level, count):
        zmask = row_mask * jnp.where(
            zi_of < W, flag[0], jnp.where(zi_of >= W + depth_len, flag[1], 1.0)
        )
        for side, (_, _, is_left, present) in enumerate(sides):
            blocks = (0, 1) if level == 0 else (0,)

            def around(lvl, field):
                pair = [block_of(lvl, side, block, field) for block in (0, 1)]
                x = side_neighbours(pair[0], pair[1], is_left, lanes, col)
                found = []
                for block in blocks:
                    value = pair[block]
                    y_up, y_down = along_y(value)
                    ups = (pltpu.roll(value, lanes - W, 1), y_up, x[block][0])
                    downs = (pltpu.roll(value, W, 1), y_down, x[block][1])
                    found.append((value, ups, downs))
                return found

            coefs = [weights(*found) for found in around(0, nfield)]
            for field in range(count):
                for block, (u, ups, downs) in zip(blocks, around(level, field)):
                    value = stencil(u, coefs[block], ups, downs, speed[field])
                    side_ref[level, side, block, field] = value * (zmask * present if block == 0 else zmask)

    def along_x(value, zi, edge):
        n = value.shape[0]
        turned = pltpu.roll(edge, lax.rem(2 * lanes - 2 - W * zi, lanes), 1)
        up = jnp.where(lane[:n] == lanes - 1, turned, pltpu.roll(value, lanes - 1, 1))
        down = jnp.where(lane[:n] == 0, turned, pltpu.roll(value, 1, 1))
        return up, down

    def around(src_ref, level, field, zi, n, slot=None):
        plane = (field if slot is None else slot) * planes + zi
        whole = src_ref[plane]
        value = whole[:n]
        y_up, y_down = along_y(whole)
        x_up, x_down = along_x(value, zi, edge_ref[level, field, :n, :])
        return (
            value,
            (src_ref[plane + 1, :n, :], y_up[:n], x_up),
            (src_ref[plane - 1, :n, :], y_down[:n], x_down),
        )

    def step_value(src_ref, level, field, zi, n, coefs):
        u, ups, downs = around(src_ref, level, field, zi, n)
        return stencil(u, coefs, ups, downs, speed[field])

    def kept(zi, n):
        found = [coef_ref[i, zi, :n, :] for i in range(7)]
        return [found[0:2], found[2:4], found[4:6], found[6]]

    halo_rows = (ylo_ref, elo_ref, yhi_ref, ehi_ref)
    assemble((fields_ref, kappa_ref, zlo_ref, zhi_ref), halo_rows, kpad_ref, [nfield])
    edges(0, nfield)
    lane_mask = row_mask * jnp.where(
        zi_of < W, flag[0], jnp.where(zi_of >= W + depth_len, flag[1], 1.0)
    )
    k_left = 0.5 * (xlo_ref[nfield] + pltpu.roll(ownlo_ref[nfield], W - 1, 1))
    k_right = 0.5 * (xhi_ref[nfield] + pltpu.roll(ownhi_ref[nfield], lanes - (W - 1), 1))
    for field in range(nfield):
        left = (k_left + speed[field][2]) * (xlo_ref[field] - pltpu.roll(ownlo_ref[field], W - 1, 1))
        right = k_right * (xhi_ref[field] - pltpu.roll(ownhi_ref[field], lanes - (W - 1), 1))
        flux_ref[field] = lane_mask * jnp.where(col == W - 1, left, pltpu.roll(right, 1, 1))
    side_step(0, nfield)
    for field in range(nfield):
        edges(1, field)
    side_step(1, 1)
    edges(2, 0)

    @pl.loop(1, planes - 1, unroll=steps(planes - 2, 6))
    def _(zi):
        coefs = weights(*around(kpad_ref, 0, nfield, zi, pitch, 0))
        for i, value in enumerate(sum(coefs[:3], ()) + (coefs[3],)):
            coef_ref[i, zi] = value
        outer = (lane == 0) | (lane == lanes - 1)
        for field in range(nfield):
            turned = pltpu.roll(flux_ref[field], lax.rem(2 * lanes - 2 - W * zi, lanes), 1)
            next_ref[field * planes + zi] = step_refs[field][zi] + jnp.where(outer, turned, 0.0)

    @pl.loop(2, planes - 2, unroll=steps(planes - 4, 17))
    def _(zi):
        coefs = kept(zi, pitch)
        last_ref[zi] = step_value(next_ref, 1, 0, zi, pitch, coefs) * (row_mask * plane_flag(zi, depth_len))

    @pl.loop(0, depth_len, unroll=steps(depth_len, 8))
    def _(z):
        zi = z + W
        coefs = kept(zi, rows)
        s, ups, downs = around(last_ref, 2, 0, zi, rows)
        held_ref[0, z] = s
        g_z, g_y, g_x = [0.5 * (ups[a] - downs[a]) for a in range(3)]
        shade = 0.35 + 0.65 * jnp.abs(0.64 * g_z + 0.6 * g_y + 0.48 * g_x) * lax.rsqrt(
            g_z * g_z + g_y * g_y + g_x * g_x + 1.0
        )
        for field in range(1, nfield):
            value = step_value(next_ref, 1, field, zi, rows, coefs)
            held_ref[field, z] = value
            if field <= 3:
                base_ref[field, z] = shade * (0.5 + 0.5 * jnp.tanh(0.5 * value))
            if field == 4:
                base_ref[0, z] = 1.0 + 0.5 * jnp.tanh(value)

    keep = pltpu.make_async_copy(held_ref, state_ref, sem)
    keep.start()
    ntf = center_ref.shape[0]
    chunk = 4 if ntf % 4 == 0 else 1
    halves = rows // SUB

    @pl.loop(0, (ntf // chunk) * halves)
    def _(step):
        first = (step // halves) * chunk
        row = pl.multiple_of((step % halves) * SUB, SUB)
        shape = (SUB, lanes)
        mid = [jnp.full(shape, center_ref[first + j], jnp.float32) for j in range(chunk)]
        bend = [jnp.full(shape, sharp_ref[first + j] * -LOG2E, jnp.float32) for j in range(chunk)]
        dense = [jnp.full(shape, gain_ref[first + j] * -LOG2E, jnp.float32) for j in range(chunk)]
        passed = [jnp.ones(shape, jnp.float32)] * chunk
        total = [jnp.zeros(shape, jnp.float32)] * chunk
        acc = [[jnp.zeros(shape, jnp.float32)] * 3 for _ in range(chunk)]
        for z in range(depth_len):
            s = held_ref[0, z, pl.ds(row, SUB), :]
            modul = base_ref[0, z, pl.ds(row, SUB), :]
            base = [base_ref[k + 1, z, pl.ds(row, SUB), :] for k in range(3)]
            for j in range(chunk):
                diff = s - mid[j]
                total[j] = total[j] + modul * jnp.exp2(diff * diff * bend[j])
                after = jnp.exp2(total[j] * dense[j])
                weight = passed[j] - after
                passed[j] = after
                acc[j] = [acc[j][k] + weight * base[k] for k in range(3)]
        for j in range(chunk):
            start = ((first + j) * rows + row) * 4
            for k in range(3):
                tile_ref[pl.ds(start + k, SUB, stride=4), :] = acc[j][k] * color_ref[k, first + j]
            tile_ref[pl.ds(start + 3, SUB, stride=4), :] = 1.0 - passed[j]

    per_owner = out_refs[0].shape[0]
    for distance, out_ref in enumerate(out_refs):
        first_slot = lax.bitwise_xor(lax.axis_index("gz"), distance) * per_owner

        @pl.loop(0, per_owner, unroll=per_owner)
        def _(place):
            tile = order_ref[first_slot + place]
            cover = mask_ref[lax.div(tile, rows), lax.rem(tile, rows)].astype(F32)
            out_ref[place] = tile_ref[pl.ds(pl.multiple_of(tile * 4, 4), 4), :] * cover

    keep.wait()


def compose_kernel(*refs):
    part_refs, out_ref = refs[:-1], refs[-1]
    slabs, rows = len(part_refs), out_ref.shape[0]
    here = lax.axis_index("gz")

    @pl.loop(0, rows // 32, unroll=rows // 32)
    def _(step):
        def load(k):
            return [ref[pl.ds(step * 32 + k, 8, stride=4), :] for ref in part_refs]

        parts = [load(k) for k in range(4)]

        def slab_of(slab, k):
            distance = lax.bitwise_xor(here, slab)
            value = parts[k][0]
            for i in range(1, slabs):
                value = jnp.where(distance == i, parts[k][i], value)
            return value

        acc = [slab_of(0, k) for k in range(4)]
        for slab in range(1, slabs):
            clear = 1.0 - acc[3]
            acc = [acc[k] + clear * slab_of(slab, k) for k in range(4)]
        for k in range(4):
            out_ref[pl.ds(step * 32 + k, 8, stride=4), :] = acc[k]


def compose(parts):
    vmem = pl.BlockSpec(memory_space=pltpu.VMEM)
    return pl.pallas_call(
        compose_kernel,
        out_shape=jax.ShapeDtypeStruct(parts[0].shape, jnp.float32),
        in_specs=[vmem] * len(parts),
        out_specs=vmem,
        compiler_params=pltpu.CompilerParams(vmem_limit_bytes=16 * 1024 * 1024),
        name="compose",
    )(*parts)


def is_odd(axis):
    return lax.rem(lax.axis_index(axis), 2) == 1


def swap_pairs(first, second, axis):
    count = lax.axis_size(axis)
    came = []
    for start, message in ((0, first), (1, second)):
        pairs = []
        for i in range(start, count - 1, 2):
            pairs += [(i, i + 1), (i + 1, i)]
        came.append(lax.ppermute(message, axis, pairs) if pairs else jnp.zeros_like(message))
    odd = is_odd(axis)
    return jnp.where(odd, came[0], came[1]), jnp.where(odd, came[1], came[0])


def swap_rows(low, high, axis):
    odd = is_odd(axis)
    first = jnp.where(odd, low, high)
    if lax.axis_size(axis) == 2:
        came = lax.ppermute(first, axis, [(0, 1), (1, 0)])
        return came, came
    return swap_pairs(first, jnp.where(odd, high, low), axis)


def shards(
    fields, diffusivity, courant, tf_center, tf_sharp, tf_gain, tf_color, tile_mask, tile_perm
):
    nfield, depth_len, rows_len, cols_len = fields.shape
    planes, pitch = depth_len + 2 * W, rows_len + SUB
    smem = pl.BlockSpec(memory_space=pltpu.SMEM)
    vmem = pl.BlockSpec(memory_space=pltpu.VMEM)
    params = pltpu.CompilerParams(vmem_limit_bytes=16 * 1024 * 1024)

    def array(*shape):
        return jax.ShapeDtypeStruct(shape, F32)

    faces = z_plan(nfield)[1]
    first, second = pl.pallas_call(
        pack_planes_kernel,
        out_shape=(array(faces, rows_len, cols_len),) * 2,
        in_specs=[pl.BlockSpec(memory_space=pl.ANY)] * 2,
        out_specs=(vmem, vmem),
        scratch_shapes=[pltpu.SemaphoreType.DMA((2 * nfield + 2,))],
        compiler_params=pltpu.CompilerParams(vmem_limit_bytes=60 * 1024 * 1024),
        name="pack_planes",
    )(fields, diffusivity)
    zlo, zhi = swap_pairs(first, second, "gz")
    kinds, outer = y_plan(nfield)
    send_lo, send_hi = pl.pallas_call(
        pack_rows_kernel,
        out_shape=(array(len(kinds), depth_len, cols_len),) * 2,
        in_specs=[vmem] * 2,
        out_specs=(vmem, vmem),
        compiler_params=params,
        name="pack_rows",
    )(fields, diffusivity)
    ylo, yhi = swap_rows(send_lo, send_hi, "gy")
    part_lo, part_hi = pl.pallas_call(
        pack_own_kernel,
        out_shape=(array(nfield + 1, rows_len, cols_len),) * 2,
        in_specs=[vmem] * 2,
        out_specs=(vmem,) * 2,
        compiler_params=params,
        cost_estimate=pl.CostEstimate(flops=10**7, bytes_accessed=4 * 10**6, transcendentals=0),
        name="pack_own",
    )(fields, diffusivity)
    extra = len(outer) + 2 * (nfield + 1) * W
    send_lo, send_hi, main_lo, main_hi = pl.pallas_call(
        pack_edges_kernel,
        out_shape=(array(extra, cols_len),) * 2 + (array(nfield + 1, rows_len, cols_len),) * 2,
        in_specs=[vmem] * 6,
        out_specs=(vmem,) * 4,
        compiler_params=params,
        name="pack_edges",
    )(fields, diffusivity, zlo, zhi, part_lo, part_hi)
    elo, ehi = swap_rows(send_lo, send_hi, "gy")
    pad = pltpu.VMEM(((nfield + 1) * planes, pitch, cols_len), F32)
    own_lo, own_hi = pl.pallas_call(
        pack_columns_kernel,
        out_shape=(array(nfield + 1, pitch, cols_len),) * 2,
        in_specs=[vmem] * 4 + [pl.BlockSpec(memory_space=pl.ANY)],
        out_specs=(vmem,) * 2,
        compiler_params=params,
        name="pack_columns",
    )(elo, ehi, main_lo, main_hi, ylo)
    odd = is_odd("gx")
    xlo, xhi = swap_pairs(jnp.where(odd, own_lo, own_hi), jnp.where(odd, own_hi, own_lo), "gx")
    stepped = pl.pallas_call(
        first_step_kernel,
        out_shape=(array(planes, pitch, cols_len),) * nfield,
        in_specs=[smem] + [vmem] * 8,
        out_specs=(vmem,) * nfield,
        scratch_shapes=[pad],
        compiler_params=params,
        cost_estimate=pl.CostEstimate(flops=10**8, bytes_accessed=8 * 10**6, transcendentals=0),
        name="first_step",
    )(courant, fields, diffusivity, zlo, zhi, ylo, elo, yhi, ehi)
    count = lax.axis_size("gz")
    order = tile_perm[0, 0]
    per_owner = order.shape[0] // count
    state, *blocks = pl.pallas_call(
        main_kernel,
        out_shape=(array(*fields.shape),) + (array(per_owner, 4, cols_len),) * count,
        in_specs=[smem] * 7 + [vmem] * (12 + nfield),
        out_specs=(pl.BlockSpec(memory_space=pl.ANY),) + (vmem,) * count,
        scratch_shapes=[
            pltpu.VMEM((planes, pitch, cols_len), F32),
            pltpu.VMEM((nfield * planes, pitch, cols_len), F32),
            pltpu.VMEM((planes, pitch, cols_len), F32),
            pltpu.VMEM((2, 2, 2, nfield, pitch, cols_len), F32),
            pltpu.VMEM((3, nfield + 1, pitch, cols_len), F32),
            pltpu.VMEM((4, depth_len, rows_len, cols_len), F32),
            pltpu.VMEM((order.shape[0] * 4, cols_len), F32),
            pltpu.VMEM((7, planes, pitch, cols_len), F32),
            pltpu.VMEM(fields.shape, F32),
            pltpu.VMEM((nfield, pitch, cols_len), F32),
            pltpu.SemaphoreType.DMA(()),
        ],
        compiler_params=pltpu.CompilerParams(vmem_limit_bytes=24 * 1024 * 1024),
        name="step_and_march",
    )(
        courant, tf_center, tf_sharp, tf_gain, tf_color, tile_mask[0, :, :, 0], order,
        fields, diffusivity, zlo, zhi, ylo, elo, yhi, ehi, xlo, xhi, own_lo, own_hi,
        *stepped,
    )
    parts = [blocks[0]]
    for distance in range(1, count):
        parts.append(lax.ppermute(blocks[distance], "gz", [(i, i ^ distance) for i in range(count)]))
    composed = compose([part.reshape(per_owner * 4, cols_len) for part in parts])
    picture = composed.reshape(1, 1, per_owner, 4, cols_len)
    return (state, picture)


def solution(mesh):
    return jax.shard_map(
        shards,
        mesh=mesh,
        in_specs=(
            P(None, "gz", "gy", "gx"),
            P("gz", "gy", "gx"),
            P(),
            P(),
            P(),
            P(),
            P(),
            P("gz", None, "gy", "gx"),
            P("gy", "gx", None),
        ),
        out_specs=(P(None, "gz", "gy", "gx"), P("gy", "gx", "gz", None, None)),
        check_vma=False,
    )
```

```python
import jax
import jax.numpy as jnp
from jax import lax
from jax.experimental import pallas as pl
from jax.experimental.pallas import tpu as pltpu
from jax.sharding import PartitionSpec as P

LOG2E = 1.4426950408889634
W = 3
SUB = 8
F32 = jnp.float32


def reach(field, nfield):
    return W if field in (0, nfield) else W - 1


def tiles_of(first, last):
    return [min(start, last - SUB) for start in range(first, last, SUB)]


def z_plan(nfield):
    plan, at = [], 0
    for field in range(nfield + 1):
        plan.append((field, at, reach(field, nfield)))
        at += reach(field, nfield)
    return plan, at


def y_plan(nfield):
    kinds, edges = [], []
    for field in range(nfield + 1):
        wide = reach(field, nfield)
        for away in range(1, wide + 1):
            kinds.append((field, away))
            for k in range(1, wide - away + 1):
                edges.append((field, away, -k))
                edges.append((field, away, k))
    return kinds, edges


def pack_planes_kernel(fields_ref, kappa_ref, first_ref, second_ref, sems):
    nfield, depth_len = fields_ref.shape[:2]
    odd = lax.rem(lax.axis_index("gz"), 2)
    copies = []
    for field, at, wide in z_plan(nfield)[0]:
        source = kappa_ref if field == nfield else fields_ref.at[field]
        for place, target in ((1 - odd, first_ref), (odd, second_ref)):
            copies.append(
                pltpu.make_async_copy(
                    source.at[pl.ds(place * (depth_len - wide), wide)], target.at[pl.ds(at, wide)], sems.at[len(copies)]
                )
            )
    for copy in copies:
        copy.start()
    for copy in copies:
        copy.wait()


def present(axis):
    here = lax.axis_index(axis)
    return jnp.where(here > 0, 1.0, 0.0), jnp.where(here < lax.axis_size(axis) - 1, 1.0, 0.0)


def steps(count, most):
    return max(k for k in range(1, most + 1) if count % k == 0)


def source_plane(refs, field, z):
    fields_ref, kappa_ref, zlo_ref, zhi_ref = refs
    nfield, depth_len = fields_ref.shape[:2]
    _, at, wide = z_plan(nfield)[0][field]
    if z < 0:
        return zlo_ref.at[at + wide + z]
    if z >= depth_len:
        return zhi_ref.at[at + z - depth_len]
    return kappa_ref.at[z] if field == nfield else fields_ref.at[field, z]


def pack_rows_kernel(fields_ref, kappa_ref, lo_ref, hi_ref):
    nfield, depth_len, rows, lanes = fields_ref.shape
    flat_fields = fields_ref.reshape(nfield * depth_len * rows, lanes)
    flat_kappa = kappa_ref.reshape(depth_len * rows, lanes)
    for out_ref, top in ((lo_ref, True), (hi_ref, False)):
        for i, (field, away) in enumerate(y_plan(nfield)[0]):
            row = away - 1 if top else rows - away
            flat, base = (flat_kappa, 0) if field == nfield else (flat_fields, field * depth_len * rows)
            for z in range(0, depth_len, SUB):
                out_ref[i, z : z + SUB, :] = flat[pl.ds(base + z * rows + row, SUB, stride=rows), :]


def pack_edges_kernel(
    fields_ref, kappa_ref, zlo_ref, zhi_ref, ownlo_ref, ownhi_ref, lo_ref, hi_ref, mainlo_ref, mainhi_ref
):
    refs = (fields_ref, kappa_ref, zlo_ref, zhi_ref)
    nfield, depth_len, rows, lanes = fields_ref.shape
    lane = lax.broadcasted_iota(jnp.int32, (1, lanes), 1)
    edges = y_plan(nfield)[1]
    for i, (field, away, k) in enumerate(edges):
        plane = source_plane(refs, field, k if k < 0 else depth_len - 1 + k)
        lo_ref[i : i + 1, :] = plane[away - 1 : away, :]
        hi_ref[i : i + 1, :] = plane[rows - away : rows - away + 1, :]
    for field in range(nfield + 1):
        wide = reach(field, nfield)
        pair = (ownlo_ref[field], ownhi_ref[field])
        for z in list(range(-wide, 0)) + list(range(depth_len, depth_len + wide)):
            pair = take_columns(source_plane(refs, field, z)[...], z + W, lane, *pair)
        mainlo_ref[field], mainhi_ref[field] = pair
        for side in range(2):
            at = len(edges) + (side * (nfield + 1) + field) * W
            lo_ref[at : at + W, :] = pair[side][:W]
            hi_ref[at : at + W, :] = pair[side][rows - W :]


def assemble(refs, halo_rows, pad_ref, chosen):
    fields_ref, kappa_ref, zlo_ref, zhi_ref = refs
    nfield, depth_len, rows, lanes = fields_ref.shape
    planes, pitch = depth_len + 2 * W, rows + SUB
    halo = jnp.zeros((SUB, lanes), F32)

    @pl.loop(0, depth_len, unroll=steps(depth_len, 4))
    def _(z):
        for slot, field in enumerate(chosen):
            plane = slot * planes + W + z
            pad_ref[plane, :rows, :] = kappa_ref[z] if field == nfield else fields_ref[field, z]
            pad_ref[plane, rows:, :] = halo

    for slot, field in enumerate(chosen):
        _, at, wide = z_plan(nfield)[0][field]
        for k in range(W):
            below, above = slot * planes + W - 1 - k, slot * planes + W + depth_len + k
            if k < wide:
                pad_ref[below, :rows, :] = zlo_ref[at + wide - 1 - k]
                pad_ref[above, :rows, :] = zhi_ref[at + k]
            for plane in (below, above):
                if k >= wide:
                    pad_ref[plane, :rows, :] = jnp.zeros((rows, lanes), F32)
                pad_ref[plane, rows:, :] = halo
    pitch, lanes = pad_ref.shape[1:]
    flat = pad_ref.reshape(pad_ref.shape[0] * pitch, lanes)
    kinds, edges = y_plan(nfield)
    for low, (ref, edge_ref) in ((True, halo_rows[:2]), (False, halo_rows[2:])):
        flag = present("gy")[0 if low else 1]
        for i, (field, away) in enumerate(kinds):
            if field not in chosen:
                continue
            row = pitch - away if low else rows + away - 1
            for z in range(0, depth_len, SUB):
                flat[pl.ds((chosen.index(field) * planes + W + z) * pitch + row, SUB, stride=pitch), :] = (
                    ref[i, z : z + SUB, :] * flag
                )
        for i, (field, away, k) in enumerate(edges):
            if field not in chosen:
                continue
            row = pitch - away if low else rows + away - 1
            plane = chosen.index(field) * planes + W + (k if k < 0 else depth_len - 1 + k)
            pad_ref[plane, row : row + 1, :] = edge_ref[i : i + 1, :] * flag


def take_columns(value, zi, lane, low, high):
    lanes = value.shape[-1]
    mine = (lane >= W * zi) & (lane < W * zi + W)
    low = jnp.where(mine, pltpu.roll(value, W * zi, 1), low)
    high = jnp.where(mine, pltpu.roll(value, (W * zi + W) % lanes, 1), high)
    return low, high


def pack_own_kernel(fields_ref, kappa_ref, lo_ref, hi_ref):
    nfield, depth_len, rows, lanes = fields_ref.shape
    lane = lax.broadcasted_iota(jnp.int32, (1, lanes), 1)
    for field in range(nfield + 1):
        low = high = jnp.zeros((rows, lanes), F32)
        for z in range(depth_len):
            value = kappa_ref[z] if field == nfield else fields_ref[field, z]
            low, high = take_columns(value, z + W, lane, low, high)
        lo_ref[field] = low
        hi_ref[field] = high


def pack_columns_kernel(
    elo_ref, ehi_ref, mainlo_ref, mainhi_ref, rows_ref, lo_ref, hi_ref
):
    del rows_ref
    count, rows, lanes = mainlo_ref.shape
    low, high = present("gy")
    at = len(y_plan(count - 1)[1])
    for main_ref, out_ref in ((mainlo_ref, lo_ref), (mainhi_ref, hi_ref)):
        for field in range(count):
            out_ref[field, :rows, :] = main_ref[field]
            out_ref[field, rows:, :] = jnp.zeros((SUB, lanes), F32)
            out_ref[field, rows : rows + W, :] = ehi_ref[at : at + W, :] * high
            out_ref[field, rows + SUB - W :, :] = elo_ref[at : at + W, :] * low
            at += W


def stencil(u, coefs, ups, downs, speeds):
    total = (coefs[3] - (speeds[0] + speeds[1] + speeds[2])) * u
    for axis in range(3):
        k_up, k_down = coefs[axis]
        total = total + k_up * ups[axis] + (k_down + speeds[axis]) * downs[axis]
    return total


def weights(k, ups, downs):
    half = 0.5 * k
    coefs = [(half + 0.5 * ups[a], half + 0.5 * downs[a]) for a in range(3)]
    rest = 1.0
    for up, down in coefs:
        rest = rest - (up + down)
    return coefs + [rest]


def row_flags(shape, rows):
    r = lax.broadcasted_iota(jnp.int32, shape, 0)
    low, high = present("gy")
    return jnp.where(r < rows, 1.0, jnp.where(r < rows + SUB // 2, high, low))


def plane_flag(zi, depth_len):
    low, high = present("gz")
    return jnp.where(zi < W, low, jnp.where(zi >= W + depth_len, high, 1.0))


def first_step_kernel(
    courant_ref, fields_ref, kappa_ref, zlo_ref, zhi_ref, ylo_ref, elo_ref, yhi_ref, ehi_ref, *rest
):
    out_refs, pad_ref = rest[:-1], rest[-1]
    nfield, depth_len, rows, lanes = fields_ref.shape
    planes, pitch = depth_len + 2 * W, rows + SUB
    refs, halo_rows = (fields_ref, kappa_ref, zlo_ref, zhi_ref), (ylo_ref, elo_ref, yhi_ref, ehi_ref)
    assemble(refs, halo_rows, pad_ref, list(range(nfield + 1)))
    lane = lax.broadcasted_iota(jnp.int32, (pitch, lanes), 1)
    row_mask = row_flags((pitch, lanes), rows)
    speed = [[courant_ref[f, a] for a in range(3)] for f in range(nfield)]

    def around(field, zi):
        plane = field * planes + zi
        value = pad_ref[plane]
        x_up = jnp.where(lane == lanes - 1, value, pltpu.roll(value, lanes - 1, 1))
        x_down = jnp.where(lane == 0, value, pltpu.roll(value, 1, 1))
        ups = (pad_ref[plane + 1], pltpu.roll(value, pitch - 1, 0), x_up)
        downs = (pad_ref[plane - 1], pltpu.roll(value, 1, 0), x_down)
        return value, ups, downs

    @pl.loop(1, planes - 1, unroll=steps(planes - 2, 6))
    def _(zi):
        mask = row_mask * plane_flag(zi, depth_len)
        coefs = weights(*around(nfield, zi))
        for field in range(nfield):
            u, ups, downs = around(field, zi)
            out_refs[field][zi] = mask * stencil(u, coefs, ups, downs, speed[field])


def side_neighbours(near, own, is_left, lanes, col):
    first, second = (near, own) if is_left else (own, near)
    first_up = jnp.where(col == W - 1, pltpu.roll(second, W - 1, 1), pltpu.roll(first, lanes - 1, 1))
    first_down = pltpu.roll(first, 1, 1)
    second_up = pltpu.roll(second, lanes - 1, 1)
    second_down = jnp.where(col == 0, pltpu.roll(first, lanes - (W - 1), 1), pltpu.roll(second, 1, 1))
    pair = ((first_up, first_down), (second_up, second_down))
    return pair if is_left else (pair[1], pair[0])


def main_kernel(
    courant_ref, center_ref, sharp_ref, gain_ref, color_ref, mask_ref, order_ref,
    fields_ref, kappa_ref, zlo_ref, zhi_ref,
    ylo_ref, elo_ref, yhi_ref, ehi_ref, xlo_ref, xhi_ref, ownlo_ref, ownhi_ref, *rest,
):
    nfield, depth_len, rows, lanes = fields_ref.shape
    step_refs = rest[:nfield]
    count = lax.axis_size("gz")
    state_ref, out_refs = rest[nfield], rest[nfield + 1 : nfield + 1 + count]
    (
        kpad_ref, next_ref, last_ref, side_ref, edge_ref, base_ref,
        tile_ref, coef_ref, held_ref, flux_ref, sem,
    ) = rest[nfield + 1 + count :]
    nfield, depth_len, rows, lanes = state_ref.shape
    planes, pitch = depth_len + 2 * W, rows + SUB
    lane = lax.broadcasted_iota(jnp.int32, (pitch, lanes), 1)
    zi_of = lane // W
    col = lane - zi_of * W
    flag = present("gz") + present("gy") + present("gx")
    speed = [[courant_ref[f, a] for a in range(3)] for f in range(nfield)]
    row_mask = row_flags((pitch, lanes), rows)

    def along_y(value):
        return pltpu.roll(value, pitch - 1, 0), pltpu.roll(value, 1, 0)

    sides = ((xlo_ref, ownlo_ref, True, flag[4]), (xhi_ref, ownhi_ref, False, flag[5]))

    def block_of(level, side, block, field):
        if level == 0 or field == nfield:
            return sides[side][block][field]
        return side_ref[level - 1, side, block, field]

    def edges(level, field):
        left, right = block_of(level, 0, 0, field), block_of(level, 1, 0, field)
        edge_ref[level, field] = jnp.where(col == W - 1, left, pltpu.roll(right, 1, 1))

    def side_step(level, count):
        zmask = row_mask * jnp.where(
            zi_of < W, flag[0], jnp.where(zi_of >= W + depth_len, flag[1], 1.0)
        )
        for side, (_, _, is_left, present) in enumerate(sides):
            blocks = (0, 1) if level == 0 else (0,)

            def around(lvl, field):
                pair = [block_of(lvl, side, block, field) for block in (0, 1)]
                x = side_neighbours(pair[0], pair[1], is_left, lanes, col)
                found = []
                for block in blocks:
                    value = pair[block]
                    y_up, y_down = along_y(value)
                    ups = (pltpu.roll(value, lanes - W, 1), y_up, x[block][0])
                    downs = (pltpu.roll(value, W, 1), y_down, x[block][1])
                    found.append((value, ups, downs))
                return found

            coefs = [weights(*found) for found in around(0, nfield)]
            for field in range(count):
                for block, (u, ups, downs) in zip(blocks, around(level, field)):
                    value = stencil(u, coefs[block], ups, downs, speed[field])
                    side_ref[level, side, block, field] = value * (zmask * present if block == 0 else zmask)

    def along_x(value, zi, edge):
        n = value.shape[0]
        turned = pltpu.roll(edge, lax.rem(2 * lanes - 2 - W * zi, lanes), 1)
        up = jnp.where(lane[:n] == lanes - 1, turned, pltpu.roll(value, lanes - 1, 1))
        down = jnp.where(lane[:n] == 0, turned, pltpu.roll(value, 1, 1))
        return up, down

    def around(src_ref, level, field, zi, n, slot=None):
        plane = (field if slot is None else slot) * planes + zi
        whole = src_ref[plane]
        value = whole[:n]
        y_up, y_down = along_y(whole)
        x_up, x_down = along_x(value, zi, edge_ref[level, field, :n, :])
        return (
            value,
            (src_ref[plane + 1, :n, :], y_up[:n], x_up),
            (src_ref[plane - 1, :n, :], y_down[:n], x_down),
        )

    def step_value(src_ref, level, field, zi, n, coefs):
        u, ups, downs = around(src_ref, level, field, zi, n)
        return stencil(u, coefs, ups, downs, speed[field])

    def kept(zi, n):
        found = [coef_ref[i, zi, :n, :] for i in range(7)]
        return [found[0:2], found[2:4], found[4:6], found[6]]

    halo_rows = (ylo_ref, elo_ref, yhi_ref, ehi_ref)
    assemble((fields_ref, kappa_ref, zlo_ref, zhi_ref), halo_rows, kpad_ref, [nfield])
    edges(0, nfield)
    lane_mask = row_mask * jnp.where(
        zi_of < W, flag[0], jnp.where(zi_of >= W + depth_len, flag[1], 1.0)
    )
    k_left = 0.5 * (xlo_ref[nfield] + pltpu.roll(ownlo_ref[nfield], W - 1, 1))
    k_right = 0.5 * (xhi_ref[nfield] + pltpu.roll(ownhi_ref[nfield], lanes - (W - 1), 1))
    for field in range(nfield):
        left = (k_left + speed[field][2]) * (xlo_ref[field] - pltpu.roll(ownlo_ref[field], W - 1, 1))
        right = k_right * (xhi_ref[field] - pltpu.roll(ownhi_ref[field], lanes - (W - 1), 1))
        flux_ref[field] = lane_mask * jnp.where(col == W - 1, left, pltpu.roll(right, 1, 1))
    side_step(0, nfield)
    for field in range(nfield):
        edges(1, field)
    side_step(1, 1)
    edges(2, 0)

    @pl.loop(1, planes - 1, unroll=steps(planes - 2, 6))
    def _(zi):
        coefs = weights(*around(kpad_ref, 0, nfield, zi, pitch, 0))
        for i, value in enumerate(sum(coefs[:3], ()) + (coefs[3],)):
            coef_ref[i, zi] = value
        outer = (lane == 0) | (lane == lanes - 1)
        for field in range(nfield):
            turned = pltpu.roll(flux_ref[field], lax.rem(2 * lanes - 2 - W * zi, lanes), 1)
            next_ref[field * planes + zi] = step_refs[field][zi] + jnp.where(outer, turned, 0.0)

    @pl.loop(2, planes - 2, unroll=steps(planes - 4, 17))
    def _(zi):
        coefs = kept(zi, pitch)
        last_ref[zi] = step_value(next_ref, 1, 0, zi, pitch, coefs) * (row_mask * plane_flag(zi, depth_len))

    @pl.loop(0, depth_len, unroll=steps(depth_len, 8))
    def _(z):
        zi = z + W
        coefs = kept(zi, rows)
        s, ups, downs = around(last_ref, 2, 0, zi, rows)
        held_ref[0, z] = s
        g_z, g_y, g_x = [0.5 * (ups[a] - downs[a]) for a in range(3)]
        shade = 0.35 + 0.65 * jnp.abs(0.64 * g_z + 0.6 * g_y + 0.48 * g_x) * lax.rsqrt(
            g_z * g_z + g_y * g_y + g_x * g_x + 1.0
        )
        for field in range(1, nfield):
            value = step_value(next_ref, 1, field, zi, rows, coefs)
            held_ref[field, z] = value
            if field <= 3:
                base_ref[field, z] = shade * (0.5 + 0.5 * jnp.tanh(0.5 * value))
            if field == 4:
                base_ref[0, z] = 1.0 + 0.5 * jnp.tanh(value)

    keep = pltpu.make_async_copy(held_ref, state_ref, sem)
    keep.start()
    ntf = center_ref.shape[0]
    chunk = 4 if ntf % 4 == 0 else 1
    halves = rows // SUB

    @pl.loop(0, (ntf // chunk) * halves)
    def _(step):
        first = (step // halves) * chunk
        row = pl.multiple_of((step % halves) * SUB, SUB)
        shape = (SUB, lanes)
        mid = [jnp.full(shape, center_ref[first + j], jnp.float32) for j in range(chunk)]
        bend = [jnp.full(shape, sharp_ref[first + j] * -LOG2E, jnp.float32) for j in range(chunk)]
        dense = [jnp.full(shape, gain_ref[first + j] * -LOG2E, jnp.float32) for j in range(chunk)]
        passed = [jnp.ones(shape, jnp.float32)] * chunk
        total = [jnp.zeros(shape, jnp.float32)] * chunk
        acc = [[jnp.zeros(shape, jnp.float32)] * 3 for _ in range(chunk)]
        for z in range(depth_len):
            s = held_ref[0, z, pl.ds(row, SUB), :]
            modul = base_ref[0, z, pl.ds(row, SUB), :]
            base = [base_ref[k + 1, z, pl.ds(row, SUB), :] for k in range(3)]
            for j in range(chunk):
                diff = s - mid[j]
                total[j] = total[j] + modul * jnp.exp2(diff * diff * bend[j])
                after = jnp.exp2(total[j] * dense[j])
                weight = passed[j] - after
                passed[j] = after
                acc[j] = [acc[j][k] + weight * base[k] for k in range(3)]
        for j in range(chunk):
            start = ((first + j) * rows + row) * 4
            for k in range(3):
                tile_ref[pl.ds(start + k, SUB, stride=4), :] = acc[j][k] * color_ref[k, first + j]
            tile_ref[pl.ds(start + 3, SUB, stride=4), :] = 1.0 - passed[j]

    per_owner = out_refs[0].shape[0]
    for distance, out_ref in enumerate(out_refs):
        first_slot = lax.bitwise_xor(lax.axis_index("gz"), distance) * per_owner

        @pl.loop(0, per_owner, unroll=per_owner)
        def _(place):
            tile = order_ref[first_slot + place]
            cover = mask_ref[lax.div(tile, rows), lax.rem(tile, rows)].astype(F32)
            out_ref[place] = tile_ref[pl.ds(pl.multiple_of(tile * 4, 4), 4), :] * cover

    keep.wait()


def compose_kernel(*refs):
    part_refs, out_ref = refs[:1] + refs[-2:0:-1], refs[-1]
    slabs, rows = len(part_refs), out_ref.shape[0]
    here = lax.axis_index("gz")

    @pl.loop(0, rows // 32, unroll=rows // 32)
    def _(step):
        def load(k):
            return [ref[pl.ds(step * 32 + k, 8, stride=4), :] for ref in part_refs]

        parts = [load(k) for k in range(4)]

        def slab_of(slab, k):
            distance = lax.bitwise_xor(here, slab)
            value = parts[k][0]
            for i in range(1, slabs):
                value = jnp.where(distance == i, parts[k][i], value)
            return value

        acc = [slab_of(0, k) for k in range(4)]
        for slab in range(1, slabs):
            clear = 1.0 - acc[3]
            acc = [acc[k] + clear * slab_of(slab, k) for k in range(4)]
        for k in range(4):
            out_ref[pl.ds(step * 32 + k, 8, stride=4), :] = acc[k]


def compose(parts):
    vmem = pl.BlockSpec(memory_space=pltpu.VMEM)
    return pl.pallas_call(
        compose_kernel,
        out_shape=jax.ShapeDtypeStruct(parts[0].shape, jnp.float32),
        in_specs=[vmem] * len(parts),
        out_specs=vmem,
        compiler_params=pltpu.CompilerParams(vmem_limit_bytes=16 * 1024 * 1024),
        name="compose",
    )(*parts)


def is_odd(axis):
    return lax.rem(lax.axis_index(axis), 2) == 1


def swap_pairs(first, second, axis):
    count = lax.axis_size(axis)
    came = []
    for start, message in ((0, first), (1, second)):
        pairs = []
        for i in range(start, count - 1, 2):
            pairs += [(i, i + 1), (i + 1, i)]
        came.append(lax.ppermute(message, axis, pairs) if pairs else jnp.zeros_like(message))
    odd = is_odd(axis)
    return jnp.where(odd, came[0], came[1]), jnp.where(odd, came[1], came[0])


def swap_rows(low, high, axis):
    odd = is_odd(axis)
    first = jnp.where(odd, low, high)
    if lax.axis_size(axis) == 2:
        came = lax.ppermute(first, axis, [(0, 1), (1, 0)])
        return came, came
    return swap_pairs(first, jnp.where(odd, high, low), axis)


def shards(
    fields, diffusivity, courant, tf_center, tf_sharp, tf_gain, tf_color, tile_mask, tile_perm
):
    nfield, depth_len, rows_len, cols_len = fields.shape
    planes, pitch = depth_len + 2 * W, rows_len + SUB
    smem = pl.BlockSpec(memory_space=pltpu.SMEM)
    vmem = pl.BlockSpec(memory_space=pltpu.VMEM)
    params = pltpu.CompilerParams(vmem_limit_bytes=16 * 1024 * 1024)

    def array(*shape):
        return jax.ShapeDtypeStruct(shape, F32)

    faces = z_plan(nfield)[1]
    first, second = pl.pallas_call(
        pack_planes_kernel,
        out_shape=(array(faces, rows_len, cols_len),) * 2,
        in_specs=[pl.BlockSpec(memory_space=pl.ANY)] * 2,
        out_specs=(vmem, vmem),
        scratch_shapes=[pltpu.SemaphoreType.DMA((2 * nfield + 2,))],
        compiler_params=pltpu.CompilerParams(vmem_limit_bytes=60 * 1024 * 1024),
        name="pack_planes",
    )(fields, diffusivity)
    zlo, zhi = swap_pairs(first, second, "gz")
    kinds, outer = y_plan(nfield)
    send_lo, send_hi = pl.pallas_call(
        pack_rows_kernel,
        out_shape=(array(len(kinds), depth_len, cols_len),) * 2,
        in_specs=[vmem] * 2,
        out_specs=(vmem, vmem),
        compiler_params=params,
        name="pack_rows",
    )(fields, diffusivity)
    ylo, yhi = swap_rows(send_lo, send_hi, "gy")
    part_lo, part_hi = pl.pallas_call(
        pack_own_kernel,
        out_shape=(array(nfield + 1, rows_len, cols_len),) * 2,
        in_specs=[vmem] * 2,
        out_specs=(vmem,) * 2,
        compiler_params=params,
        cost_estimate=pl.CostEstimate(flops=10**7, bytes_accessed=4 * 10**6, transcendentals=0),
        name="pack_own",
    )(fields, diffusivity)
    extra = len(outer) + 2 * (nfield + 1) * W
    send_lo, send_hi, main_lo, main_hi = pl.pallas_call(
        pack_edges_kernel,
        out_shape=(array(extra, cols_len),) * 2 + (array(nfield + 1, rows_len, cols_len),) * 2,
        in_specs=[vmem] * 6,
        out_specs=(vmem,) * 4,
        compiler_params=params,
        name="pack_edges",
    )(fields, diffusivity, zlo, zhi, part_lo, part_hi)
    elo, ehi = swap_rows(send_lo, send_hi, "gy")
    pad = pltpu.VMEM(((nfield + 1) * planes, pitch, cols_len), F32)
    own_lo, own_hi = pl.pallas_call(
        pack_columns_kernel,
        out_shape=(array(nfield + 1, pitch, cols_len),) * 2,
        in_specs=[vmem] * 4 + [pl.BlockSpec(memory_space=pl.ANY)],
        out_specs=(vmem,) * 2,
        compiler_params=params,
        name="pack_columns",
    )(elo, ehi, main_lo, main_hi, ylo)
    odd = is_odd("gx")
    xlo, xhi = swap_pairs(jnp.where(odd, own_lo, own_hi), jnp.where(odd, own_hi, own_lo), "gx")
    stepped = pl.pallas_call(
        first_step_kernel,
        out_shape=(array(planes, pitch, cols_len),) * nfield,
        in_specs=[smem] + [vmem] * 8,
        out_specs=(vmem,) * nfield,
        scratch_shapes=[pad],
        compiler_params=params,
        cost_estimate=pl.CostEstimate(flops=10**8, bytes_accessed=8 * 10**6, transcendentals=0),
        name="first_step",
    )(courant, fields, diffusivity, zlo, zhi, ylo, elo, yhi, ehi)
    count = lax.axis_size("gz")
    order = tile_perm[0, 0]
    per_owner = order.shape[0] // count
    state, *blocks = pl.pallas_call(
        main_kernel,
        out_shape=(array(*fields.shape),) + (array(per_owner, 4, cols_len),) * count,
        in_specs=[smem] * 7 + [vmem] * (12 + nfield),
        out_specs=(pl.BlockSpec(memory_space=pl.ANY),) + (vmem,) * count,
        scratch_shapes=[
            pltpu.VMEM((planes, pitch, cols_len), F32),
            pltpu.VMEM((nfield * planes, pitch, cols_len), F32),
            pltpu.VMEM((planes, pitch, cols_len), F32),
            pltpu.VMEM((2, 2, 2, nfield, pitch, cols_len), F32),
            pltpu.VMEM((3, nfield + 1, pitch, cols_len), F32),
            pltpu.VMEM((4, depth_len, rows_len, cols_len), F32),
            pltpu.VMEM((order.shape[0] * 4, cols_len), F32),
            pltpu.VMEM((7, planes, pitch, cols_len), F32),
            pltpu.VMEM(fields.shape, F32),
            pltpu.VMEM((nfield, pitch, cols_len), F32),
            pltpu.SemaphoreType.DMA(()),
        ],
        compiler_params=pltpu.CompilerParams(vmem_limit_bytes=24 * 1024 * 1024),
        name="step_and_march",
    )(
        courant, tf_center, tf_sharp, tf_gain, tf_color, tile_mask[0, :, :, 0], order,
        fields, diffusivity, zlo, zhi, ylo, elo, yhi, ehi, xlo, xhi, own_lo, own_hi,
        *stepped,
    )
    parts = [blocks[0]] * count
    for distance in reversed(range(1, count)):
        parts[distance] = lax.ppermute(blocks[distance], "gz", [(i, i ^ distance) for i in range(count)])
    farthest_first = parts[:1] + parts[:0:-1]
    composed = compose([part.reshape(per_owner * 4, cols_len) for part in farthest_first])
    picture = composed.reshape(1, 1, per_owner, 4, cols_len)
    return (state, picture)


def solution(mesh):
    return jax.shard_map(
        shards,
        mesh=mesh,
        in_specs=(
            P(None, "gz", "gy", "gx"),
            P("gz", "gy", "gx"),
            P(),
            P(),
            P(),
            P(),
            P(),
            P("gz", None, "gy", "gx"),
            P("gy", "gx", None),
        ),
        out_specs=(P(None, "gz", "gy", "gx"), P("gy", "gx", "gz", None, None)),
        check_vma=False,
    )
```

```python
import jax
import jax.numpy as jnp
from jax import lax
from jax.experimental import pallas as pl
from jax.experimental.pallas import tpu as pltpu
from jax.sharding import PartitionSpec as P

LOG2E = 1.4426950408889634
W = 3
SUB = 8
F32 = jnp.float32


def reach(field, nfield):
    return W if field in (0, nfield) else W - 1


def tiles_of(first, last):
    return [min(start, last - SUB) for start in range(first, last, SUB)]


def z_plan(nfield):
    plan, at = [], 0
    for field in range(nfield + 1):
        plan.append((field, at, reach(field, nfield)))
        at += reach(field, nfield)
    return plan, at


def y_plan(nfield):
    kinds, edges = [], []
    for field in range(nfield + 1):
        wide = reach(field, nfield)
        for away in range(1, wide + 1):
            kinds.append((field, away))
            for k in range(1, wide - away + 1):
                edges.append((field, away, -k))
                edges.append((field, away, k))
    return kinds, edges


def pack_planes_kernel(fields_ref, kappa_ref, first_ref, second_ref, sems):
    nfield, depth_len = fields_ref.shape[:2]
    odd = lax.rem(lax.axis_index("gz"), 2)
    copies = []
    for field, at, wide in z_plan(nfield)[0]:
        source = kappa_ref if field == nfield else fields_ref.at[field]
        for place, target in ((1 - odd, first_ref), (odd, second_ref)):
            copies.append(
                pltpu.make_async_copy(
                    source.at[pl.ds(place * (depth_len - wide), wide)], target.at[pl.ds(at, wide)], sems.at[len(copies)]
                )
            )
    for copy in copies:
        copy.start()
    for copy in copies:
        copy.wait()


def present(axis):
    here = lax.axis_index(axis)
    return jnp.where(here > 0, 1.0, 0.0), jnp.where(here < lax.axis_size(axis) - 1, 1.0, 0.0)


def steps(count, most):
    return max(k for k in range(1, most + 1) if count % k == 0)


def source_plane(refs, field, z):
    fields_ref, kappa_ref, zlo_ref, zhi_ref = refs
    nfield, depth_len = fields_ref.shape[:2]
    _, at, wide = z_plan(nfield)[0][field]
    if z < 0:
        return zlo_ref.at[at + wide + z]
    if z >= depth_len:
        return zhi_ref.at[at + z - depth_len]
    return kappa_ref.at[z] if field == nfield else fields_ref.at[field, z]


def pack_rows_kernel(fields_ref, kappa_ref, lo_ref, hi_ref):
    nfield, depth_len, rows, lanes = fields_ref.shape
    flat_fields = fields_ref.reshape(nfield * depth_len * rows, lanes)
    flat_kappa = kappa_ref.reshape(depth_len * rows, lanes)
    for out_ref, top in ((lo_ref, True), (hi_ref, False)):
        for i, (field, away) in enumerate(y_plan(nfield)[0]):
            row = away - 1 if top else rows - away
            flat, base = (flat_kappa, 0) if field == nfield else (flat_fields, field * depth_len * rows)
            for z in range(0, depth_len, SUB):
                out_ref[i, z : z + SUB, :] = flat[pl.ds(base + z * rows + row, SUB, stride=rows), :]


def pack_edges_kernel(
    fields_ref, kappa_ref, zlo_ref, zhi_ref, ownlo_ref, ownhi_ref, lo_ref, hi_ref, mainlo_ref, mainhi_ref
):
    refs = (fields_ref, kappa_ref, zlo_ref, zhi_ref)
    nfield, depth_len, rows, lanes = fields_ref.shape
    lane = lax.broadcasted_iota(jnp.int32, (1, lanes), 1)
    edges = y_plan(nfield)[1]
    for i, (field, away, k) in enumerate(edges):
        plane = source_plane(refs, field, k if k < 0 else depth_len - 1 + k)
        lo_ref[i : i + 1, :] = plane[away - 1 : away, :]
        hi_ref[i : i + 1, :] = plane[rows - away : rows - away + 1, :]
    for field in range(nfield + 1):
        wide = reach(field, nfield)
        pair = (ownlo_ref[field], ownhi_ref[field])
        for z in list(range(-wide, 0)) + list(range(depth_len, depth_len + wide)):
            pair = take_columns(source_plane(refs, field, z)[...], z + W, lane, *pair)
        mainlo_ref[field], mainhi_ref[field] = pair
        for side in range(2):
            at = len(edges) + (side * (nfield + 1) + field) * W
            lo_ref[at : at + W, :] = pair[side][:W]
            hi_ref[at : at + W, :] = pair[side][rows - W :]


def assemble(refs, halo_rows, pad_ref, chosen):
    fields_ref, kappa_ref, zlo_ref, zhi_ref = refs
    nfield, depth_len, rows, lanes = fields_ref.shape
    planes, pitch = depth_len + 2 * W, rows + SUB
    halo = jnp.zeros((SUB, lanes), F32)

    @pl.loop(0, depth_len, unroll=steps(depth_len, 4))
    def _(z):
        for slot, field in enumerate(chosen):
            plane = slot * planes + W + z
            pad_ref[plane, :rows, :] = kappa_ref[z] if field == nfield else fields_ref[field, z]
            pad_ref[plane, rows:, :] = halo

    for slot, field in enumerate(chosen):
        _, at, wide = z_plan(nfield)[0][field]
        for k in range(W):
            below, above = slot * planes + W - 1 - k, slot * planes + W + depth_len + k
            if k < wide:
                pad_ref[below, :rows, :] = zlo_ref[at + wide - 1 - k]
                pad_ref[above, :rows, :] = zhi_ref[at + k]
            for plane in (below, above):
                if k >= wide:
                    pad_ref[plane, :rows, :] = jnp.zeros((rows, lanes), F32)
                pad_ref[plane, rows:, :] = halo
    pitch, lanes = pad_ref.shape[1:]
    flat = pad_ref.reshape(pad_ref.shape[0] * pitch, lanes)
    kinds, edges = y_plan(nfield)
    for low, (ref, edge_ref) in ((True, halo_rows[:2]), (False, halo_rows[2:])):
        flag = present("gy")[0 if low else 1]
        for i, (field, away) in enumerate(kinds):
            if field not in chosen:
                continue
            row = pitch - away if low else rows + away - 1
            for z in range(0, depth_len, SUB):
                flat[pl.ds((chosen.index(field) * planes + W + z) * pitch + row, SUB, stride=pitch), :] = (
                    ref[i, z : z + SUB, :] * flag
                )
        for i, (field, away, k) in enumerate(edges):
            if field not in chosen:
                continue
            row = pitch - away if low else rows + away - 1
            plane = chosen.index(field) * planes + W + (k if k < 0 else depth_len - 1 + k)
            pad_ref[plane, row : row + 1, :] = edge_ref[i : i + 1, :] * flag


def take_columns(value, zi, lane, low, high):
    lanes = value.shape[-1]
    mine = (lane >= W * zi) & (lane < W * zi + W)
    low = jnp.where(mine, pltpu.roll(value, W * zi, 1), low)
    high = jnp.where(mine, pltpu.roll(value, (W * zi + W) % lanes, 1), high)
    return low, high


def pack_own_kernel(fields_ref, kappa_ref, lo_ref, hi_ref):
    nfield, depth_len, rows, lanes = fields_ref.shape
    lane = lax.broadcasted_iota(jnp.int32, (1, lanes), 1)
    for field in range(nfield + 1):
        low = high = jnp.zeros((rows, lanes), F32)
        for z in range(depth_len):
            value = kappa_ref[z] if field == nfield else fields_ref[field, z]
            low, high = take_columns(value, z + W, lane, low, high)
        lo_ref[field] = low
        hi_ref[field] = high


def pack_columns_kernel(
    elo_ref, ehi_ref, mainlo_ref, mainhi_ref, rows_ref, lo_ref, hi_ref
):
    del rows_ref
    count, rows, lanes = mainlo_ref.shape
    low, high = present("gy")
    at = len(y_plan(count - 1)[1])
    for main_ref, out_ref in ((mainlo_ref, lo_ref), (mainhi_ref, hi_ref)):
        for field in range(count):
            out_ref[field, :rows, :] = main_ref[field]
            out_ref[field, rows:, :] = jnp.zeros((SUB, lanes), F32)
            out_ref[field, rows : rows + W, :] = ehi_ref[at : at + W, :] * high
            out_ref[field, rows + SUB - W :, :] = elo_ref[at : at + W, :] * low
            at += W


def stencil(u, coefs, ups, downs, speeds):
    total = (coefs[3] - (speeds[0] + speeds[1] + speeds[2])) * u
    for axis in range(3):
        k_up, k_down = coefs[axis]
        total = total + k_up * ups[axis] + (k_down + speeds[axis]) * downs[axis]
    return total


def weights(k, ups, downs):
    half = 0.5 * k
    coefs = [(half + 0.5 * ups[a], half + 0.5 * downs[a]) for a in range(3)]
    rest = 1.0
    for up, down in coefs:
        rest = rest - (up + down)
    return coefs + [rest]


def row_flags(shape, rows):
    r = lax.broadcasted_iota(jnp.int32, shape, 0)
    low, high = present("gy")
    return jnp.where(r < rows, 1.0, jnp.where(r < rows + SUB // 2, high, low))


def plane_flag(zi, depth_len):
    low, high = present("gz")
    return jnp.where(zi < W, low, jnp.where(zi >= W + depth_len, high, 1.0))


def first_step_kernel(
    courant_ref, fields_ref, kappa_ref, zlo_ref, zhi_ref, ylo_ref, elo_ref, yhi_ref, ehi_ref, *rest
):
    out_refs, pad_ref = rest[:-1], rest[-1]
    nfield, depth_len, rows, lanes = fields_ref.shape
    planes, pitch = depth_len + 2 * W, rows + SUB
    refs, halo_rows = (fields_ref, kappa_ref, zlo_ref, zhi_ref), (ylo_ref, elo_ref, yhi_ref, ehi_ref)
    assemble(refs, halo_rows, pad_ref, list(range(nfield + 1)))
    lane = lax.broadcasted_iota(jnp.int32, (pitch, lanes), 1)
    row_mask = row_flags((pitch, lanes), rows)
    speed = [[courant_ref[f, a] for a in range(3)] for f in range(nfield)]

    def around(field, zi):
        plane = field * planes + zi
        value = pad_ref[plane]
        x_up = jnp.where(lane == lanes - 1, value, pltpu.roll(value, lanes - 1, 1))
        x_down = jnp.where(lane == 0, value, pltpu.roll(value, 1, 1))
        ups = (pad_ref[plane + 1], pltpu.roll(value, pitch - 1, 0), x_up)
        downs = (pad_ref[plane - 1], pltpu.roll(value, 1, 0), x_down)
        return value, ups, downs

    @pl.loop(1, planes - 1, unroll=steps(planes - 2, 6))
    def _(zi):
        mask = row_mask * plane_flag(zi, depth_len)
        coefs = weights(*around(nfield, zi))
        for field in range(nfield):
            u, ups, downs = around(field, zi)
            out_refs[field][zi] = mask * stencil(u, coefs, ups, downs, speed[field])


def side_neighbours(near, own, is_left, lanes, col):
    first, second = (near, own) if is_left else (own, near)
    first_up = jnp.where(col == W - 1, pltpu.roll(second, W - 1, 1), pltpu.roll(first, lanes - 1, 1))
    first_down = pltpu.roll(first, 1, 1)
    second_up = pltpu.roll(second, lanes - 1, 1)
    second_down = jnp.where(col == 0, pltpu.roll(first, lanes - (W - 1), 1), pltpu.roll(second, 1, 1))
    pair = ((first_up, first_down), (second_up, second_down))
    return pair if is_left else (pair[1], pair[0])


def main_kernel(
    courant_ref, center_ref, sharp_ref, gain_ref, color_ref, mask_ref, order_ref,
    fields_ref, kappa_ref, zlo_ref, zhi_ref,
    ylo_ref, elo_ref, yhi_ref, ehi_ref, xlo_ref, xhi_ref, ownlo_ref, ownhi_ref, *rest,
):
    nfield, depth_len, rows, lanes = fields_ref.shape
    step_refs = rest[:nfield]
    count = lax.axis_size("gz")
    state_ref, out_refs = rest[nfield], rest[nfield + 1 : nfield + 1 + count]
    (
        kpad_ref, next_ref, last_ref, side_ref, edge_ref, base_ref,
        tile_ref, coef_ref, held_ref, flux_ref, sem,
    ) = rest[nfield + 1 + count :]
    nfield, depth_len, rows, lanes = state_ref.shape
    planes, pitch = depth_len + 2 * W, rows + SUB
    lane = lax.broadcasted_iota(jnp.int32, (pitch, lanes), 1)
    zi_of = lane // W
    col = lane - zi_of * W
    flag = present("gz") + present("gy") + present("gx")
    speed = [[courant_ref[f, a] for a in range(3)] for f in range(nfield)]
    row_mask = row_flags((pitch, lanes), rows)

    def along_y(value):
        return pltpu.roll(value, pitch - 1, 0), pltpu.roll(value, 1, 0)

    sides = ((xlo_ref, ownlo_ref, True, flag[4]), (xhi_ref, ownhi_ref, False, flag[5]))

    def block_of(level, side, block, field):
        if level == 0 or field == nfield:
            return sides[side][block][field]
        return side_ref[level - 1, side, block, field]

    def edges(level, field):
        left, right = block_of(level, 0, 0, field), block_of(level, 1, 0, field)
        edge_ref[level, field] = jnp.where(col == W - 1, left, pltpu.roll(right, 1, 1))

    def side_step(level, count):
        zmask = row_mask * jnp.where(
            zi_of < W, flag[0], jnp.where(zi_of >= W + depth_len, flag[1], 1.0)
        )
        for side, (_, _, is_left, present) in enumerate(sides):
            blocks = (0, 1) if level == 0 else (0,)

            def around(lvl, field):
                pair = [block_of(lvl, side, block, field) for block in (0, 1)]
                x = side_neighbours(pair[0], pair[1], is_left, lanes, col)
                found = []
                for block in blocks:
                    value = pair[block]
                    y_up, y_down = along_y(value)
                    ups = (pltpu.roll(value, lanes - W, 1), y_up, x[block][0])
                    downs = (pltpu.roll(value, W, 1), y_down, x[block][1])
                    found.append((value, ups, downs))
                return found

            coefs = [weights(*found) for found in around(0, nfield)]
            for field in range(count):
                for block, (u, ups, downs) in zip(blocks, around(level, field)):
                    value = stencil(u, coefs[block], ups, downs, speed[field])
                    side_ref[level, side, block, field] = value * (zmask * present if block == 0 else zmask)

    def along_x(value, zi, edge):
        n = value.shape[0]
        turned = pltpu.roll(edge, lax.rem(2 * lanes - 2 - W * zi, lanes), 1)
        up = jnp.where(lane[:n] == lanes - 1, turned, pltpu.roll(value, lanes - 1, 1))
        down = jnp.where(lane[:n] == 0, turned, pltpu.roll(value, 1, 1))
        return up, down

    def around(src_ref, level, field, zi, n, slot=None):
        plane = (field if slot is None else slot) * planes + zi
        whole = src_ref[plane]
        value = whole[:n]
        y_up, y_down = along_y(whole)
        x_up, x_down = along_x(value, zi, edge_ref[level, field, :n, :])
        return (
            value,
            (src_ref[plane + 1, :n, :], y_up[:n], x_up),
            (src_ref[plane - 1, :n, :], y_down[:n], x_down),
        )

    def step_value(src_ref, level, field, zi, n, coefs):
        u, ups, downs = around(src_ref, level, field, zi, n)
        return stencil(u, coefs, ups, downs, speed[field])

    def kept(zi, n):
        found = [coef_ref[i, zi, :n, :] for i in range(7)]
        return [found[0:2], found[2:4], found[4:6], found[6]]

    halo_rows = (ylo_ref, elo_ref, yhi_ref, ehi_ref)
    assemble((fields_ref, kappa_ref, zlo_ref, zhi_ref), halo_rows, kpad_ref, [nfield])
    edges(0, nfield)
    lane_mask = row_mask * jnp.where(
        zi_of < W, flag[0], jnp.where(zi_of >= W + depth_len, flag[1], 1.0)
    )
    k_left = 0.5 * (xlo_ref[nfield] + pltpu.roll(ownlo_ref[nfield], W - 1, 1))
    k_right = 0.5 * (xhi_ref[nfield] + pltpu.roll(ownhi_ref[nfield], lanes - (W - 1), 1))
    for field in range(nfield):
        left = (k_left + speed[field][2]) * (xlo_ref[field] - pltpu.roll(ownlo_ref[field], W - 1, 1))
        right = k_right * (xhi_ref[field] - pltpu.roll(ownhi_ref[field], lanes - (W - 1), 1))
        flux_ref[field] = lane_mask * jnp.where(col == W - 1, left, pltpu.roll(right, 1, 1))
    side_step(0, nfield)
    for field in range(nfield):
        edges(1, field)
    side_step(1, 1)
    edges(2, 0)

    @pl.loop(1, planes - 1, unroll=steps(planes - 2, 6))
    def _(zi):
        coefs = weights(*around(kpad_ref, 0, nfield, zi, pitch, 0))
        for i, value in enumerate(sum(coefs[:3], ()) + (coefs[3],)):
            coef_ref[i, zi] = value
        outer = (lane == 0) | (lane == lanes - 1)
        for field in range(nfield):
            turned = pltpu.roll(flux_ref[field], lax.rem(2 * lanes - 2 - W * zi, lanes), 1)
            next_ref[field * planes + zi] = step_refs[field][zi] + jnp.where(outer, turned, 0.0)

    @pl.loop(2, planes - 2, unroll=steps(planes - 4, 17))
    def _(zi):
        coefs = kept(zi, pitch)
        last_ref[zi] = step_value(next_ref, 1, 0, zi, pitch, coefs) * (row_mask * plane_flag(zi, depth_len))

    @pl.loop(0, depth_len, unroll=steps(depth_len, 8))
    def _(z):
        zi = z + W
        coefs = kept(zi, rows)
        s, ups, downs = around(last_ref, 2, 0, zi, rows)
        held_ref[0, z] = s
        g_z, g_y, g_x = [0.5 * (ups[a] - downs[a]) for a in range(3)]
        shade = 0.35 + 0.65 * jnp.abs(0.64 * g_z + 0.6 * g_y + 0.48 * g_x) * lax.rsqrt(
            g_z * g_z + g_y * g_y + g_x * g_x + 1.0
        )
        for field in range(1, nfield):
            value = step_value(next_ref, 1, field, zi, rows, coefs)
            held_ref[field, z] = value
            if field <= 3:
                base_ref[field, z] = shade * (0.5 + 0.5 * jnp.tanh(0.5 * value))
            if field == 4:
                base_ref[0, z] = 1.0 + 0.5 * jnp.tanh(value)

    keep = pltpu.make_async_copy(held_ref, state_ref, sem)
    keep.start()
    ntf = center_ref.shape[0]
    chunk = 4 if ntf % 4 == 0 else 1
    halves = rows // SUB

    @pl.loop(0, (ntf // chunk) * halves)
    def _(step):
        first = (step // halves) * chunk
        row = pl.multiple_of((step % halves) * SUB, SUB)
        shape = (SUB, lanes)
        mid = [jnp.full(shape, center_ref[first + j], jnp.float32) for j in range(chunk)]
        bend = [jnp.full(shape, sharp_ref[first + j] * -LOG2E, jnp.float32) for j in range(chunk)]
        dense = [jnp.full(shape, gain_ref[first + j] * -LOG2E, jnp.float32) for j in range(chunk)]
        passed = [jnp.ones(shape, jnp.float32)] * chunk
        total = [jnp.zeros(shape, jnp.float32)] * chunk
        acc = [[jnp.zeros(shape, jnp.float32)] * 3 for _ in range(chunk)]
        for z in range(depth_len):
            s = held_ref[0, z, pl.ds(row, SUB), :]
            modul = base_ref[0, z, pl.ds(row, SUB), :]
            base = [base_ref[k + 1, z, pl.ds(row, SUB), :] for k in range(3)]
            for j in range(chunk):
                diff = s - mid[j]
                total[j] = total[j] + modul * jnp.exp2(diff * diff * bend[j])
                after = jnp.exp2(total[j] * dense[j])
                weight = passed[j] - after
                passed[j] = after
                acc[j] = [acc[j][k] + weight * base[k] for k in range(3)]
        for j in range(chunk):
            start = ((first + j) * rows + row) * 4
            for k in range(3):
                tile_ref[pl.ds(start + k, SUB, stride=4), :] = acc[j][k] * color_ref[k, first + j]
            tile_ref[pl.ds(start + 3, SUB, stride=4), :] = 1.0 - passed[j]

    per_owner = out_refs[0].shape[0]
    for distance, out_ref in enumerate(out_refs):
        first_slot = lax.bitwise_xor(lax.axis_index("gz"), distance) * per_owner

        @pl.loop(0, per_owner, unroll=per_owner)
        def _(place):
            tile = order_ref[first_slot + place]
            cover = mask_ref[lax.div(tile, rows), lax.rem(tile, rows)].astype(F32)
            out_ref[place] = tile_ref[pl.ds(pl.multiple_of(tile * 4, 4), 4), :] * cover

    keep.wait()


def compose_kernel(*refs):
    part_refs, out_ref = refs[:1] + refs[-2:0:-1], refs[-1]
    slabs, rows = len(part_refs), out_ref.shape[0]
    here = lax.axis_index("gz")

    @pl.loop(0, rows // 32, unroll=rows // 32)
    def _(step):
        def load(k):
            return [ref[pl.ds(step * 32 + k, 8, stride=4), :] for ref in part_refs]

        parts = [load(k) for k in range(4)]

        def slab_of(slab, k):
            distance = lax.bitwise_xor(here, slab)
            value = parts[k][0]
            for i in range(1, slabs):
                value = jnp.where(distance == i, parts[k][i], value)
            return value

        acc = [slab_of(0, k) for k in range(4)]
        for slab in range(1, slabs):
            clear = 1.0 - acc[3]
            acc = [acc[k] + clear * slab_of(slab, k) for k in range(4)]
        for k in range(4):
            out_ref[pl.ds(step * 32 + k, 8, stride=4), :] = acc[k]


def compose(parts):
    vmem = pl.BlockSpec(memory_space=pltpu.VMEM)
    return pl.pallas_call(
        compose_kernel,
        out_shape=jax.ShapeDtypeStruct(parts[0].shape, jnp.float32),
        in_specs=[vmem] * len(parts),
        out_specs=vmem,
        compiler_params=pltpu.CompilerParams(vmem_limit_bytes=16 * 1024 * 1024),
        name="compose",
    )(*parts)


def is_odd(axis):
    return lax.rem(lax.axis_index(axis), 2) == 1


def swap_pairs(first, second, axis, flip=False):
    count = lax.axis_size(axis)
    came = []
    for start, message in ((0, first), (1, second)):
        pairs = []
        for i in range(start, count - 1, 2):
            pairs += [(i, i + 1), (i + 1, i)]
        came.append(lax.ppermute(message, axis, pairs) if pairs else jnp.zeros_like(message))
    odd = is_odd(axis)
    if flip:
        even = jnp.logical_not(odd)
        return jnp.where(even, came[1], came[0]), jnp.where(even, came[0], came[1])
    return jnp.where(odd, came[0], came[1]), jnp.where(odd, came[1], came[0])


def swap_rows(low, high, axis):
    odd = is_odd(axis)
    first = jnp.where(odd, low, high)
    if lax.axis_size(axis) == 2:
        came = lax.ppermute(first, axis, [(0, 1), (1, 0)])
        return came, came
    return swap_pairs(first, jnp.where(odd, high, low), axis)


def shards(
    fields, diffusivity, courant, tf_center, tf_sharp, tf_gain, tf_color, tile_mask, tile_perm
):
    nfield, depth_len, rows_len, cols_len = fields.shape
    planes, pitch = depth_len + 2 * W, rows_len + SUB
    smem = pl.BlockSpec(memory_space=pltpu.SMEM)
    vmem = pl.BlockSpec(memory_space=pltpu.VMEM)
    params = pltpu.CompilerParams(vmem_limit_bytes=16 * 1024 * 1024)

    def array(*shape):
        return jax.ShapeDtypeStruct(shape, F32)

    faces = z_plan(nfield)[1]
    first, second = pl.pallas_call(
        pack_planes_kernel,
        out_shape=(array(faces, rows_len, cols_len),) * 2,
        in_specs=[pl.BlockSpec(memory_space=pl.ANY)] * 2,
        out_specs=(vmem, vmem),
        scratch_shapes=[pltpu.SemaphoreType.DMA((2 * nfield + 2,))],
        compiler_params=pltpu.CompilerParams(vmem_limit_bytes=60 * 1024 * 1024),
        name="pack_planes",
    )(fields, diffusivity)
    zlo, zhi = swap_pairs(first, second, "gz")
    kinds, outer = y_plan(nfield)
    send_lo, send_hi = pl.pallas_call(
        pack_rows_kernel,
        out_shape=(array(len(kinds), depth_len, cols_len),) * 2,
        in_specs=[vmem] * 2,
        out_specs=(vmem, vmem),
        compiler_params=params,
        name="pack_rows",
    )(fields, diffusivity)
    ylo, yhi = swap_rows(send_lo, send_hi, "gy")
    part_lo, part_hi = pl.pallas_call(
        pack_own_kernel,
        out_shape=(array(nfield + 1, rows_len, cols_len),) * 2,
        in_specs=[vmem] * 2,
        out_specs=(vmem,) * 2,
        compiler_params=params,
        cost_estimate=pl.CostEstimate(flops=10**7, bytes_accessed=4 * 10**6, transcendentals=0),
        name="pack_own",
    )(fields, diffusivity)
    extra = len(outer) + 2 * (nfield + 1) * W
    send_lo, send_hi, main_lo, main_hi = pl.pallas_call(
        pack_edges_kernel,
        out_shape=(array(extra, cols_len),) * 2 + (array(nfield + 1, rows_len, cols_len),) * 2,
        in_specs=[vmem] * 6,
        out_specs=(vmem,) * 4,
        compiler_params=params,
        name="pack_edges",
    )(fields, diffusivity, zlo, zhi, part_lo, part_hi)
    elo, ehi = swap_rows(send_lo, send_hi, "gy")
    pad = pltpu.VMEM(((nfield + 1) * planes, pitch, cols_len), F32)
    own_lo, own_hi = pl.pallas_call(
        pack_columns_kernel,
        out_shape=(array(nfield + 1, pitch, cols_len),) * 2,
        in_specs=[vmem] * 4 + [pl.BlockSpec(memory_space=pl.ANY)],
        out_specs=(vmem,) * 2,
        compiler_params=params,
        name="pack_columns",
    )(elo, ehi, main_lo, main_hi, ylo)
    odd = is_odd("gx")
    xlo, xhi = swap_pairs(jnp.where(odd, own_lo, own_hi), jnp.where(odd, own_hi, own_lo), "gx", True)
    stepped = pl.pallas_call(
        first_step_kernel,
        out_shape=(array(planes, pitch, cols_len),) * nfield,
        in_specs=[smem] + [vmem] * 8,
        out_specs=(vmem,) * nfield,
        scratch_shapes=[pad],
        compiler_params=params,
        cost_estimate=pl.CostEstimate(flops=10**8, bytes_accessed=8 * 10**6, transcendentals=0),
        name="first_step",
    )(courant, fields, diffusivity, zlo, zhi, ylo, elo, yhi, ehi)
    count = lax.axis_size("gz")
    order = tile_perm[0, 0]
    per_owner = order.shape[0] // count
    state, *blocks = pl.pallas_call(
        main_kernel,
        out_shape=(array(*fields.shape),) + (array(per_owner, 4, cols_len),) * count,
        in_specs=[smem] * 7 + [vmem] * (12 + nfield),
        out_specs=(pl.BlockSpec(memory_space=pl.ANY),) + (vmem,) * count,
        scratch_shapes=[
            pltpu.VMEM((planes, pitch, cols_len), F32),
            pltpu.VMEM((nfield * planes, pitch, cols_len), F32),
            pltpu.VMEM((planes, pitch, cols_len), F32),
            pltpu.VMEM((2, 2, 2, nfield, pitch, cols_len), F32),
            pltpu.VMEM((3, nfield + 1, pitch, cols_len), F32),
            pltpu.VMEM((4, depth_len, rows_len, cols_len), F32),
            pltpu.VMEM((order.shape[0] * 4, cols_len), F32),
            pltpu.VMEM((7, planes, pitch, cols_len), F32),
            pltpu.VMEM(fields.shape, F32),
            pltpu.VMEM((nfield, pitch, cols_len), F32),
            pltpu.SemaphoreType.DMA(()),
        ],
        compiler_params=pltpu.CompilerParams(vmem_limit_bytes=24 * 1024 * 1024),
        name="step_and_march",
    )(
        courant, tf_center, tf_sharp, tf_gain, tf_color, tile_mask[0, :, :, 0], order,
        fields, diffusivity, zlo, zhi, ylo, elo, yhi, ehi, xlo, xhi, own_lo, own_hi,
        *stepped,
    )
    parts = [blocks[0]] * count
    for distance in reversed(range(1, count)):
        parts[distance] = lax.ppermute(blocks[distance], "gz", [(i, i ^ distance) for i in range(count)])
    farthest_first = parts[:1] + parts[:0:-1]
    composed = compose([part.reshape(per_owner * 4, cols_len) for part in farthest_first])
    picture = composed.reshape(1, 1, per_owner, 4, cols_len)
    return (state, picture)


def solution(mesh):
    return jax.shard_map(
        shards,
        mesh=mesh,
        in_specs=(
            P(None, "gz", "gy", "gx"),
            P("gz", "gy", "gx"),
            P(),
            P(),
            P(),
            P(),
            P(),
            P("gz", None, "gy", "gx"),
            P("gy", "gx", None),
        ),
        out_specs=(P(None, "gz", "gy", "gx"), P("gy", "gx", "gz", None, None)),
        check_vma=False,
    )
```
